32 devices in a mesh: shard: 8 (over z, y), rep: 4 (over x, core).
Axes of the slice: x: 2, y: 2, z: 4, core: 2. Of those that a mesh axis runs over, the one named last changes fastest.
Arguments:
- tokens: bfloat16 [4, 1024, 1024], P('rep', 'shard'), may hold values from -16 to 16
- segment_ids: int32 [4, 1024], P('rep', 'shard'), may hold values from 0 to 8, as said below
- expert_ids: int32 [4, 1024, 8], P('rep', 'shard'), may hold values from 0 to 15, all different within a row; in each aligned block of 128 rows (0 to 127, 128 to 255, ..., all dimensions but the last counted through in order) at most 80 rows name the same one
- attn_gain: bfloat16 [1024], P('shard'), may hold values from 0.5 to 1.5
- w_query: bfloat16 [1024, 1024], P('shard'), may hold values from -1 to 1
- w_key: bfloat16 [1024, 512], P('shard'), may hold values from -1 to 1
- w_value: bfloat16 [1024, 512], P('shard'), may hold values from -0.1875 to 0.1875
- w_output: bfloat16 [1024, 1024], P('shard'), may hold values from -3 to 3
- ffn_gain: bfloat16 [1024], P('shard'), may hold values from 0.5 to 1.5
- w_router: bfloat16 [1024, 16], P('shard'), may hold values from -1 to 1
- w_gate: bfloat16 [16, 1024, 512], P('shard'), may hold values from -0.1875 to 0.1875
- w_up: bfloat16 [16, 1024, 512], P('shard'), may hold values from -0.1875 to 0.1875
- w_down: bfloat16 [16, 512, 1024], P('shard'), may hold values from -2 to 2
- out_grad: bfloat16 [4, 1024, 1024], P('rep', 'shard'), may hold values from -6 to 6
Outputs:
- mixed: bfloat16 [4, 1024, 1024], P('rep', 'shard')
- grad_tokens: bfloat16 [4, 1024, 1024], P('rep', 'shard')
- grad_attn_gain: float32 [1024], P('shard')
- grad_w_query: float32 [1024, 1024], P('shard')
- grad_w_key: float32 [1024, 512], P('shard')
- grad_w_value: float32 [1024, 512], P('shard')
- grad_w_output: float32 [1024, 1024], P('shard')
- grad_ffn_gain: float32 [1024], P('shard')
- grad_w_router: float32 [1024, 16], P('shard')
- grad_w_gate: float32 [16, 1024, 512], P('shard', 'rep')
- grad_w_up: float32 [16, 1024, 512], P('shard', 'rep')
- grad_w_down: float32 [16, 512, 1024], P('shard', 'rep')
The draws below stay inside these ranges and needn't reach their ends.
Inputs may be any that keep to these rules, and one draw needn't show every extreme that they name: `expert_ids`: each row names 8 different experts. In every aligned block of 128 rows (the rows of one device) no expert is named by more than 80 rows, a bound that some block reaches. `segment_ids`: ids never fall along a replica row and start at 0; each aligned block of 128 rows (the rows of one device) holds exactly one rise of the id by one, from 32 to 95 rows into the block.
All inputs are finite; a program needn't handle non-finite values.
Results may differ from the reference program's by a relative error of at most 0.013.
The reference program's roundings to bfloat16 on the way count: a program that leaves them out, or rounds other values in their place, can miss the bound.
Values may be sent and summed in bfloat16 or wider, within the bound.
No kernel may reach another device: no remote copies, remote signals or barrier semaphores. Data moves between devices by JAX's collectives and lax.ppermute only.
A program may use at most 128 MiB of HBM per device.

```python
import math
import jax
import jax.numpy as jnp
import numpy as np
from jax import lax

D = 1024
HEADS = 16
KV_HEADS = 8
HEAD_DIM = 64
FF = 512
TOPK = 8
TOK_DEV = 128
EXPERTS = 16
REPLICAS = 4
GROUP_TOK = 1024
CAP = 80


def draw_tokens(key, part):
    scale_key, value_key = jax.random.split(jax.random.fold_in(key, 11))
    scales = jnp.exp(jax.random.uniform(scale_key, (REPLICAS, GROUP_TOK, 1), jnp.float32, math.log(0.3), math.log(3.0)))
    values = jnp.clip(jax.random.normal(value_key, (REPLICAS, GROUP_TOK, D), jnp.float32), -5.0, 5.0)
    return (values * scales).astype(jnp.bfloat16)


def draw_segment_ids(key, part):
    block_count = GROUP_TOK // TOK_DEV
    starts = jax.random.randint(jax.random.fold_in(key, 41), (REPLICAS, block_count, 1), TOK_DEV // 4, 3 * TOK_DEV // 4, jnp.int32)
    within = jnp.arange(TOK_DEV, dtype=jnp.int32)[None, None, :]
    ids = jnp.arange(block_count, dtype=jnp.int32)[None, :, None] + (within >= starts).astype(jnp.int32)
    return ids.reshape(REPLICAS, GROUP_TOK)


def projection_pair(key):
    base_key = jax.random.fold_in(key, 23)
    query_key, key_key = jax.random.split(base_key)
    query_part = jnp.clip(jax.random.normal(query_key, (D, HEADS * HEAD_DIM), jnp.float32), -5.0, 5.0) / math.sqrt(D)
    key_part = jnp.clip(jax.random.normal(key_key, (D, KV_HEADS * HEAD_DIM), jnp.float32), -5.0, 5.0) / math.sqrt(D)
    return (query_part, key_part)


def draw_w_query(key, part):
    query_part, key_part = projection_pair(key)
    return query_part.astype(jnp.bfloat16)


def draw_w_key(key, part):
    query_part, key_part = projection_pair(key)
    return key_part.astype(jnp.bfloat16)


def draw_w_router(key, part):
    values = jnp.clip(jax.random.normal(jax.random.fold_in(key, 31), (D, EXPERTS), jnp.float32), -5.0, 5.0) * (0.5 / math.sqrt(D))
    return values.astype(jnp.bfloat16)


def block_levels(own_key, dims, shards, smallest, high):
    def one(axis_at, blocks):
        steps = jax.random.uniform(jax.random.fold_in(jax.random.fold_in(own_key, 6), axis_at), (blocks,), jnp.float32, smallest / len(shards), high / len(shards))
        return jnp.repeat(jnp.exp(steps), dims[axis_at] // blocks).reshape((-1,) + (1,) * (len(dims) - axis_at - 1))

    level = one(*shards[0])
    for cut in shards[1:]:
        level = level * one(*cut)
    return level


def shared_out(stream_key, own, number, rows, number_of, top, most, slope):
    order = jax.random.permutation(stream_key, number_of)
    crowded, usual = portions_of(number_of, rows * top, most, slope, True), portions_of(number_of, rows * top, most, slope, False)
    places = jnp.arange(number_of)

    def named(tallies, rotation):
        used = int((tallies > 0).sum())
        fixed = max(1, used // 4)
        moved = fixed + (places - fixed + rotation * (used - fixed)) % max(1, number_of - fixed)
        return jnp.zeros((number_of,), jnp.int32).at[order[jnp.where(places < fixed, places, moved)]].set(jnp.asarray(tallies, jnp.int32))

    tallies = jnp.where(number % 4 == 0, named(crowded, number // 4), named(usual, number - number // 4 - 1))
    mixed = jax.random.permutation(jax.random.fold_in(own, 3), number_of)
    giver, receiver = mixed[0:number_of // 2 * 2:2], mixed[1:number_of // 2 * 2:2]
    room = jnp.minimum(tallies[giver] - 1, most - tallies[receiver]) // 2
    room = jnp.where((giver == order[0]) | (receiver == order[0]) | (tallies[receiver] == 0), 0, jnp.maximum(room, 0))
    moved = jax.random.randint(jax.random.fold_in(own, 4), (number_of // 2,), 0, 1 << 20) % (room + 1)
    tallies = tallies.at[giver].add(-moved).at[receiver].add(moved)
    members = jnp.searchsorted(jnp.cumsum(tallies), jnp.arange(rows * top), side="right").astype(jnp.int32)
    grid = members.reshape(top, rows).T
    grid = grid[jax.random.permutation(jax.random.fold_in(own, 1), rows)]
    rotation = jax.random.randint(jax.random.fold_in(own, 2), (rows, 1), 0, top)
    return jnp.take_along_axis(grid, (jnp.arange(top)[None, :] + rotation) % top, axis=1)


def portions_of(count, total, reach, slope, full):
    weights = [(1 << 20) // math.isqrt(grade ** slope) + 1 for grade in range(1, count + 1)]
    largest = reach if full else min(reach, max(-(-total // count), total * weights[0] // sum(weights)))
    least = 1 if total - largest >= count - 1 else 0
    holding, surplus = [largest] + [least] * (count - 1), total - largest - least * (count - 1)
    while surplus > 0:
        candidates = [i for i in range(1, count) if holding[i] < largest] or [i for i in range(1, count) if holding[i] < reach]
        pool, budget = sum([weights[i] for i in candidates]), surplus
        for i in candidates:
            addition = min(reach - holding[i], max(1, budget * weights[i] // pool), surplus)
            holding[i] = holding[i] + addition
            surplus = surplus - addition
    return np.array(holding)


def noise(rng, shape, deviation, limit, cuts=(), kind=jnp.bfloat16):
    entries = jax.random.normal(rng, shape, jnp.float32) * deviation
    if len(cuts) > 0:
        entries = block_levels(rng, shape, cuts, -0.22, 0.18) * entries
    return jnp.clip(entries, min=-limit, max=limit).astype(kind)


def setup_inputs(seed: int = 0) -> dict:
    splits = jax.random.split(jax.random.key(seed), 15)
    tokens = draw_tokens(jax.random.fold_in(splits[14], 71), 0)
    segment_ids = draw_segment_ids(jax.random.fold_in(splits[14], 71), 0)
    expert_ids_keys = jax.random.split(jax.random.fold_in(splits[2], 1), REPLICAS * GROUP_TOK // TOK_DEV)
    expert_ids_turns = jax.random.permutation(jax.random.fold_in(splits[2], 3), REPLICAS * GROUP_TOK // TOK_DEV)
    expert_ids = jax.vmap(lambda own, number: shared_out(jax.random.fold_in(splits[2], 2), own, number, TOK_DEV, EXPERTS, TOPK, CAP, 2))(expert_ids_keys, expert_ids_turns).reshape((REPLICAS, GROUP_TOK, TOPK))
    attn_gain = jnp.clip(1.0 + 0.1 * jax.random.normal(splits[3], (D,), jnp.float32), 0.5, 1.5).astype(jnp.bfloat16)
    w_query = draw_w_query(jax.random.fold_in(splits[14], 71), 0)
    w_key = draw_w_key(jax.random.fold_in(splits[14], 71), 0)
    w_value = noise(splits[6], (D, KV_HEADS * HEAD_DIM), D ** -0.5, 0.1875, ((0, 8),))
    w_output = noise(splits[7], (HEADS * HEAD_DIM, D), (max(1, HEADS * HEAD_DIM // 256)) ** -0.5, 3.0, ((0, 8),))
    ffn_gain = jnp.clip(1.0 + 0.1 * jax.random.normal(splits[8], (D,), jnp.float32), 0.5, 1.5).astype(jnp.bfloat16)
    w_router = draw_w_router(jax.random.fold_in(splits[14], 71), 0)
    w_gate = noise(splits[10], (EXPERTS, D, FF), D ** -0.5, 0.1875, ((0, 8),))
    w_up = noise(splits[11], (EXPERTS, D, FF), D ** -0.5, 0.1875, ((0, 8),))
    w_down = noise(splits[12], (EXPERTS, FF, D), (max(1, FF // 64)) ** -0.5, 2.0, ((0, 8),))
    out_grad = noise(splits[13], (REPLICAS, GROUP_TOK, D), 1.0, 6.0, ((0, 4), (1, 8)))
    return dict(tokens=tokens, segment_ids=segment_ids, expert_ids=expert_ids, attn_gain=attn_gain, w_query=w_query, w_key=w_key, w_value=w_value, w_output=w_output, ffn_gain=ffn_gain, w_router=w_router, w_gate=w_gate, w_up=w_up, w_down=w_down, out_grad=out_grad)


EPSILON = 1e-06
RESIDUAL_SCALE = 0.22
SCORE_SCALE = 0.015625
ROPE_BASE = 10000.0
NEG_LARGE = -1e+30

def rms_forward(values, norm_gain):
    inv_rms = lax.rsqrt(lax.optimization_barrier(jnp.mean(values * values, axis=-1, keepdims=True)) + EPSILON)
    return (values * inv_rms * norm_gain, inv_rms)

def rms_backward(values, inv_rms, norm_gain, upstream):
    scaled = upstream * norm_gain
    through = inv_rms * scaled - values * (inv_rms * inv_rms * inv_rms) * lax.optimization_barrier(jnp.mean(scaled * values, axis=-1, keepdims=True))
    gain_grad = lax.optimization_barrier(jnp.sum(upstream * values * inv_rms, axis=0))
    return (through, gain_grad)

def rotary_tables(positions):
    indices = jnp.arange(HEAD_DIM // 2, dtype=jnp.float32)
    inverse = jnp.exp(indices * (-2.0 * math.log(ROPE_BASE) / HEAD_DIM))
    angles = positions.astype(jnp.float32)[:, None] * inverse[None, :]
    cos_table = jnp.concatenate([jnp.cos(angles), jnp.cos(angles)], axis=-1)[:, None, :]
    sin_table = jnp.concatenate([jnp.sin(angles), jnp.sin(angles)], axis=-1)[:, None, :]
    return (cos_table, sin_table)

def rotate_half(values):
    lower_half, upper_half = jnp.split(values, 2, axis=-1)
    return jnp.concatenate([-upper_half, lower_half], axis=-1)

def rotate_back(values):
    lower_half, upper_half = jnp.split(values, 2, axis=-1)
    return jnp.concatenate([upper_half, -lower_half], axis=-1)

def rotary_apply(values, cos_table, sin_table):
    return values * cos_table + rotate_half(values) * sin_table

def rotary_grad(upstream, cos_table, sin_table):
    return upstream * cos_table + rotate_back(upstream * sin_table)

def score_block(queries, key_rows, allowed):
    scores = jnp.einsum('qkgd,pkd->kgqp', queries.astype(jnp.float32), key_rows.astype(jnp.float32)) * SCORE_SCALE
    return jnp.where(allowed[None, None], scores, NEG_LARGE)

def attention_forward(queries, key_rows, value_rows, allowed):
    scores = score_block(queries, key_rows, allowed)
    highest = lax.optimization_barrier(jnp.max(scores, axis=-1, keepdims=True))
    log_total = highest + jnp.log(lax.optimization_barrier(jnp.sum(jnp.exp(scores - highest), axis=-1, keepdims=True)))
    probs = lax.optimization_barrier(jnp.exp(scores - log_total).astype(jnp.bfloat16)).astype(jnp.float32)
    attended = jnp.einsum('kgqp,pkd->qkgd', probs, value_rows.astype(jnp.float32))
    return (attended.astype(jnp.bfloat16), log_total)

def attention_backward(queries, key_rows, value_rows, allowed, attended, log_total, attended_grad):
    scores = score_block(queries, key_rows, allowed)
    probs = jnp.exp(scores - log_total)
    probs_low = lax.optimization_barrier(probs.astype(jnp.bfloat16)).astype(jnp.float32)
    grad_full = attended_grad.astype(jnp.float32)
    value_grad = jnp.einsum('kgqp,qkgd->pkd', probs_low, grad_full)
    prob_grad = jnp.einsum('qkgd,pkd->kgqp', grad_full, value_rows.astype(jnp.float32))
    delta = jnp.einsum('qkgd,qkgd->kgq', grad_full, attended.astype(jnp.float32))[..., None]
    score_grad = probs * (prob_grad - delta) * SCORE_SCALE
    score_grad = lax.optimization_barrier(score_grad.astype(jnp.bfloat16)).astype(jnp.float32)
    query_grad = jnp.einsum('kgqp,pkd->qkgd', score_grad, key_rows.astype(jnp.float32))
    key_grad = jnp.einsum('kgqp,qkgd->pkd', score_grad, queries.astype(jnp.float32))
    return (query_grad, key_grad, value_grad)

def block_mask(seg_window, block_index):
    half = TOK_DEV // 2
    query_place = jnp.arange(TOK_DEV, dtype=jnp.int32)
    key_place = jnp.arange(TOK_DEV + half, dtype=jnp.int32) - half
    seq_query = (query_place + half) // TOK_DEV
    seq_key = (key_place + half) // TOK_DEV
    allowed = (key_place[None, :] <= query_place[:, None]) & (seq_key[None, :] == seq_query[:, None])
    allowed = allowed & (seg_window[None, :] == seg_window[half:][:, None])
    leading = block_index % (GROUP_TOK // TOK_DEV) == 0
    return allowed & ((key_place[None, :] >= 0) | jnp.logical_not(leading))

def reference(tokens, segment_ids, expert_ids, attn_gain, w_query, w_key, w_value, w_output, ffn_gain, w_router, w_gate, w_up, w_down, out_grad):
    count = REPLICAS * GROUP_TOK
    half = TOK_DEV // 2
    window = TOK_DEV + half
    blocks = count // TOK_DEV
    group = HEADS // KV_HEADS
    first_gain = attn_gain.astype(jnp.float32)
    second_gain = ffn_gain.astype(jnp.float32)
    inputs = tokens.reshape(count, D).astype(jnp.float32)
    normed_f, inv_first = rms_forward(inputs, first_gain)
    normed = normed_f.astype(jnp.bfloat16)
    positions = (jnp.arange(count, dtype=jnp.int32) % TOK_DEV + half) % TOK_DEV
    cos_table, sin_table = rotary_tables(positions)
    query_lin = jnp.dot(normed, w_query, preferred_element_type=jnp.float32).reshape(count, HEADS, HEAD_DIM)
    queries = rotary_apply(query_lin, cos_table, sin_table).astype(jnp.bfloat16).reshape(blocks, TOK_DEV, KV_HEADS, group, HEAD_DIM)
    key_lin = jnp.dot(normed, w_key, preferred_element_type=jnp.float32).reshape(count, KV_HEADS, HEAD_DIM)
    key_rows = rotary_apply(key_lin, cos_table, sin_table).astype(jnp.bfloat16)
    value_rows = jnp.dot(normed, w_value, preferred_element_type=jnp.float32).astype(jnp.bfloat16).reshape(count, KV_HEADS, HEAD_DIM)
    key_pad = jnp.concatenate([jnp.zeros((half, KV_HEADS, HEAD_DIM), jnp.bfloat16), key_rows], axis=0)
    value_pad = jnp.concatenate([jnp.zeros((half, KV_HEADS, HEAD_DIM), jnp.bfloat16), value_rows], axis=0)
    seg_pad = jnp.concatenate([jnp.zeros((half,), jnp.int32), segment_ids.reshape(count).astype(jnp.int32)], axis=0)
    block_ids = jnp.arange(blocks, dtype=jnp.int32)

    def block_inputs(block_index):
        start = (block_index * TOK_DEV).astype(jnp.int32)
        keys_here = lax.dynamic_slice_in_dim(key_pad, start, window, 0)
        values_here = lax.dynamic_slice_in_dim(value_pad, start, window, 0)
        segs_here = lax.dynamic_slice_in_dim(seg_pad, start, window, 0)
        return (keys_here, values_here, block_mask(segs_here, block_index))

    def forward_block(packed):
        keys_here, values_here, allowed = block_inputs(packed[1])
        return attention_forward(packed[0], keys_here, values_here, allowed)
    attended, log_total = lax.map(forward_block, (queries, block_ids))
    attended_flat = attended.reshape(count, HEADS * HEAD_DIM)
    hidden = inputs + RESIDUAL_SCALE * jnp.dot(attended_flat, w_output, preferred_element_type=jnp.float32)
    ffn_f, inv_second = rms_forward(hidden, second_gain)
    ffn_inputs = ffn_f.astype(jnp.bfloat16)
    logits = jnp.dot(ffn_inputs, w_router, preferred_element_type=jnp.float32)
    routes = expert_ids.reshape(count, TOPK)
    choose = routes[:, :, None] == jnp.arange(EXPERTS, dtype=jnp.int32)[None, None, :]
    chosen = lax.optimization_barrier(jnp.sum(jnp.where(choose, logits[:, None, :], 0.0), axis=-1))
    highest = lax.optimization_barrier(jnp.max(chosen, axis=-1, keepdims=True))
    raised = jnp.exp(chosen - highest)
    gates = raised / lax.optimization_barrier(jnp.sum(raised, axis=-1, keepdims=True))
    assign_total = count * TOPK
    flat_experts = routes.reshape(blocks, TOK_DEV * TOPK)
    flat_hot = (flat_experts[:, :, None] == jnp.arange(EXPERTS, dtype=jnp.int32)[None, None, :]).astype(jnp.int32)
    earlier = jnp.cumsum(flat_hot, axis=1) - flat_hot
    slot_index = lax.optimization_barrier(jnp.sum(earlier * flat_hot, axis=-1))
    destination = flat_experts * CAP + slot_index
    assign_ids = jnp.arange(assign_total, dtype=jnp.int32).reshape(blocks, TOK_DEV * TOPK)
    table = jnp.full((blocks, EXPERTS * CAP), assign_total, jnp.int32)
    table = table.at[jnp.arange(blocks, dtype=jnp.int32)[:, None], destination].set(assign_ids)
    table = table.reshape(blocks, EXPERTS, CAP).transpose(1, 0, 2).reshape(EXPERTS, blocks * CAP)
    ffn_padded = jnp.concatenate([ffn_inputs, jnp.zeros((1, D), jnp.bfloat16)], axis=0)
    gates_padded = jnp.concatenate([gates.reshape(-1), jnp.zeros((1,), jnp.float32)], axis=0)

    def expert_rows(per_expert):
        assign_index, gate_weight, up_weight, down_weight = per_expert
        token_index = assign_index // TOPK
        rows = ffn_padded[token_index]
        gate_pre = jnp.dot(rows, gate_weight, preferred_element_type=jnp.float32)
        up_pre = jnp.dot(rows, up_weight, preferred_element_type=jnp.float32)
        gate_sig = jax.nn.sigmoid(gate_pre)
        activated = (gate_pre * gate_sig * up_pre).astype(jnp.bfloat16)
        expert_out = jnp.dot(activated, down_weight, preferred_element_type=jnp.float32).astype(jnp.bfloat16)
        return (token_index, rows, gate_pre, up_pre, gate_sig, activated, expert_out)

    def expert_forward(running, per_expert):
        token_index, rows, gate_pre, up_pre, gate_sig, activated, expert_out = expert_rows(per_expert)
        weight_rows = gates_padded[per_expert[0]]
        running = running.at[token_index].add(weight_rows[:, None] * expert_out.astype(jnp.float32))
        return (running, None)
    moe_sum, unused = lax.scan(expert_forward, jnp.zeros((count + 1, D), jnp.float32), (table, w_gate, w_up, w_down))
    output = hidden + RESIDUAL_SCALE * moe_sum[:count]
    mixed = output.astype(jnp.bfloat16).reshape(REPLICAS, GROUP_TOK, D)
    upstream = out_grad.reshape(count, D).astype(jnp.float32)
    moe_grad = RESIDUAL_SCALE * upstream
    moe_grad_padded = jnp.concatenate([moe_grad, jnp.zeros((1, D), jnp.float32)], axis=0)

    def expert_backward(running, per_expert):
        input_acc, gate_acc = running
        token_index, rows, gate_pre, up_pre, gate_sig, activated, expert_out = expert_rows(per_expert)
        gate_weight, up_weight, down_weight = (per_expert[1], per_expert[2], per_expert[3])
        weight_rows = gates_padded[per_expert[0]]
        grad_rows = moe_grad_padded[token_index]
        gate_acc = gate_acc.at[per_expert[0]].add(lax.optimization_barrier(jnp.sum(grad_rows * expert_out.astype(jnp.float32), axis=-1)))
        row_grad = (weight_rows[:, None] * grad_rows).astype(jnp.bfloat16)
        unit_grad = jnp.dot(row_grad, down_weight.T, preferred_element_type=jnp.float32)
        down_grad = jnp.dot(activated.T, row_grad, preferred_element_type=jnp.float32)
        gate_pre_grad = (unit_grad * up_pre * gate_sig * (1.0 + gate_pre * (1.0 - gate_sig))).astype(jnp.bfloat16)
        up_grad = (unit_grad * (gate_pre * gate_sig)).astype(jnp.bfloat16)
        gate_wgrad = jnp.dot(rows.T, gate_pre_grad, preferred_element_type=jnp.float32)
        up_wgrad = jnp.dot(rows.T, up_grad, preferred_element_type=jnp.float32)
        routed_grad = jnp.dot(gate_pre_grad, gate_weight.T, preferred_element_type=jnp.float32) + jnp.dot(up_grad, up_weight.T, preferred_element_type=jnp.float32)
        input_acc = input_acc.at[token_index].add(routed_grad.astype(jnp.bfloat16).astype(jnp.float32))
        return ((input_acc, gate_acc), (gate_wgrad, up_wgrad, down_grad))
    start_acc = (jnp.zeros((count + 1, D), jnp.float32), jnp.zeros((assign_total + 1,), jnp.float32))
    finals, stacked = lax.scan(expert_backward, start_acc, (table, w_gate, w_up, w_down))
    routed_sum, gate_grad_flat = finals
    grad_w_gate, grad_w_up, grad_w_down = stacked
    gate_grad = gate_grad_flat[:assign_total].reshape(count, TOPK)
    chosen_grad = gates * (gate_grad - lax.optimization_barrier(jnp.sum(gates * gate_grad, axis=-1, keepdims=True)))
    logit_grad = lax.optimization_barrier(jnp.sum(jnp.where(choose, chosen_grad[:, :, None], 0.0), axis=1)).astype(jnp.bfloat16)
    grad_w_router = jnp.dot(ffn_inputs.T, logit_grad, preferred_element_type=jnp.float32)
    ffn_input_grad = routed_sum[:count] + jnp.dot(logit_grad, w_router.T, preferred_element_type=jnp.float32)
    through_second, grad_ffn_gain = rms_backward(hidden, inv_second, second_gain, ffn_input_grad)
    hidden_grad = upstream + through_second
    branch_grad = (RESIDUAL_SCALE * hidden_grad).astype(jnp.bfloat16)
    grad_w_output = jnp.dot(attended_flat.T, branch_grad, preferred_element_type=jnp.float32)
    attended_grad = jnp.dot(branch_grad, w_output.T, preferred_element_type=jnp.float32).astype(jnp.bfloat16)
    attended_grad = attended_grad.reshape(blocks, TOK_DEV, KV_HEADS, group, HEAD_DIM)

    def backward_block(packed):
        keys_here, values_here, allowed = block_inputs(packed[1])
        return attention_backward(packed[0], keys_here, values_here, allowed, packed[2], packed[3], packed[4])
    query_grad, key_grad, value_grad = lax.map(backward_block, (queries, block_ids, attended, log_total, attended_grad))
    zero_rows = jnp.zeros((blocks, half, KV_HEADS, HEAD_DIM), jnp.float32)
    zero_block = jnp.zeros((1, half, KV_HEADS, HEAD_DIM), jnp.float32)
    key_next = jnp.concatenate([key_grad[1:, :half], zero_block], axis=0)
    value_next = jnp.concatenate([value_grad[1:, :half], zero_block], axis=0)
    key_total = (key_grad[:, half:] + jnp.concatenate([zero_rows, key_next], axis=1)).reshape(count, KV_HEADS, HEAD_DIM)
    value_total = (value_grad[:, half:] + jnp.concatenate([zero_rows, value_next], axis=1)).reshape(count, KV_HEADS, HEAD_DIM)
    query_pre = rotary_grad(query_grad.reshape(count, HEADS, HEAD_DIM), cos_table, sin_table).astype(jnp.bfloat16).reshape(count, HEADS * HEAD_DIM)
    key_pre = rotary_grad(key_total, cos_table, sin_table).astype(jnp.bfloat16).reshape(count, KV_HEADS * HEAD_DIM)
    value_pre = value_total.astype(jnp.bfloat16).reshape(count, KV_HEADS * HEAD_DIM)
    grad_w_query = jnp.dot(normed.T, query_pre, preferred_element_type=jnp.float32)
    grad_w_key = jnp.dot(normed.T, key_pre, preferred_element_type=jnp.float32)
    grad_w_value = jnp.dot(normed.T, value_pre, preferred_element_type=jnp.float32)
    attn_input_grad = jnp.dot(query_pre, w_query.T, preferred_element_type=jnp.float32) + jnp.dot(key_pre, w_key.T, preferred_element_type=jnp.float32) + jnp.dot(value_pre, w_value.T, preferred_element_type=jnp.float32)
    through_first, grad_attn_gain = rms_backward(inputs, inv_first, first_gain, attn_input_grad)
    grad_tokens = (upstream + through_first).astype(jnp.bfloat16).reshape(REPLICAS, GROUP_TOK, D)
    return (mixed, grad_tokens, grad_attn_gain, grad_w_query, grad_w_key, grad_w_value, grad_w_output, grad_ffn_gain, grad_w_router, grad_w_gate, grad_w_up, grad_w_down)
```

```python
import math

import jax
import jax.numpy as jnp
from jax import lax
from jax.sharding import PartitionSpec as P

D = 1024
HEADS = 16
KV_HEADS = 8
HEAD_DIM = 64
GROUP = HEADS // KV_HEADS
QW = HEADS * HEAD_DIM
KW = KV_HEADS * HEAD_DIM
TOK_DEV = 128
HALF = TOK_DEV // 2
EXP_DEV = 2
LANES = 128

EPSILON = 1e-06
RESIDUAL_SCALE = 0.22
SCORE_SCALE = 0.015625
ROPE_BASE = 10000.0
NEG_LARGE = -1e30

bf16 = jnp.bfloat16
f32 = jnp.float32


def dot(a, b, contract=((1,), (0,))):
    return lax.dot_general(a, b, (contract, ((), ())), preferred_element_type=f32)


def dot_t(a, b):
    return dot(a, b, ((1,), (1,)))


def t_dot(a, b):
    return dot(a, b, ((0,), (0,)))


def cycle(length):
    rows = 4 if length % 4 == 0 else 1
    cols = length // rows
    if cols == 1:
        return list(range(length))
    order = [z * cols for z in range(rows)]
    for k, z in enumerate(reversed(range(rows))):
        ys = list(range(1, cols))
        order += [z * cols + y for y in (ys if k % 2 == 0 else reversed(ys))]
    return order


class Ring:
    def __init__(self):
        n = self.n = lax.axis_size("shard")
        cyc = cycle(n)
        self.next = [(cyc[i], cyc[(i + 1) % n]) for i in range(n)]
        self.prev = [(b, a) for a, b in self.next]
        self.ahead, self.back = n // 2, (n - 1) // 2
        self.offsets = [0]
        for s in range(1, self.ahead + 1):
            self.offsets.append(-s)
            if s <= self.back:
                self.offsets.append(s)
        place = {dev: i for i, dev in enumerate(cyc)}
        table = [[cyc[(place[dev] + o) % n] for o in self.offsets] for dev in range(n)]
        row = lax.dynamic_index_in_dim(jnp.asarray(table, jnp.int32), lax.axis_index("shard"), 0, False)
        self.owners = [row[k] for k in range(n)]

    def gather(self, block):
        got = {0: block}
        ahead = back = block
        for s in range(1, self.ahead + 1):
            ahead = got[-s] = lax.ppermute(ahead, "shard", self.next)
            if s <= self.back:
                back = got[s] = lax.ppermute(back, "shard", self.prev)
        return [got[o] for o in self.offsets]

    def scatter(self, parts):
        part = dict(zip(self.offsets, parts))
        total = part[0].astype(f32)
        sums = {}
        for sign, steps, pairs in ((-1, self.ahead, self.prev), (1, self.back, self.next)):
            sums[sign] = part[sign * steps]
        for s in range(self.ahead, 0, -1):
            for sign, steps, pairs in ((-1, self.ahead, self.prev), (1, self.back, self.next)):
                if s > steps:
                    continue
                got = lax.ppermute(sums[sign], "shard", pairs).astype(f32)
                if s > 1:
                    sums[sign] = (got + part[sign * (s - 1)].astype(f32)).astype(bf16)
                else:
                    total = total + got
        return total

    def place(self, blocks):
        rows = blocks[0].shape[0]
        whole = jnp.zeros((self.n * rows, blocks[0].shape[1]), blocks[0].dtype)
        for owner, block in zip(self.owners, blocks):
            whole = lax.dynamic_update_slice_in_dim(whole, block, owner * rows, 0)
        return whole

    def cut(self, whole):
        rows = whole.shape[0] // self.n
        return [lax.dynamic_slice_in_dim(whole, owner * rows, rows, 0) for owner in self.owners]


def swap(value, bit):
    size = lax.axis_size("rep")
    return lax.ppermute(value, "rep", [(r, r ^ bit) for r in range(size)])


def bits():
    size, bit = lax.axis_size("rep"), 1
    while bit < size:
        yield bit
        bit *= 2


def rep_halving(value):
    size = lax.axis_size("rep")
    rep = lax.axis_index("rep")
    count, rows, width = value.shape
    own = rows // size
    left = size
    for bit in bits():
        left //= 2
        pairs = value.reshape(count, left, 2, own, width)
        here = (rep // bit) % 2
        keep = lax.dynamic_index_in_dim(pairs, here, 2, False)
        send = lax.dynamic_index_in_dim(pairs, 1 - here, 2, False)
        value = keep.astype(f32) + swap(send.astype(bf16), bit).astype(f32)
        if left > 1:
            value = value.astype(bf16)
    return value.reshape(count, own, width)


def rep_sum(value):
    for bit in list(bits())[1:]:
        low = lax.reduce_precision(value, 8, 7)
        value = low + swap(low.astype(bf16), bit).astype(f32)
    return value


def rms_forward(values, norm_gain):
    inv_rms = lax.rsqrt(jnp.mean(values * values, axis=-1, keepdims=True) + EPSILON)
    return (values * inv_rms * norm_gain, inv_rms)


def rms_backward(values, inv_rms, norm_gain, upstream):
    scaled = upstream * norm_gain
    through = inv_rms * scaled - values * (inv_rms * inv_rms * inv_rms) * jnp.mean(
        scaled * values, axis=-1, keepdims=True
    )
    gain_grad = jnp.sum(upstream * values * inv_rms, axis=0)
    return (through, gain_grad)


def rotary_tables(positions):
    indices = jnp.arange(HEAD_DIM // 2, dtype=f32)
    inverse = jnp.exp(indices * (-2.0 * math.log(ROPE_BASE) / HEAD_DIM))
    angles = positions.astype(f32)[:, None] * inverse[None, :]
    cos_table = jnp.concatenate([jnp.cos(angles), jnp.cos(angles)], axis=-1)[:, None, :]
    sin_table = jnp.concatenate([jnp.sin(angles), jnp.sin(angles)], axis=-1)[:, None, :]
    return (cos_table, sin_table)


def rotate_half(values):
    lower_half, upper_half = jnp.split(values, 2, axis=-1)
    return jnp.concatenate([-upper_half, lower_half], axis=-1)


def rotate_back(values):
    lower_half, upper_half = jnp.split(values, 2, axis=-1)
    return jnp.concatenate([upper_half, -lower_half], axis=-1)


def rotary_apply(values, cos_table, sin_table):
    return values * cos_table + rotate_half(values) * sin_table


def rotary_grad(upstream, cos_table, sin_table):
    return upstream * cos_table + rotate_back(upstream * sin_table)


def score_block(queries, key_rows, allowed):
    scores = (
        jnp.einsum("qkgd,pkd->kgqp", queries, key_rows, preferred_element_type=f32) * SCORE_SCALE
    )
    return jnp.where(allowed[None, None], scores, NEG_LARGE)


def attention_forward(queries, key_rows, value_rows, allowed):
    scores = score_block(queries, key_rows, allowed)
    highest = jnp.max(scores, axis=-1, keepdims=True)
    log_total = highest + jnp.log(jnp.sum(jnp.exp(scores - highest), axis=-1, keepdims=True))
    probs = jnp.exp(scores - log_total).astype(bf16)
    attended = jnp.einsum("kgqp,pkd->qkgd", probs, value_rows, preferred_element_type=f32)
    return (attended.astype(bf16), log_total)


def attention_backward(queries, key_rows, value_rows, allowed, attended, log_total, attended_grad):
    scores = score_block(queries, key_rows, allowed)
    probs = jnp.exp(scores - log_total)
    probs_low = probs.astype(bf16)
    value_grad = jnp.einsum("kgqp,qkgd->pkd", probs_low, attended_grad, preferred_element_type=f32)
    prob_grad = jnp.einsum("qkgd,pkd->kgqp", attended_grad, value_rows, preferred_element_type=f32)
    delta = jnp.einsum("qkgd,qkgd->kgq", attended_grad, attended, preferred_element_type=f32)[
        ..., None
    ]
    score_grad = (probs * (prob_grad - delta) * SCORE_SCALE).astype(bf16)
    query_grad = jnp.einsum("kgqp,pkd->qkgd", score_grad, key_rows, preferred_element_type=f32)
    key_grad = jnp.einsum("kgqp,qkgd->pkd", score_grad, queries, preferred_element_type=f32)
    return (query_grad, key_grad, value_grad)


def per_device(
    tokens,
    segment_ids,
    expert_ids,
    attn_gain,
    w_query,
    w_key,
    w_value,
    w_output,
    ffn_gain,
    w_router,
    w_gate,
    w_up,
    w_down,
    out_grad,
):
    shard = lax.axis_index("shard")
    core = lax.axis_index("rep") % 2
    first_core = core == 0
    ring = Ring()
    experts = EXP_DEV * ring.n
    rows = w_query.shape[0]

    def pick(a, b):
        return jnp.where(first_core, a, b)

    shift_up = [(i, i + 1) for i in range(ring.n - 1)]
    shift_down = [(i + 1, i) for i in range(ring.n - 1)]
    before = lax.ppermute(tokens[0, HALF:], "shard", shift_up)
    seg_before = lax.ppermute(segment_ids[0, HALF:], "shard", shift_up)

    small = jnp.concatenate([attn_gain[:, None], ffn_gain[:, None], w_router], axis=1)
    small = jnp.pad(small, ((0, 0), (0, LANES - small.shape[1])))
    mine = pick(w_query, jnp.concatenate([w_key, w_value], axis=1))
    first_blocks = ring.gather(jnp.concatenate([mine, small], axis=1))
    in_mine = ring.place([b[:, :QW] for b in first_blocks])
    small = ring.place([b[:, QW:] for b in first_blocks])
    in_other = swap(in_mine, 1)
    half_width = D // 2
    out_mine = ring.place(ring.gather(pick(w_output[:, :half_width], w_output[:, half_width:])))
    out_other = swap(out_mine, 1)
    first_gain = small[:, 0].astype(f32)
    second_gain = small[:, 1].astype(f32)
    router = small[:, 2 : 2 + experts]

    expert_range = jnp.arange(experts, dtype=jnp.int32)
    chosen = jnp.any(expert_ids[0][:, :, None] == expert_range, axis=1).astype(bf16)
    chosen = jnp.pad(chosen, ((0, 0), (0, LANES - experts)))
    up_blocks = ring.gather(jnp.concatenate([out_grad[0], chosen], axis=1))
    group_grad = jnp.concatenate([b[:, :D] for b in up_blocks], axis=0)
    group_chosen = jnp.concatenate([b[:, D : D + experts] for b in up_blocks], axis=0) > 0

    inputs = tokens[0].astype(f32)
    normed_f, inv_first = rms_forward(inputs, first_gain)
    normed = normed_f.astype(bf16)
    normed_before = rms_forward(before.astype(f32), first_gain)[0].astype(bf16)
    normed_window = jnp.concatenate([normed_before, normed], axis=0)
    window_place = jnp.arange(TOK_DEV + HALF, dtype=jnp.int32)
    cos_window, sin_window = rotary_tables(window_place % TOK_DEV)
    cos_table, sin_table = cos_window[HALF:], sin_window[HALF:]
    lin_mine = dot(normed_window, in_mine)
    lin_other = dot(normed_window, in_other)
    query_lin = pick(lin_mine[HALF:], lin_other[HALF:]).reshape(TOK_DEV, HEADS, HEAD_DIM)
    queries = (
        rotary_apply(query_lin, cos_table, sin_table)
        .astype(bf16)
        .reshape(TOK_DEV, KV_HEADS, GROUP, HEAD_DIM)
    )
    kv_lin = pick(lin_other, lin_mine)
    key_lin = kv_lin[:, :KW].reshape(TOK_DEV + HALF, KV_HEADS, HEAD_DIM)
    key_rows = rotary_apply(key_lin, cos_window, sin_window).astype(bf16)
    value_rows = kv_lin[:, KW:].astype(bf16).reshape(TOK_DEV + HALF, KV_HEADS, HEAD_DIM)
    seg_own = segment_ids[0]
    seg_keys = jnp.concatenate([seg_before, seg_own], axis=0)
    query_place = jnp.arange(TOK_DEV, dtype=jnp.int32)
    key_place = window_place - HALF
    seq_query = (query_place + HALF) // TOK_DEV
    seq_key = window_place // TOK_DEV
    allowed = (key_place[None, :] <= query_place[:, None]) & (
        seq_key[None, :] == seq_query[:, None]
    )
    allowed = allowed & (seg_keys[None, :] == seg_own[:, None])
    allowed = allowed & ((key_place[None, :] >= 0) | (shard > 0))
    attended, log_total = attention_forward(queries, key_rows, value_rows, allowed)
    attended_flat = attended.reshape(TOK_DEV, QW)
    proj_mine = dot(attended_flat, out_mine)
    proj_other = dot(attended_flat, out_other)
    proj = jnp.concatenate([pick(proj_mine, proj_other), pick(proj_other, proj_mine)], axis=1)
    hidden = inputs + RESIDUAL_SCALE * proj
    ffn_f, inv_second = rms_forward(hidden, second_gain)
    ffn_inputs = ffn_f.astype(bf16)

    group_in = jnp.concatenate(ring.gather(ffn_inputs), axis=0)
    logits = jnp.where(group_chosen, dot(group_in, router), NEG_LARGE)
    raised = jnp.where(
        group_chosen, jnp.exp(logits - jnp.max(logits, axis=-1, keepdims=True)), 0.0
    )
    gates = raised / jnp.sum(raised, axis=-1, keepdims=True)
    moe_grad = RESIDUAL_SCALE * group_grad.astype(f32)
    mix = 0.0
    routed = 0.0
    gate_cols = 0.0
    wgrads = []
    for e in range(EXP_DEV):
        here = expert_range[None, :] == shard * EXP_DEV + e
        gate = jnp.sum(jnp.where(here, gates, 0.0), axis=-1, keepdims=True)
        gate_pre = dot(group_in, w_gate[e])
        up_pre = dot(group_in, w_up[e])
        gate_sig = jax.nn.sigmoid(gate_pre)
        activated = (gate_pre * gate_sig * up_pre).astype(bf16)
        expert_out = dot(activated, w_down[e]).astype(bf16).astype(f32)
        mix = mix + gate * expert_out
        gate_grad = jnp.sum(moe_grad * expert_out, axis=-1, keepdims=True)
        gate_cols = gate_cols + jnp.where(here, gate_grad, 0.0)
        row_grad = (gate * moe_grad).astype(bf16)
        unit_grad = dot_t(row_grad, w_down[e])
        gate_pre_grad = (
            unit_grad * up_pre * gate_sig * (1.0 + gate_pre * (1.0 - gate_sig))
        ).astype(bf16)
        up_grad = (unit_grad * (gate_pre * gate_sig)).astype(bf16)
        routed = routed + dot_t(gate_pre_grad, w_gate[e]) + dot_t(up_grad, w_up[e])
        wgrads.append(
            (
                t_dot(group_in, gate_pre_grad).astype(bf16),
                t_dot(group_in, up_grad).astype(bf16),
                t_dot(activated, row_grad).astype(bf16),
            )
        )
    high = lax.reduce_precision(gate_cols, 8, 7)
    low = (gate_cols - high).astype(bf16)
    back = jnp.concatenate([routed.astype(bf16), high.astype(bf16), low], axis=1)
    back = jnp.pad(back, ((0, 0), (0, LANES - 2 * experts)))
    back = ring.scatter(jnp.split(back, ring.n, axis=0))
    routed_sum = back[:, :D]
    gate_grad = back[:, D : D + experts] + back[:, D + experts : D + 2 * experts]
    moe_sum = ring.scatter(jnp.split(mix.astype(bf16), ring.n, axis=0))
    mixed = (hidden + RESIDUAL_SCALE * moe_sum).astype(bf16)
    expert_sums = [rep_halving(jnp.stack(g)) for g in zip(*wgrads)]

    upstream = out_grad[0].astype(f32)
    own_gates = gates[:TOK_DEV]
    logit_grad = (
        own_gates * (gate_grad - jnp.sum(own_gates * gate_grad, axis=-1, keepdims=True))
    ).astype(bf16)
    router_grad = t_dot(ffn_inputs, logit_grad)
    ffn_input_grad = routed_sum + dot_t(logit_grad, router)
    through_second, ffn_gain_grad = rms_backward(hidden, inv_second, second_gain, ffn_input_grad)
    hidden_grad = upstream + through_second
    branch_grad = (RESIDUAL_SCALE * hidden_grad).astype(bf16)
    branch_mine = pick(branch_grad[:, :half_width], branch_grad[:, half_width:])
    branch_other = pick(branch_grad[:, half_width:], branch_grad[:, :half_width])

    def chip_sum(keep, send, extra):
        extra = jnp.pad(extra, ((0, 0), (0, LANES - extra.shape[1])))
        got = swap(jnp.concatenate([send, extra], axis=1).astype(bf16), 1).astype(f32)
        extra = lax.reduce_precision(extra, 8, 7)
        return (jnp.concatenate([keep, extra], axis=1) + got).astype(bf16)

    def owned(chip):
        return rep_sum(ring.scatter(ring.cut(chip)))

    out_grads = chip_sum(
        t_dot(attended_flat, branch_mine),
        t_dot(attended_flat, branch_other),
        jnp.concatenate([ffn_gain_grad[:, None], router_grad], axis=1),
    )
    out_sum = owned(out_grads)
    attended_grad = (
        (dot_t(branch_mine, out_mine) + dot_t(branch_other, out_other))
        .astype(bf16)
        .reshape(TOK_DEV, KV_HEADS, GROUP, HEAD_DIM)
    )
    query_grad, key_grad, value_grad = attention_backward(
        queries, key_rows, value_rows, allowed, attended, log_total, attended_grad
    )
    later = lax.ppermute(
        jnp.concatenate(
            [key_grad[:HALF].reshape(HALF, KW), value_grad[:HALF].reshape(HALF, KW)], axis=1
        ),
        "shard",
        shift_down,
    )
    later = jnp.pad(later, ((HALF, 0), (0, 0)))
    key_total = key_grad[HALF:] + later[:, :KW].reshape(TOK_DEV, KV_HEADS, HEAD_DIM)
    value_total = value_grad[HALF:].reshape(TOK_DEV, KW) + later[:, KW:]
    query_pre = (
        rotary_grad(query_grad.reshape(TOK_DEV, HEADS, HEAD_DIM), cos_table, sin_table)
        .astype(bf16)
        .reshape(TOK_DEV, QW)
    )
    key_pre = rotary_grad(key_total, cos_table, sin_table).astype(bf16).reshape(TOK_DEV, KW)
    kv_pre = jnp.concatenate([key_pre, value_total.astype(bf16)], axis=1)
    pre_mine = pick(query_pre, kv_pre)
    pre_other = pick(kv_pre, query_pre)
    attn_input_grad = dot_t(pre_mine, in_mine) + dot_t(pre_other, in_other)
    through_first, attn_gain_grad = rms_backward(inputs, inv_first, first_gain, attn_input_grad)
    input_grad = (upstream + through_first).astype(bf16)
    in_sum = owned(
        chip_sum(t_dot(normed, pre_mine), t_dot(normed, pre_other), attn_gain_grad[:, None])
    )

    in_own = in_sum[:, :QW]
    in_got = swap(in_own, 1)
    out_own = out_sum[:, :half_width]
    out_got = swap(out_own, 1)
    kv_sum = pick(in_got, in_own)
    return (
        mixed[None],
        input_grad[None],
        in_sum[:, QW],
        pick(in_own, in_got),
        kv_sum[:, :KW],
        kv_sum[:, KW:],
        jnp.concatenate([pick(out_own, out_got), pick(out_got, out_own)], axis=1),
        out_sum[:, half_width],
        out_sum[:, half_width + 1 : half_width + 1 + experts],
        expert_sums[0],
        expert_sums[1],
        expert_sums[2],
    )


def solution(mesh):
    return jax.shard_map(
        per_device,
        mesh=mesh,
        in_specs=(
            P("rep", "shard", None),
            P("rep", "shard"),
            P("rep", "shard", None),
            P("shard"),
            P("shard", None),
            P("shard", None),
            P("shard", None),
            P("shard", None),
            P("shard"),
            P("shard", None),
            P("shard", None, None),
            P("shard", None, None),
            P("shard", None, None),
            P("rep", "shard", None),
        ),
        out_specs=(
            P("rep", "shard", None),
            P("rep", "shard", None),
            P("shard"),
            P("shard", None),
            P("shard", None),
            P("shard", None),
            P("shard", None),
            P("shard"),
            P("shard", None),
            P("shard", "rep", None),
            P("shard", "rep", None),
            P("shard", "rep", None),
        ),
        check_vma=False,
    )
```

```python
import functools

import jax
import jax.numpy as jnp
import numpy as np
from jax import lax
from jax.experimental import pallas as pl
from jax.experimental.pallas import tpu as pltpu
from jax.sharding import PartitionSpec as P

D = 1024
HEADS = 16
KV_HEADS = 8
HEAD_DIM = 64
GROUP = HEADS // KV_HEADS
QW = HEADS * HEAD_DIM
KW = KV_HEADS * HEAD_DIM
QC = QW // 2
KC = KW // 2
TOK_DEV = 128
HALF = TOK_DEV // 2
HALO = TOK_DEV + HALF
SEG_ROWS = 16
EXP_DEV = 2
LANES = 128

EPSILON = 1e-06
RESIDUAL_SCALE = 0.22
SCORE_SCALE = 0.015625
ROPE_BASE = 10000.0
NEG_LARGE = -1e30

bf16 = jnp.bfloat16
f32 = jnp.float32


def dot(a, b, contract=((1,), (0,))):
    return lax.dot_general(a, b, (contract, ((), ())), preferred_element_type=f32)


def dot_t(a, b):
    return dot(a, b, ((1,), (1,)))


def t_dot(a, b):
    return dot(a, b, ((0,), (0,)))


def cycle(length):
    rows = 4 if length % 4 == 0 else 1
    cols = length // rows
    if cols == 1:
        return list(range(length))
    order = [z * cols for z in range(rows)]
    for k, z in enumerate(reversed(range(rows))):
        ys = list(range(1, cols))
        order += [z * cols + y for y in (ys if k % 2 == 0 else reversed(ys))]
    return order


class Ring:
    def __init__(self):
        n = self.n = lax.axis_size("shard")
        cyc = self.cyc = cycle(n)
        self.next = [(cyc[i], cyc[(i + 1) % n]) for i in range(n)]
        self.prev = [(b, a) for a, b in self.next]
        self.ahead, self.back = n // 2, (n - 1) // 2
        self.offsets = [0, -self.ahead]
        for s in range(1, self.back + 1):
            self.offsets += [-s, s]
        place = {dev: i for i, dev in enumerate(cyc)}
        table = [[cyc[(place[dev] + o) % n] for o in self.offsets] for dev in range(n)]
        row = lax.dynamic_index_in_dim(jnp.asarray(table, jnp.int32), lax.axis_index("shard"), 0, False)
        self.row = row


class Gather:
    def __init__(self, ring, block):
        self.ring, self.got, self.done = ring, {0: block}, 0

    @property
    def left(self):
        return self.ring.ahead - self.done

    def step(self):
        s = self.done = self.done + 1
        new = [-s]
        self.got[-s] = lax.ppermute(self.got[1 - s], "shard", self.ring.next)
        if s <= self.ring.back:
            new.append(s)
            self.got[s] = lax.ppermute(self.got[s - 1], "shard", self.ring.prev)
        return new

    def blocks(self):
        return [self.got[o] for o in self.ring.offsets]


class Scatter:
    def __init__(self, ring, parts):
        self.part = dict(zip(ring.offsets, parts))
        self.ways = ((-1, ring.ahead, ring.prev), (1, ring.back, ring.next))
        self.sums = {sign: self.part[sign * steps] for sign, steps, _ in self.ways}
        self.left = ring.ahead
        self.got = {}

    def step(self):
        for sign, got in self.got.items():
            part = self.part[sign * self.left].astype(f32)
            self.sums[sign] = (got.astype(f32) + part).astype(bf16)
        self.got = {
            sign: lax.ppermute(self.sums[sign], "shard", pairs)
            for sign, steps, pairs in self.ways
            if self.left <= steps
        }
        self.left -= 1

    def terms(self):
        return self.part[0], self.got[-1], self.got[1]


def after(value, *earlier):
    return lax.optimization_barrier((value, *earlier))[0] if earlier else value


def together(*values):
    return lax.optimization_barrier(values)


def swap(value, bit):
    size = lax.axis_size("rep")
    return lax.ppermute(value, "rep", [(r, r ^ bit) for r in range(size)])


def bits():
    size, bit = lax.axis_size("rep"), 1
    while bit < size:
        yield bit
        bit *= 2


def rep_sum(value):
    for bit in list(bits())[1:]:
        low = lax.reduce_precision(value, 8, 7)
        value = low + swap(low.astype(bf16), bit).astype(f32)
    return value


def rotary_tables():
    positions = (np.arange(2 * TOK_DEV) + HALF) % TOK_DEV
    inverse = ROPE_BASE ** (-2.0 * np.arange(HEAD_DIM // 2) / HEAD_DIM)
    angles = positions[:, None] * inverse[None, :]
    cos, sin = np.cos(angles), np.sin(angles)
    cos, sin = np.concatenate([cos] * 4, axis=1), np.concatenate([-sin, sin] * 2, axis=1)
    return jnp.asarray(cos, f32), jnp.asarray(sin, f32)


def lane_index(shape):
    return lax.broadcasted_iota(jnp.int32, shape, 1)


def rotate(values, cos, sin):
    first = lane_index(values.shape) % HEAD_DIM < HEAD_DIM // 2
    turned = jnp.where(first, pltpu.roll(values, LANES - 32, 1), pltpu.roll(values, 32, 1))
    return values * cos + turned * sin


def rotate_back(values, cos, sin):
    first = lane_index(values.shape) % HEAD_DIM < HEAD_DIM // 2
    moved = values * sin
    turned = jnp.where(first, pltpu.roll(moved, LANES - 32, 1), pltpu.roll(moved, 32, 1))
    return values * cos + turned


def apart(pair):
    pair = pair.astype(f32)
    turned = pltpu.roll(pair, HEAD_DIM, 1)
    low = lane_index(pair.shape) < HEAD_DIM
    zero = jnp.zeros_like(pair)
    return (
        (jnp.where(low, pair, zero).astype(bf16), jnp.where(low, zero, turned).astype(bf16)),
        (jnp.where(low, turned, zero).astype(bf16), jnp.where(low, zero, pair).astype(bf16)),
    )


def allowed_pairs(shard_index, packet_ref):
    seg_before = packet_ref[HALO : HALO + 1, :LANES].astype(f32)
    seg_own = packet_ref[HALO + SEG_ROWS : HALO + SEG_ROWS + 1, :LANES].astype(f32)
    seg_key = jnp.concatenate([seg_before, seg_own], 1)
    seg_query = jnp.broadcast_to(seg_own, (TOK_DEV, TOK_DEV)).T[:, :1]
    shape = (TOK_DEV, 2 * TOK_DEV)
    query = lax.broadcasted_iota(jnp.int32, shape, 0)
    key = lax.broadcasted_iota(jnp.int32, shape, 1) - TOK_DEV
    allowed = (key <= query) & (key >= -HALF) & ((query >= HALF) == (key >= HALF))
    return allowed & ((key >= 0) | (shard_index > 0)) & (seg_query == seg_key)


def inverse_rms(values):
    return lax.rsqrt(jnp.mean(values * values, axis=-1, keepdims=True) + EPSILON)


def vmem(shape, dtype):
    return jax.ShapeDtypeStruct(shape, dtype)


def call(kernel, out_shape, scalars, arrays, scratch=(), flops=0, limit=60, anywhere=(), out_space=None):
    return pl.pallas_call(
        kernel,
        in_specs=[pl.BlockSpec(memory_space=pltpu.SMEM)] * len(scalars)
        + [pl.BlockSpec()] * len(arrays)
        + [pl.BlockSpec(memory_space=pl.ANY)] * len(anywhere),
        out_specs=[pl.BlockSpec(memory_space=out_space) if out_space else pl.BlockSpec()] * len(out_shape),
        out_shape=out_shape,
        scratch_shapes=list(scratch),
        compiler_params=pltpu.CompilerParams(vmem_limit_bytes=limit * 2**20),
        cost_estimate=pl.CostEstimate(flops=flops, bytes_accessed=2**22, transcendentals=0),
    )(*scalars, *arrays, *anywhere)


SMALL_ROWS = 16


def split_kernel(place_ref, gains_ref, router_ref, ids_ref, wq_ref, wk_ref, wv_ref, wo_ref, mine, out_mine, out_other):
    half = D // 2
    experts, rows = router_ref.shape
    ids = ids_ref[...]
    expert = lax.broadcasted_iota(jnp.int32, (experts, TOK_DEV), 0)
    chosen = jnp.zeros((experts, TOK_DEV), f32)
    for k in range(ids.shape[0]):
        chosen = jnp.where(expert == ids[k : k + 1], 1.0, chosen)
    mine[rows:] = jnp.zeros((SMALL_ROWS, D), bf16)
    mine[rows : rows + 1, :rows] = gains_ref[:1]
    mine[rows + 1 : rows + 2, :rows] = gains_ref[1:]
    for t in range(experts // SMALL_ROWS):
        part = slice(t * SMALL_ROWS, (t + 1) * SMALL_ROWS)
        at = (1 + t) * LANES
        mine[rows:, at : at + rows] = router_ref[part]
        at = (1 + t + experts // SMALL_ROWS) * LANES
        mine[rows:, at : at + LANES] = chosen[part].astype(bf16)
    for core in range(2):

        @pl.when(place_ref[1] == core)
        def _(core=core):
            mine[:rows, :QC] = wq_ref[:, core * QC : (core + 1) * QC]
            mine[:rows, QC : QC + KC] = wk_ref[:, core * KC : (core + 1) * KC]
            mine[:rows, QC + KC :] = wv_ref[:, core * KC : (core + 1) * KC]
            out_mine[...] = wo_ref[:, core * half : (core + 1) * half]
            out_other[...] = wo_ref[:, (1 - core) * half : (2 - core) * half]


def put_lanes(ref, piece, owner, rows):
    start = owner * rows
    at = pl.ds(pl.multiple_of(start // LANES * LANES, LANES), LANES)
    if rows < LANES:
        off = start % LANES
        lane = lane_index(piece.shape)
        piece = pltpu.roll(piece, off, 1)
        piece = jnp.where((lane >= off) & (lane < off + rows), piece, ref[:, at])
    ref[:, at] = piece


def fetch(n, rows, owner_ref, pairs, sems, small=None):
    copies = []
    for blocks, target in pairs:
        for k in range(n):
            at = pl.ds(pl.multiple_of(owner_ref[k] * rows, rows), rows)
            copies.append(pltpu.make_async_copy(blocks[k].at[pl.ds(0, rows)], target.at[at], sems.at[len(copies)]))
    for k in range(n if small is not None else 0):
        source = pairs[0][0][k].at[pl.ds(rows, SMALL_ROWS)]
        copies.append(pltpu.make_async_copy(source, small.at[k], sems.at[len(copies)]))
    for copy in copies:
        copy.start()
    return copies


def attention_kernel(n, rows, place_ref, owner_ref, own_ref, other_ref, cos_ref, sin_ref, *refs):
    blocks = refs[:n]
    w_ref, small_ref, gain_ref, normed_ref, inv_ref, q_ref, k_ref, v_ref, lse_ref, *att_refs, window, sems = refs[n:]
    copies = fetch(n, rows, owner_ref, ((blocks, w_ref),), sems, small_ref)
    packets = (own_ref, other_ref)
    scaled = []
    for g, packet in enumerate(packets):
        values = packet[:HALO].astype(f32)
        inv = inverse_rms(values)
        inv_ref[g * TOK_DEV : (g + 1) * TOK_DEV] = inv[:TOK_DEV]
        scaled.append(values * inv)
    for k in range(n):
        copies[n + k].wait()
    for k in range(n):
        put_lanes(gain_ref, small_ref[k, :1, :LANES].astype(f32), owner_ref[k], rows)
    gain = gain_ref[...]
    for g in range(2):
        base = 2 * TOK_DEV * g
        normed = (scaled[g] * gain).astype(bf16)
        window[base : base + HALF] = jnp.zeros((HALF, D), bf16)
        window[base + HALF : base + TOK_DEV] = normed[TOK_DEV:]
        window[base + TOK_DEV : base + 2 * TOK_DEV] = normed[:TOK_DEV]
        normed_ref[g * TOK_DEV : (g + 1) * TOK_DEV] = normed[:TOK_DEV]
    for copy in copies[:n]:
        copy.wait()
    q_both = dot(normed_ref[...], w_ref[:, :QC])
    kv_both = dot(window[...], w_ref[:, QC:])
    cos, sin = cos_ref[...], sin_ref[...]
    lane = lane_index((TOK_DEV, LANES))
    for g in range(2):
        tok = slice(g * TOK_DEV, (g + 1) * TOK_DEV)
        win = slice(2 * g * TOK_DEV, 2 * (g + 1) * TOK_DEV)
        q_lin, kv_lin = q_both[tok], kv_both[win]
        allowed = allowed_pairs(place_ref[0], packets[g])
        v_ref[win] = kv_lin[:, KC:].astype(bf16)
        lse = jnp.zeros((TOK_DEV, LANES), f32)
        for pair in range(KC // LANES):
            cols = slice(pair * LANES, (pair + 1) * LANES)
            keys = rotate(kv_lin[:, cols], cos, sin)
            k_ref[win, cols] = keys.astype(bf16)
            key_sides = apart(keys)
            value_sides = apart(kv_lin[:, KC + pair * LANES : KC + (pair + 1) * LANES])
            for one in range(2):
                head = 2 * pair + one
                q_cols = slice(head * LANES, (head + 1) * LANES)
                queries = rotate(q_lin[:, q_cols], cos[TOK_DEV:], sin[TOK_DEV:]).astype(bf16)
                q_ref[tok, q_cols] = queries
                out = 0.0
                for side in range(2):
                    scores = dot_t(queries, key_sides[one][side]) * SCORE_SCALE
                    scores = jnp.where(allowed, scores, NEG_LARGE)
                    highest = jnp.max(scores, -1, keepdims=True)
                    raised = jnp.exp(scores - highest)
                    log_total = highest + jnp.log(jnp.sum(raised, -1, keepdims=True))
                    lse = jnp.where(lane == 2 * head + side, log_total, lse)
                    probs = jnp.exp(scores - log_total).astype(bf16)
                    out = out + dot(probs, value_sides[one][side])
                att_refs[g][:, q_cols] = out.astype(bf16)
        lse_ref[tok] = lse


def output_kernel(n, rows, experts, place_ref, owner_ref, own_ref, got_ref, tok_ref, small_ref, *refs):
    mine, other = refs[:n], refs[n : 2 * n]
    w_mine, w_other, gain_ref, router_ref, chosen_ref, hidden_ref, inv_ref, ffn_ref, att_ref, router, sems = refs[2 * n :]
    copies = fetch(n, rows, owner_ref, ((mine, w_mine), (other, w_other)), sems)
    for k in range(n):
        tiles = [small_ref[k, :, i * LANES : (i + 1) * LANES].astype(f32) for i in range(1 + 2 * experts // SMALL_ROWS)]
        put_lanes(gain_ref, tiles[0][1:2], owner_ref[k], rows)
        put_lanes(router, jnp.concatenate(tiles[1 : 1 + experts // SMALL_ROWS], 0), owner_ref[k], rows)
        chosen = jnp.concatenate(tiles[1 + experts // SMALL_ROWS :], 0)
        chosen = jnp.concatenate([chosen, jnp.zeros((LANES - experts, LANES), f32)], 0).T
        chosen_ref[k * TOK_DEV : (k + 1) * TOK_DEV] = chosen[:, :experts]
    router_ref[...] = router[...].astype(bf16)
    first_core = place_ref[1] == 0
    own, got = own_ref[...].astype(f32), got_ref[...].astype(f32)
    att_ref[:, :QC] = jnp.where(first_core, own, got).astype(bf16)
    att_ref[:, QC:] = jnp.where(first_core, got, own).astype(bf16)
    for copy in copies:
        copy.wait()
    out_mine, out_other = dot(att_ref[...], w_mine[...]), dot(att_ref[...], w_other[...])
    proj = jnp.concatenate(
        [jnp.where(first_core, out_mine, out_other), jnp.where(first_core, out_other, out_mine)], 1
    )
    hidden = tok_ref[...].astype(f32) + RESIDUAL_SCALE * proj
    hidden_ref[...] = hidden
    inv = inverse_rms(hidden)
    inv_ref[...] = inv
    ffn_ref[...] = (hidden * inv * gain_ref[...]).astype(bf16)


def block_lanes(ref, row, owner, rows):
    start = owner * rows
    piece = ref[row : row + 1, pl.ds(pl.multiple_of(start // LANES * LANES, LANES), LANES)]
    if rows < LANES:
        piece = pltpu.roll(piece, (LANES - start % LANES) % LANES, 1)
    return piece


def hidden_grad_kernel(experts, place_ref, back0_ref, back1_ref, back2_ref, gates_ref, ffn_ref, hidden_ref, inv_ref, gain_ref, router_ref, up_ref, att_ref, w_mine, w_other, ag_own_ref, ag_send_ref, send_ref, keep_ref, small_ref):
    back = back0_ref[...].astype(f32) + back1_ref[...].astype(f32) + back2_ref[...].astype(f32)
    gate_grad = back[:, D : D + experts] + back[:, D + experts : D + 2 * experts]
    gates = gates_ref[...]
    logit_grad = (gates * (gate_grad - jnp.sum(gates * gate_grad, -1, keepdims=True))).astype(bf16)
    hidden, inv, gain = hidden_ref[...], inv_ref[...], gain_ref[...]
    grad = back[:, :D] + dot(logit_grad, router_ref[...])
    scaled = grad * gain
    through = inv * scaled - hidden * (inv * inv * inv) * jnp.mean(scaled * hidden, -1, keepdims=True)
    hidden_grad = up_ref[...].astype(f32) + through
    small_ref[:experts] = t_dot(logit_grad, ffn_ref[...])
    small_ref[experts : experts + 1] = jnp.sum(grad * hidden * inv, 0, keepdims=True)
    branch = (RESIDUAL_SCALE * hidden_grad).astype(bf16)
    half = D // 2
    first_core = place_ref[1] == 0
    b_mine = jnp.where(first_core, branch[:, :half].astype(f32), branch[:, half:].astype(f32)).astype(bf16)
    b_other = jnp.where(first_core, branch[:, half:].astype(f32), branch[:, :half].astype(f32)).astype(bf16)
    ag = dot_t(b_mine, w_mine[...]) + dot_t(b_other, w_other[...])
    ag_own_ref[...] = jnp.where(first_core, ag[:, :QC], ag[:, QC:]).astype(bf16)
    ag_send_ref[...] = jnp.where(first_core, ag[:, QC:], ag[:, :QC]).astype(bf16)
    send_ref[...] = t_dot(att_ref[...], b_other).astype(bf16)
    keep_ref[...] = t_dot(att_ref[...], b_mine).astype(bf16)


def attention_grad_kernel(place_ref, own_ref, other_ref, q_ref, k_ref, v_ref, lse_ref, att_own_ref, att_other_ref, ag_own_ref, ag_other_ref, cos_ref, sin_ref, q_pre_ref, kv_own_ref, kv_before_ref):
    cos, sin = cos_ref[...], sin_ref[...]
    low = lane_index((TOK_DEV, LANES)) < HEAD_DIM
    groups = ((own_ref, att_own_ref, ag_own_ref), (other_ref, att_other_ref, ag_other_ref))
    for g, (packet_ref, att_ref, ag_ref) in enumerate(groups):
        tok = slice(g * TOK_DEV, (g + 1) * TOK_DEV)
        win = slice(2 * g * TOK_DEV, 2 * (g + 1) * TOK_DEV)
        halo = slice(g * HALF, (g + 1) * HALF)
        allowed = allowed_pairs(place_ref[0], packet_ref)
        for pair in range(KC // LANES):
            cols = slice(pair * LANES, (pair + 1) * LANES)
            key_sides, value_sides = apart(k_ref[win, cols]), apart(v_ref[win, cols])
            key_grad = jnp.zeros((2 * TOK_DEV, LANES), f32)
            value_grad = jnp.zeros((2 * TOK_DEV, LANES), f32)
            for one in range(2):
                head = 2 * pair + one
                q_cols = slice(head * LANES, (head + 1) * LANES)
                queries, grads = q_ref[tok, q_cols], ag_ref[:, q_cols]
                query_sides, grad_sides = apart(queries), apart(grads)
                product = grads.astype(f32) * att_ref[:, q_cols].astype(f32)
                query_grad = jnp.zeros((TOK_DEV, LANES), f32)
                for side in range(2):
                    k_side, v_side = key_sides[one][side], value_sides[one][side]
                    log_total = lse_ref[tok, 2 * head + side : 2 * head + side + 1]
                    delta = jnp.sum(jnp.where(low == (side == 0), product, 0.0), -1, keepdims=True)
                    scores = dot_t(queries, k_side) * SCORE_SCALE
                    probs = jnp.where(allowed, jnp.exp(scores - log_total), 0.0)
                    prob_grad = dot_t(grads, v_side)
                    score_grad = (probs * (prob_grad - delta) * SCORE_SCALE).astype(bf16)
                    query_grad = query_grad + dot(score_grad, k_side)
                    key_grad = key_grad + t_dot(score_grad, query_sides[side][one])
                    value_grad = value_grad + t_dot(probs.astype(bf16), grad_sides[side][one])
                q_pre_ref[tok, q_cols] = rotate_back(query_grad, cos[TOK_DEV:], sin[TOK_DEV:]).astype(bf16)
            v_cols = slice(KC + pair * LANES, KC + (pair + 1) * LANES)
            key_grad = rotate_back(key_grad, cos, sin)
            kv_own_ref[tok, cols] = key_grad[TOK_DEV:]
            kv_own_ref[tok, v_cols] = value_grad[TOK_DEV:]
            kv_before_ref[halo, cols] = key_grad[HALF:TOK_DEV].astype(bf16)
            kv_before_ref[halo, v_cols] = value_grad[HALF:TOK_DEV].astype(bf16)


def projection_grad_kernel(n, rows, owner_ref, q_pre_ref, kv_own_ref, later_ref, normed_ref, w_ref, own_ref, other_ref, inv_ref, *refs):
    blocks, (aig_own_ref, aig_send_ref, grads, gain_grad) = refs[:n], refs[n:]
    kv, later = kv_own_ref[...], later_ref[...].astype(f32)
    parts = []
    for g in range(2):
        at = g * TOK_DEV
        parts += [kv[at : at + HALF], kv[at + HALF : at + TOK_DEV] + later[g * HALF : (g + 1) * HALF]]
    pre = jnp.concatenate([q_pre_ref[...], jnp.concatenate(parts, 0).astype(bf16)], 1)
    grads[...] = t_dot(normed_ref[...], pre)
    aig = dot_t(pre, w_ref[...])
    values = jnp.concatenate([own_ref[:TOK_DEV], other_ref[:TOK_DEV]], 0).astype(f32)
    gain_grad[...] = jnp.sum(aig * values * inv_ref[...], 0, keepdims=True)
    for k in range(n):
        at = pl.ds(pl.multiple_of(owner_ref[k] * rows, rows), rows)
        blocks[k][:rows] = grads[at, :].astype(bf16)
        blocks[k][rows:] = jnp.zeros((blocks[k].shape[0] - rows, D), bf16)
        blocks[k][rows : rows + 1, :LANES] = block_lanes(gain_grad, 0, owner_ref[k], rows).astype(bf16)
    aig_own_ref[...] = aig[:TOK_DEV]
    aig_send_ref[...] = aig[TOK_DEV:]


def input_grad_kernel(aig_ref, got_ref, own_ref, inv_ref, gain_ref, up_ref, out_ref):
    grad = aig_ref[...] + got_ref[...]
    values, inv = own_ref[:TOK_DEV].astype(f32), inv_ref[:TOK_DEV]
    scaled = grad * gain_ref[...]
    through = inv * scaled - values * (inv * inv * inv) * jnp.mean(scaled * values, -1, keepdims=True)
    out_ref[...] = (up_ref[...].astype(f32) + through).astype(bf16)


def assemble_kernel(place_ref, in_own, in_got, out_own, out_got, wq_ref, wk_ref, wv_ref, wo_ref):
    rows = wq_ref.shape[0]
    half = D // 2
    for core, first, second, low, high in ((0, in_own, in_got, out_own, out_got), (1, in_got, in_own, out_got, out_own)):

        @pl.when(place_ref[1] == core)
        def _(sides=((first, low), (second, high))):
            for c, (into, out) in enumerate(sides):
                wq_ref[:, c * QC : (c + 1) * QC] = into[:rows, :QC]
                wk_ref[:, c * KC : (c + 1) * KC] = into[:rows, QC : QC + KC]
                wv_ref[:, c * KC : (c + 1) * KC] = into[:rows, QC + KC :]
                wo_ref[:, c * half : (c + 1) * half] = out[:rows]


def chip_sum_kernel(n, rows, small_count, owner_ref, keep_ref, got_ref, small_ref, small_got_ref, *outs):
    width = keep_ref.shape[1]
    packed = width // LANES
    sums = outs[-1]
    sums[...] = small_ref[...].astype(bf16).astype(f32) + small_got_ref[...].astype(bf16).astype(f32)
    for k in range(n):
        at = pl.ds(pl.multiple_of(owner_ref[k] * rows, rows), rows)
        outs[k][:rows] = (keep_ref[at, :].astype(f32) + got_ref[at, :].astype(f32)).astype(bf16)
        outs[k][rows:] = jnp.zeros((outs[k].shape[0] - rows, width), bf16)
        for i in range(small_count):
            piece = block_lanes(sums, i, owner_ref[k], rows)
            outs[k][rows + i // packed : rows + i // packed + 1, i % packed * LANES : (i % packed + 1) * LANES] = piece.astype(bf16)


def expert_kernel(size, count, experts, shard_ref, *refs):
    x_refs, up_refs = refs[:count], refs[count : 2 * count]
    chosen_ref, router_ref, wg_ref, wu_ref, wd_ref = refs[2 * count : 2 * count + 5]
    refs = refs[-(2 * count + 6 + 3) :]
    back_refs, mix_refs = refs[:count], refs[count : 2 * count]
    gates_ref, all_x, all_act, all_row, all_gate, all_up = refs[2 * count : 2 * count + 6]
    back_acc, mix_acc, cols_acc = refs[-3:]
    e = pl.program_id(0)
    rows = size * count
    x = jnp.concatenate([ref[...] for ref in x_refs], 0)
    grad = RESIDUAL_SCALE * jnp.concatenate([ref[...] for ref in up_refs], 0).astype(f32)

    @pl.when(e == 0)
    def _():
        chosen = chosen_ref[...] > 0
        logits = jnp.where(chosen, dot_t(x, router_ref[...]), NEG_LARGE)
        raised = jnp.where(chosen, jnp.exp(logits - jnp.max(logits, -1, keepdims=True)), 0.0)
        gates_ref[...] = raised / jnp.sum(raised, -1, keepdims=True)
        all_x[...] = x

    here = lax.broadcasted_iota(jnp.int32, (rows, experts), 1) == shard_ref[0] * EXP_DEV + e
    gate = jnp.sum(jnp.where(here, gates_ref[...], 0.0), -1, keepdims=True)
    gate_pre = dot(x, wg_ref[0])
    up_pre = dot(x, wu_ref[0])
    gate_sig = 1.0 / (1.0 + jnp.exp(-gate_pre))
    silu = gate_pre * gate_sig
    activated = (silu * up_pre).astype(bf16)
    all_act[0] = activated
    expert_out = dot(activated, wd_ref[0]).astype(bf16).astype(f32)
    mix = gate * expert_out
    cols = jnp.where(here, jnp.sum(grad * expert_out, -1, keepdims=True), 0.0)
    row_grad = (gate * grad).astype(bf16)
    all_row[0] = row_grad
    unit = dot_t(row_grad, wd_ref[0])
    gate_grad = (unit * up_pre * gate_sig * (1.0 + gate_pre * (1.0 - gate_sig))).astype(bf16)
    up_grad = (unit * silu).astype(bf16)
    all_gate[0] = gate_grad
    all_up[0] = up_grad
    back = dot_t(gate_grad, wg_ref[0]) + dot_t(up_grad, wu_ref[0])

    @pl.when(e == 0)
    def _():
        back_acc[...] = back
        mix_acc[...] = mix
        cols_acc[...] = cols

    @pl.when(e == EXP_DEV - 1)
    def _():
        whole_back = (back_acc[...] + back).astype(bf16)
        whole_mix = (mix_acc[...] + mix).astype(bf16)
        whole_cols = cols_acc[...] + cols
        high = whole_cols.astype(bf16)
        low = (whole_cols - high.astype(f32)).astype(bf16)
        for k in range(count):
            part = slice(k * size, (k + 1) * size)
            back_refs[k][:, :D] = whole_back[part]
            back_refs[k][:, D:] = jnp.zeros((size, LANES), bf16)
            back_refs[k][:, D : D + experts] = high[part]
            back_refs[k][:, D + experts : D + 2 * experts] = low[part]
            mix_refs[k][...] = whole_mix[part]


def expert_weight_kernel(replicas, place_ref, x_ref, act_ref, row_ref, gate_ref, up_ref, keep_ref, send_ref, wide, tall):
    x = x_ref[...]
    for kind, grads in enumerate((gate_ref, up_ref)):
        tall[...] = t_dot(x, grads[0])
        own = tall.shape[0] // replicas
        for j in range(replicas // 2):
            for target, core in ((keep_ref, place_ref[1]), (send_ref, 1 - place_ref[1])):
                at = pl.ds(pl.multiple_of((2 * j + core) * own, own), own)
                target[kind, j] = tall[at, :].astype(bf16)
    wide[...] = t_dot(act_ref[0], row_ref[0])
    own = wide.shape[0] // replicas
    half = wide.shape[1] // 2
    for j in range(replicas // 2):
        for target, core in ((keep_ref, place_ref[1]), (send_ref, 1 - place_ref[1])):
            at = pl.ds(pl.multiple_of((2 * j + core) * own, own), own)
            target[2, j, :own] = wide[at, :half].astype(bf16)
            target[2, j, own:] = wide[at, half:].astype(bf16)


def expert_weight_grads(replicas, place, held, e):
    group_in, act, row, gate, up = held
    ff = act.shape[2]
    own = D // replicas
    shape = (3, replicas // 2, own, ff)

    def one(width):
        return pl.BlockSpec((1, group_in.shape[0], width), lambda i: (e, 0, 0))

    return pl.pallas_call(
        functools.partial(expert_weight_kernel, replicas),
        grid=(1,),
        in_specs=[
            pl.BlockSpec(memory_space=pltpu.SMEM),
            pl.BlockSpec(group_in.shape, lambda i: (0, 0)),
            one(ff),
            one(D),
            one(ff),
            one(ff),
        ],
        out_specs=[pl.BlockSpec(shape, lambda i: (0, 0, 0, 0))] * 2,
        out_shape=[jax.ShapeDtypeStruct(shape, bf16)] * 2,
        scratch_shapes=[pltpu.VMEM((ff, D), f32), pltpu.VMEM((D, ff), f32)],
        compiler_params=pltpu.CompilerParams(vmem_limit_bytes=60 * 2**20),
        cost_estimate=pl.CostEstimate(flops=2**32, bytes_accessed=2**23, transcendentals=0),
    )(place, group_in, act, row, gate, up)


def replica_split_kernel(place_ref, *refs):
    keeps, gots, outs = refs[:EXP_DEV], refs[EXP_DEV : 2 * EXP_DEV], refs[2 * EXP_DEV :]
    here = place_ref[2] // 2 % 2
    for e in range(EXP_DEV):
        for kind in range(3):
            keep_ref, send_ref = outs[kind], outs[3 + kind]
            for j in range(keep_ref.shape[1]):
                for target, at in ((keep_ref, 2 * j + here), (send_ref, 2 * j + 1 - here)):
                    target[e, j] = (keeps[e][kind, at].astype(f32) + gots[e][kind, at].astype(f32)).astype(bf16)


def run_experts(block, count, total, shard, x, up, chosen, router, w_gate, w_up, w_down, held):
    rows = TOK_DEV * count
    experts = chosen.shape[1]
    ff = w_gate.shape[2]
    at = block // count

    def whole(shape):
        return pl.BlockSpec(shape, lambda e: (0,) * len(shape))

    def one(shape):
        return pl.BlockSpec((1,) + shape, lambda e: (e,) + (0,) * len(shape))

    def filled(width):
        return pl.BlockSpec((1, rows, width), lambda e: (e, at, 0))

    every = TOK_DEV * total
    out_shape = (
        [jax.ShapeDtypeStruct((TOK_DEV, D + LANES), bf16)] * count
        + [jax.ShapeDtypeStruct((TOK_DEV, D), bf16)] * count
        + [jax.ShapeDtypeStruct((rows, experts), f32)]
    )
    held_shape = [
        jax.ShapeDtypeStruct((every, D), bf16),
        jax.ShapeDtypeStruct((EXP_DEV, every, ff), bf16),
        jax.ShapeDtypeStruct((EXP_DEV, every, D), bf16),
        jax.ShapeDtypeStruct((EXP_DEV, every, ff), bf16),
        jax.ShapeDtypeStruct((EXP_DEV, every, ff), bf16),
    ]
    out_specs = (
        [whole((TOK_DEV, D + LANES))] * count
        + [whole((TOK_DEV, D))] * count
        + [whole((rows, experts))]
        + [pl.BlockSpec((rows, D), lambda e: (at, 0))]
        + [filled(ff), filled(D), filled(ff), filled(ff)]
    )
    in_specs = [
        pl.BlockSpec(memory_space=pltpu.SMEM),
        *[whole((TOK_DEV, D))] * (2 * count),
        pl.BlockSpec((rows, experts), lambda e: (at, 0)),
        whole(router.shape),
        one(w_gate.shape[1:]),
        one(w_up.shape[1:]),
        one(w_down.shape[1:]),
    ]
    args = [shard, *x, *up, chosen, router, w_gate, w_up, w_down]
    aliases = {}
    if held is not None:
        aliases = {len(args) + k: len(out_shape) + k for k in range(len(held))}
        in_specs = in_specs + [pl.BlockSpec(memory_space=pl.ANY)] * len(held)
        args = args + list(held)
    flops = 12 * rows * D * ff * EXP_DEV
    outs = pl.pallas_call(
        functools.partial(expert_kernel, TOK_DEV, count, experts),
        grid=(EXP_DEV,),
        in_specs=in_specs,
        out_specs=out_specs,
        out_shape=out_shape + held_shape,
        scratch_shapes=[
            pltpu.VMEM((rows, D), f32),
            pltpu.VMEM((rows, D), f32),
            pltpu.VMEM((rows, experts), f32),
        ],
        input_output_aliases=aliases,
        compiler_params=pltpu.CompilerParams(vmem_limit_bytes=60 * 2**20),
        cost_estimate=pl.CostEstimate(
            flops=flops, bytes_accessed=6 * D * ff * EXP_DEV + 16 * rows * D, transcendentals=rows * ff * EXP_DEV
        ),
    )(*args)
    return outs[:count], outs[count : 2 * count], outs[2 * count], outs[2 * count + 1 :]


def per_device(
    tokens,
    segment_ids,
    expert_ids,
    attn_gain,
    w_query,
    w_key,
    w_value,
    w_output,
    ffn_gain,
    w_router,
    w_gate,
    w_up,
    w_down,
    out_grad,
):
    shard = lax.axis_index("shard")
    core = lax.axis_index("rep") % 2
    ring = Ring()
    n = ring.n
    experts = EXP_DEV * n
    rows = w_query.shape[0]
    half_width = D // 2

    replicas = lax.axis_size("rep")
    place = jnp.stack([shard, core, lax.axis_index("rep")]).astype(jnp.int32)
    owners = ring.row
    cos, sin = rotary_tables()
    shift_up = [(i, i + 1) for i in range(n - 1)]
    shift_down = [(i + 1, i) for i in range(n - 1)]

    in_own, out_own, out_own_other = call(
        split_kernel,
        [vmem((rows + SMALL_ROWS, D), bf16)] + [vmem((rows, half_width), bf16)] * 2,
        [place],
        [jnp.stack([attn_gain, ffn_gain]), w_router.T, expert_ids[0].T, w_query, w_key, w_value, w_output],
    )
    in_ring = Gather(ring, in_own)
    in_ring.step()
    seg_row = jnp.pad(segment_ids.astype(bf16), ((0, SEG_ROWS - 1), (0, D - TOK_DEV)))
    before = jnp.concatenate([tokens[0, HALF:], seg_row], axis=0)
    before = lax.ppermute(after(before, in_ring.got[-1]), "shard", shift_up)
    packet = jnp.concatenate([tokens[0], before, seg_row], axis=0)
    in_ring.step()
    packet_other = swap(after(packet, in_ring.got[-2]), 1)
    while in_ring.left:
        in_ring.step()
    out_ring = Gather(ring, after(out_own, *in_ring.blocks()))
    out_other = {0: out_own_other}
    for o in out_ring.step():
        out_other[o] = swap(out_ring.got[o], 1)

    in_w, small, first_gain, normed, inv_first, queries, keys, values, log_total, att_own, att_send = call(
        functools.partial(attention_kernel, n, rows),
        [
            vmem((D, D), bf16),
            vmem((n, SMALL_ROWS, D), bf16),
            vmem((1, D), f32),
            vmem((2 * TOK_DEV, D), bf16),
            vmem((2 * TOK_DEV, 1), f32),
            vmem((2 * TOK_DEV, QC), bf16),
            vmem((4 * TOK_DEV, KC), bf16),
            vmem((4 * TOK_DEV, KC), bf16),
            vmem((2 * TOK_DEV, LANES), f32),
            vmem((TOK_DEV, QC), bf16),
            vmem((TOK_DEV, QC), bf16),
        ],
        [place, owners],
        [packet, packet_other, cos, sin],
        [pltpu.VMEM((4 * TOK_DEV, D), bf16), pltpu.SemaphoreType.DMA((2 * n,))],
        flops=2**32,
        anywhere=in_ring.blocks(),
    )
    out_ring.got, att_send = together(out_ring.got, att_send)
    att_got = swap(att_send, 1)
    while out_ring.left:
        for o in out_ring.step():
            out_other[o] = swap(out_ring.got[o], 1)
    out_w, out_w_other, second_gain, router, group_chosen, hidden, inv_second, ffn_inputs, attended = call(
        functools.partial(output_kernel, n, rows, experts),
        [
            vmem((QW, half_width), bf16),
            vmem((QW, half_width), bf16),
            vmem((1, D), f32),
            vmem((experts, D), bf16),
            vmem((n * TOK_DEV, experts), f32),
            vmem((TOK_DEV, D), f32),
            vmem((TOK_DEV, 1), f32),
            vmem((TOK_DEV, D), bf16),
            vmem((TOK_DEV, QW), bf16),
        ],
        [place, owners],
        [att_own, att_got, tokens[0], small],
        [pltpu.VMEM((experts, D), f32), pltpu.SemaphoreType.DMA((2 * n,))],
        flops=2**31,
        anywhere=[*out_ring.blocks(), *[out_other[o] for o in ring.offsets]],
    )

    group = Gather(ring, ffn_inputs)
    up = Gather(ring, after(out_grad[0], *out_ring.blocks()))
    while group.left:
        up.step()
        group.step()
    held = None
    back_parts = [None] * n
    own_gates = None
    mix_parts = [None] * n
    runs = [(0, 1)] + [(k, 2) for k in range(2, n, 2)] + [(1, 1)]
    for block, count in runs:
        part = slice(block, block + count)
        backs, mixes, gates, held = run_experts(
            block,
            count,
            n,
            place[:1],
            [group.got[o] for o in ring.offsets[part]],
            [up.got[o] for o in ring.offsets[part]],
            group_chosen,
            router,
            w_gate,
            w_up,
            w_down,
            held,
        )
        back_parts[part] = backs
        mix_parts[part] = mixes
        own_gates = gates if block == 0 else own_gates

    back = Scatter(ring, back_parts)
    keeps, gots = [], []
    while back.left:
        back.step()
        if len(keeps) < EXP_DEV:
            held = after(held, back.got)
            keep, send = expert_weight_grads(replicas, place, held, len(keeps))
            keeps.append(keep)
            gots.append(swap(send, 1))
    own_gates, keeps = together(own_gates, keeps)
    mix = Scatter(ring, after(mix_parts, *back.terms()))
    mix.step()

    ag_own, ag_send, out_send, out_keep, out_small = call(
        functools.partial(hidden_grad_kernel, experts),
        [
            vmem((TOK_DEV, QC), bf16),
            vmem((TOK_DEV, QC), bf16),
            vmem((QW, half_width), bf16),
            vmem((QW, half_width), bf16),
            vmem((experts + 1, D), f32),
        ],
        [place],
        [
            *back.terms(),
            own_gates,
            ffn_inputs,
            hidden,
            inv_second,
            second_gain,
            router,
            out_grad[0],
            attended,
            out_w,
            out_w_other,
        ],
        flops=2**31,
    )
    ag_got = swap(ag_send, 1)
    out_send, out_small = after((out_send, out_small), ag_got)
    out_got, small_got = swap(out_send, 1), swap(out_small, 1)
    split = call(
        replica_split_kernel,
        [vmem((EXP_DEV, replicas // 4, *keeps[0].shape[2:]), bf16)] * 6,
        [place],
        [*keeps, *gots],
    )
    split, ag_got = together(split, ag_got)
    crossed = [swap(part, 2) for part in split[3:]]
    q_pre, kv_own, kv_before = call(
        attention_grad_kernel,
        [
            vmem((2 * TOK_DEV, QC), bf16),
            vmem((2 * TOK_DEV, 2 * KC), f32),
            vmem((TOK_DEV, 2 * KC), bf16),
        ],
        [place],
        [packet, packet_other, queries, keys, values, log_total, att_own, att_send, ag_own, ag_got, cos, sin],
        flops=2**32,
    )
    later = lax.ppermute(kv_before, "shard", shift_down)
    out_small = after(out_small, kv_before)
    extra = -(-(experts + 1) // (8 * (half_width // LANES))) * 8
    out_blocks = call(
        functools.partial(chip_sum_kernel, n, rows, experts + 1),
        [vmem((rows + extra, half_width), bf16)] * n,
        [owners],
        [out_keep, out_got, out_small, small_got],
        [pltpu.VMEM((experts + 1, D), f32)],
        flops=2**29,
    )
    out = Scatter(ring, out_blocks)
    out.step()
    later = after(later, *out_blocks)
    *in_blocks, aig_own, aig_send = call(
        functools.partial(projection_grad_kernel, n, rows),
        [vmem((rows + 8, D), bf16)] * n + [vmem((TOK_DEV, D), f32)] * 2,
        [owners],
        [q_pre, kv_own, later, normed, in_w, packet, packet_other, inv_first],
        [pltpu.VMEM((D, D), f32), pltpu.VMEM((1, D), f32)],
        flops=2**32,
    )
    into = Scatter(ring, in_blocks)
    into.step()
    out.step()
    aig_got = swap(after(aig_send, out.got), 1)
    input_grad = call(
        input_grad_kernel,
        [vmem((TOK_DEV, D), bf16)],
        [],
        [aig_own, aig_got, packet, inv_first, first_gain, out_grad[0]],
    )[0]
    while out.left:
        out.step()
    while into.left:
        into.step()
    mix.sums = after(mix.sums, into.got)
    while mix.left:
        mix.step()
    moe_sum = sum(term.astype(f32) for term in mix.terms())

    def owned(sums):
        own, ahead, behind = sums.terms()
        return rep_sum(own.astype(f32) + ahead.astype(f32) + behind.astype(f32))

    in_sum, out_sum = owned(into), owned(out)
    in_got, out_got = swap(in_sum, 1), swap(out_sum, 1)
    g_query, g_key, g_value, g_output = call(
        assemble_kernel,
        [vmem((rows, QW), f32), vmem((rows, KW), f32), vmem((rows, KW), f32), vmem((rows, D), f32)],
        [place],
        [in_sum, in_got, out_sum, out_got],
    )
    mixed = (hidden + RESIDUAL_SCALE * moe_sum).astype(bf16)

    expert_sums = []
    for keep, got in zip(split[:3], crossed):
        value = keep.astype(f32) + got.astype(f32)
        left = replicas // 4
        for bit in list(bits())[2:]:
            left //= 2
            pairs = value.astype(bf16).reshape(EXP_DEV, left, 2, *value.shape[2:])
            here = (lax.axis_index("rep") // bit) % 2
            stay = lax.dynamic_index_in_dim(pairs, here, 2, False)
            send = lax.dynamic_index_in_dim(pairs, 1 - here, 2, False)
            value = stay.astype(f32) + swap(send, bit).astype(f32)
        expert_sums.append(value[:, 0])
    gate_sum, up_sum, down_sum = expert_sums
    own_ff = down_sum.shape[1] // 2
    down_sum = jnp.concatenate([down_sum[:, :own_ff], down_sum[:, own_ff:]], axis=2)

    out_extra = out_sum[rows:].reshape(-1, LANES)[: experts + 1, :rows]
    return (
        mixed[None],
        input_grad[None],
        in_sum[rows, :rows] + in_got[rows, :rows],
        g_query,
        g_key,
        g_value,
        g_output,
        out_extra[experts],
        out_extra[:experts].T,
        gate_sum,
        up_sum,
        down_sum,
    )


def solution(mesh):
    return jax.shard_map(
        per_device,
        mesh=mesh,
        in_specs=(
            P("rep", "shard", None),
            P("rep", "shard"),
            P("rep", "shard", None),
            P("shard"),
            P("shard", None),
            P("shard", None),
            P("shard", None),
            P("shard", None),
            P("shard"),
            P("shard", None),
            P("shard", None, None),
            P("shard", None, None),
            P("shard", None, None),
            P("rep", "shard", None),
        ),
        out_specs=(
            P("rep", "shard", None),
            P("rep", "shard", None),
            P("shard"),
            P("shard", None),
            P("shard", None),
            P("shard", None),
            P("shard", None),
            P("shard"),
            P("shard", None),
            P("shard", "rep", None),
            P("shard", "rep", None),
            P("shard", "rep", None),
        ),
        check_vma=False,
    )
```

```python
import functools

import jax
import jax.numpy as jnp
import numpy as np
from jax import lax
from jax.experimental import pallas as pl
from jax.experimental.pallas import tpu as pltpu
from jax.sharding import PartitionSpec as P

D = 1024
HEADS = 16
KV_HEADS = 8
HEAD_DIM = 64
GROUP = HEADS // KV_HEADS
QW = HEADS * HEAD_DIM
KW = KV_HEADS * HEAD_DIM
QC = QW // 2
KC = KW // 2
TOK_DEV = 128
HALF = TOK_DEV // 2
HALO = TOK_DEV + HALF
SEG_ROWS = 16
EXP_DEV = 2
LANES = 128

EPSILON = 1e-06
RESIDUAL_SCALE = 0.22
SCORE_SCALE = 0.015625
ROPE_BASE = 10000.0
NEG_LARGE = -1e30

bf16 = jnp.bfloat16
f32 = jnp.float32


def dot(a, b, contract=((1,), (0,))):
    return lax.dot_general(a, b, (contract, ((), ())), preferred_element_type=f32)


def dot_t(a, b):
    return dot(a, b, ((1,), (1,)))


def t_dot(a, b):
    return dot(a, b, ((0,), (0,)))


def cycle(length):
    rows = 4 if length % 4 == 0 else 1
    cols = length // rows
    if cols == 1:
        return list(range(length))
    order = [z * cols for z in range(rows)]
    for k, z in enumerate(reversed(range(rows))):
        ys = list(range(1, cols))
        order += [z * cols + y for y in (ys if k % 2 == 0 else reversed(ys))]
    return order


class Ring:
    def __init__(self):
        n = self.n = lax.axis_size("shard")
        cyc = self.cyc = cycle(n)
        self.next = [(cyc[i], cyc[(i + 1) % n]) for i in range(n)]
        self.prev = [(b, a) for a, b in self.next]
        self.ahead, self.back = n // 2, (n - 1) // 2
        self.offsets = [0, -self.ahead]
        for s in range(1, self.back + 1):
            self.offsets += [-s, s]
        place = {dev: i for i, dev in enumerate(cyc)}
        table = [[cyc[(place[dev] + o) % n] for o in self.offsets] for dev in range(n)]
        row = lax.dynamic_index_in_dim(jnp.asarray(table, jnp.int32), lax.axis_index("shard"), 0, False)
        self.row = row


class Gather:
    def __init__(self, ring, block):
        self.ring, self.got, self.done = ring, {0: block}, 0

    @property
    def left(self):
        return self.ring.ahead - self.done

    def step(self):
        s = self.done = self.done + 1
        new = [-s]
        self.got[-s] = lax.ppermute(self.got[1 - s], "shard", self.ring.next)
        if s <= self.ring.back:
            new.append(s)
            self.got[s] = lax.ppermute(self.got[s - 1], "shard", self.ring.prev)
        return new

    def blocks(self):
        return [self.got[o] for o in self.ring.offsets]


class Scatter:
    def __init__(self, ring, parts):
        self.part = dict(zip(ring.offsets, parts))
        self.ways = ((-1, ring.ahead, ring.prev), (1, ring.back, ring.next))
        self.sums = {sign: self.part[sign * steps] for sign, steps, _ in self.ways}
        self.left = ring.ahead
        self.got = {}

    def step(self):
        for sign, got in self.got.items():
            part = self.part[sign * self.left].astype(f32)
            self.sums[sign] = (got.astype(f32) + part).astype(bf16)
        self.got = {
            sign: lax.ppermute(self.sums[sign], "shard", pairs)
            for sign, steps, pairs in self.ways
            if self.left <= steps
        }
        self.left -= 1

    def terms(self):
        return self.part[0], self.got[-1], self.got[1]


def after(value, *earlier):
    return lax.optimization_barrier((value, *earlier))[0] if earlier else value


def together(*values):
    return lax.optimization_barrier(values)


def swap(value, bit):
    size = lax.axis_size("rep")
    return lax.ppermute(value, "rep", [(r, r ^ bit) for r in range(size)])


def bits():
    size, bit = lax.axis_size("rep"), 1
    while bit < size:
        yield bit
        bit *= 2


def rep_sum(value):
    for bit in list(bits())[1:]:
        low = lax.reduce_precision(value, 8, 7)
        value = low + swap(low.astype(bf16), bit).astype(f32)
    return value


def rotary_tables():
    positions = (np.arange(2 * TOK_DEV) + HALF) % TOK_DEV
    inverse = ROPE_BASE ** (-2.0 * np.arange(HEAD_DIM // 2) / HEAD_DIM)
    angles = positions[:, None] * inverse[None, :]
    cos, sin = np.cos(angles), np.sin(angles)
    cos, sin = np.concatenate([cos] * 4, axis=1), np.concatenate([-sin, sin] * 2, axis=1)
    return jnp.asarray(cos, f32), jnp.asarray(sin, f32)


def lane_index(shape):
    return lax.broadcasted_iota(jnp.int32, shape, 1)


def rotate(values, cos, sin):
    first = lane_index(values.shape) % HEAD_DIM < HEAD_DIM // 2
    turned = jnp.where(first, pltpu.roll(values, LANES - 32, 1), pltpu.roll(values, 32, 1))
    return values * cos + turned * sin


def rotate_back(values, cos, sin):
    first = lane_index(values.shape) % HEAD_DIM < HEAD_DIM // 2
    moved = values * sin
    turned = jnp.where(first, pltpu.roll(moved, LANES - 32, 1), pltpu.roll(moved, 32, 1))
    return values * cos + turned


def apart(pair):
    pair = pair.astype(f32)
    turned = pltpu.roll(pair, HEAD_DIM, 1)
    low = lane_index(pair.shape) < HEAD_DIM
    zero = jnp.zeros_like(pair)
    return (
        (jnp.where(low, pair, zero).astype(bf16), jnp.where(low, zero, turned).astype(bf16)),
        (jnp.where(low, turned, zero).astype(bf16), jnp.where(low, zero, pair).astype(bf16)),
    )


def allowed_pairs(shard_index, packet_ref):
    seg_before = packet_ref[HALO : HALO + 1, :LANES].astype(f32)
    seg_own = packet_ref[HALO + SEG_ROWS : HALO + SEG_ROWS + 1, :LANES].astype(f32)
    seg_key = jnp.concatenate([seg_before, seg_own], 1)
    seg_query = jnp.broadcast_to(seg_own, (TOK_DEV, TOK_DEV)).T[:, :1]
    shape = (TOK_DEV, 2 * TOK_DEV)
    query = lax.broadcasted_iota(jnp.int32, shape, 0)
    key = lax.broadcasted_iota(jnp.int32, shape, 1) - TOK_DEV
    allowed = (key <= query) & (key >= -HALF) & ((query >= HALF) == (key >= HALF))
    return allowed & ((key >= 0) | (shard_index > 0)) & (seg_query == seg_key)


def inverse_rms(values):
    return lax.rsqrt(jnp.mean(values * values, axis=-1, keepdims=True) + EPSILON)


def vmem(shape, dtype):
    return jax.ShapeDtypeStruct(shape, dtype)


def call(kernel, out_shape, scalars, arrays, scratch=(), flops=0, limit=20, anywhere=(), out_space=None):
    return pl.pallas_call(
        kernel,
        in_specs=[pl.BlockSpec(memory_space=pltpu.SMEM)] * len(scalars)
        + [pl.BlockSpec()] * len(arrays)
        + [pl.BlockSpec(memory_space=pl.ANY)] * len(anywhere),
        out_specs=[pl.BlockSpec(memory_space=out_space) if out_space else pl.BlockSpec()] * len(out_shape),
        out_shape=out_shape,
        scratch_shapes=list(scratch),
        compiler_params=pltpu.CompilerParams(vmem_limit_bytes=limit * 2**20),
        cost_estimate=pl.CostEstimate(flops=flops, bytes_accessed=2**22, transcendentals=0),
    )(*scalars, *arrays, *anywhere)


SMALL_ROWS = 16


def split_kernel(place_ref, gains_ref, router_ref, ids_ref, wq_ref, wk_ref, wv_ref, wo_ref, mine, out_mine):
    half = D // 2
    experts, rows = router_ref.shape
    ids = ids_ref[...]
    expert = lax.broadcasted_iota(jnp.int32, (experts, TOK_DEV), 0)
    chosen = jnp.zeros((experts, TOK_DEV), f32)
    for k in range(ids.shape[0]):
        chosen = jnp.where(expert == ids[k : k + 1], 1.0, chosen)
    mine[rows:] = jnp.zeros((SMALL_ROWS, D), bf16)
    mine[rows : rows + 1, :rows] = gains_ref[:1]
    mine[rows + 1 : rows + 2, :rows] = gains_ref[1:]
    for t in range(experts // SMALL_ROWS):
        part = slice(t * SMALL_ROWS, (t + 1) * SMALL_ROWS)
        at = (1 + t) * LANES
        mine[rows:, at : at + rows] = router_ref[part]
        at = (1 + t + experts // SMALL_ROWS) * LANES
        mine[rows:, at : at + LANES] = chosen[part].astype(bf16)
    for core in range(2):

        @pl.when(place_ref[1] == core)
        def _(core=core):
            mine[:rows, :QC] = wq_ref[:, core * QC : (core + 1) * QC]
            mine[:rows, QC : QC + KC] = wk_ref[:, core * KC : (core + 1) * KC]
            mine[:rows, QC + KC :] = wv_ref[:, core * KC : (core + 1) * KC]
            out_mine[...] = wo_ref[:, core * half : (core + 1) * half]


def put_lanes(ref, piece, owner, rows):
    start = owner * rows
    at = pl.ds(pl.multiple_of(start // LANES * LANES, LANES), LANES)
    if rows < LANES:
        off = start % LANES
        lane = lane_index(piece.shape)
        piece = pltpu.roll(piece, off, 1)
        piece = jnp.where((lane >= off) & (lane < off + rows), piece, ref[:, at])
    ref[:, at] = piece


def fetch(n, rows, owner_ref, pairs, sems, small=None):
    copies = []
    for blocks, target in pairs:
        for k in range(n):
            at = pl.ds(pl.multiple_of(owner_ref[k] * rows, rows), rows)
            copies.append(pltpu.make_async_copy(blocks[k].at[pl.ds(0, rows)], target.at[at], sems.at[len(copies)]))
    for k in range(n if small is not None else 0):
        source = pairs[0][0][k].at[pl.ds(rows, SMALL_ROWS)]
        copies.append(pltpu.make_async_copy(source, small.at[k], sems.at[len(copies)]))
    for copy in copies:
        copy.start()
    return copies


def attention_kernel(n, rows, place_ref, owner_ref, own_ref, other_ref, cos_ref, sin_ref, *refs):
    blocks = refs[:n]
    w_ref, small_ref, gain_ref, normed_ref, inv_ref, q_ref, k_ref, v_ref, lse_ref, att_ref, window, sems = refs[n:]
    copies = fetch(n, rows, owner_ref, ((blocks, w_ref),), sems, small_ref)
    packets = (own_ref, other_ref)
    scaled = []
    for g, packet in enumerate(packets):
        values = packet[:HALO].astype(f32)
        inv = inverse_rms(values)
        inv_ref[g * TOK_DEV : (g + 1) * TOK_DEV] = inv[:TOK_DEV]
        scaled.append(values * inv)
    for k in range(n):
        copies[n + k].wait()
    for k in range(n):
        put_lanes(gain_ref, small_ref[k, :1, :LANES].astype(f32), owner_ref[k], rows)
    gain = gain_ref[...]
    for g in range(2):
        base = 2 * TOK_DEV * g
        normed = (scaled[g] * gain).astype(bf16)
        window[base : base + HALF] = jnp.zeros((HALF, D), bf16)
        window[base + HALF : base + TOK_DEV] = normed[TOK_DEV:]
        window[base + TOK_DEV : base + 2 * TOK_DEV] = normed[:TOK_DEV]
        normed_ref[g * TOK_DEV : (g + 1) * TOK_DEV] = normed[:TOK_DEV]
    for copy in copies[:n]:
        copy.wait()
    q_both = dot(normed_ref[...], w_ref[:, :QC])
    kv_both = dot(window[...], w_ref[:, QC:])
    cos, sin = cos_ref[...], sin_ref[...]
    lane = lane_index((TOK_DEV, LANES))
    for g in range(2):
        tok = slice(g * TOK_DEV, (g + 1) * TOK_DEV)
        win = slice(2 * g * TOK_DEV, 2 * (g + 1) * TOK_DEV)
        q_lin, kv_lin = q_both[tok], kv_both[win]
        allowed = allowed_pairs(place_ref[0], packets[g])
        v_ref[win] = kv_lin[:, KC:].astype(bf16)
        lse = jnp.zeros((TOK_DEV, LANES), f32)
        for pair in range(KC // LANES):
            cols = slice(pair * LANES, (pair + 1) * LANES)
            keys = rotate(kv_lin[:, cols], cos, sin)
            k_ref[win, cols] = keys.astype(bf16)
            key_sides = apart(keys)
            value_sides = apart(kv_lin[:, KC + pair * LANES : KC + (pair + 1) * LANES])
            for one in range(2):
                head = 2 * pair + one
                q_cols = slice(head * LANES, (head + 1) * LANES)
                queries = rotate(q_lin[:, q_cols], cos[TOK_DEV:], sin[TOK_DEV:]).astype(bf16)
                q_ref[tok, q_cols] = queries
                out = 0.0
                for side in range(2):
                    scores = dot_t(queries, key_sides[one][side]) * SCORE_SCALE
                    scores = jnp.where(allowed, scores, NEG_LARGE)
                    highest = jnp.max(scores, -1, keepdims=True)
                    raised = jnp.exp(scores - highest)
                    log_total = highest + jnp.log(jnp.sum(raised, -1, keepdims=True))
                    lse = jnp.where(lane == 2 * head + side, log_total, lse)
                    probs = jnp.exp(scores - log_total).astype(bf16)
                    out = out + dot(probs, value_sides[one][side])
                att_ref[tok, q_cols] = out.astype(bf16)
        lse_ref[tok] = lse


def both_halves(place_ref, mine, got):
    first_core = place_ref[1] == 0
    mine, got = mine.astype(f32), got.astype(f32)
    return jnp.concatenate([jnp.where(first_core, mine, got), jnp.where(first_core, got, mine)], 1)


def output_kernel(n, rows, place_ref, owner_ref, att_ref, got_ref, *refs):
    blocks, (w_ref, both_ref, own_ref, send_ref, sems) = refs[:n], refs[n:]
    copies = fetch(n, rows, owner_ref, ((blocks, w_ref),), sems)
    own, other = slice(0, TOK_DEV), slice(TOK_DEV, 2 * TOK_DEV)
    both_ref[own] = both_halves(place_ref, att_ref[own], got_ref[other]).astype(bf16)
    both_ref[other] = both_halves(place_ref, att_ref[other], got_ref[own]).astype(bf16)
    for copy in copies:
        copy.wait()
    proj = dot(both_ref[...], w_ref[...])
    own_ref[...] = proj[own]
    send_ref[...] = proj[other]


def hidden_kernel(n, rows, experts, place_ref, owner_ref, own_ref, got_ref, tok_ref, small_ref, gain_ref, router_ref, chosen_ref, hidden_ref, inv_ref, ffn_ref, router):
    for k in range(n):
        tiles = [small_ref[k, :, i * LANES : (i + 1) * LANES].astype(f32) for i in range(1 + 2 * experts // SMALL_ROWS)]
        put_lanes(gain_ref, tiles[0][1:2], owner_ref[k], rows)
        put_lanes(router, jnp.concatenate(tiles[1 : 1 + experts // SMALL_ROWS], 0), owner_ref[k], rows)
        chosen = jnp.concatenate(tiles[1 + experts // SMALL_ROWS :], 0)
        chosen = jnp.concatenate([chosen, jnp.zeros((LANES - experts, LANES), f32)], 0).T
        chosen_ref[k * TOK_DEV : (k + 1) * TOK_DEV] = chosen[:, :experts]
    router_ref[...] = router[...].astype(bf16)
    hidden = tok_ref[...].astype(f32) + RESIDUAL_SCALE * both_halves(place_ref, own_ref[...], got_ref[...])
    hidden_ref[...] = hidden
    inv = inverse_rms(hidden)
    inv_ref[...] = inv
    ffn_ref[...] = (hidden * inv * gain_ref[...]).astype(bf16)


def block_lanes(ref, row, owner, rows):
    start = owner * rows
    piece = ref[row : row + 1, pl.ds(pl.multiple_of(start // LANES * LANES, LANES), LANES)]
    if rows < LANES:
        piece = pltpu.roll(piece, (LANES - start % LANES) % LANES, 1)
    return piece


def hidden_grad_kernel(experts, back0_ref, back1_ref, back2_ref, gates_ref, ffn_ref, hidden_ref, inv_ref, gain_ref, router_ref, up_ref, branch_ref, small_ref):
    back = back0_ref[...].astype(f32) + back1_ref[...].astype(f32) + back2_ref[...].astype(f32)
    gate_grad = back[:, D : D + experts] + back[:, D + experts : D + 2 * experts]
    gates = gates_ref[...]
    logit_grad = (gates * (gate_grad - jnp.sum(gates * gate_grad, -1, keepdims=True))).astype(bf16)
    hidden, inv, gain = hidden_ref[...], inv_ref[...], gain_ref[...]
    grad = back[:, :D] + dot(logit_grad, router_ref[...])
    scaled = grad * gain
    through = inv * scaled - hidden * (inv * inv * inv) * jnp.mean(scaled * hidden, -1, keepdims=True)
    hidden_grad = up_ref[...].astype(f32) + through
    branch_ref[...] = (RESIDUAL_SCALE * hidden_grad).astype(bf16)
    small_ref[:experts] = t_dot(logit_grad, ffn_ref[...])
    small_ref[experts : experts + 1] = jnp.sum(grad * hidden * inv, 0, keepdims=True)


def output_grad_kernel(place_ref, own_ref, got_ref, w_ref, keep_ref, send_ref, cols_ref):
    half = D // 2
    first_core = place_ref[1] == 0
    both = jnp.concatenate([own_ref[...], got_ref[...]], 0).astype(f32)
    cols = jnp.where(first_core, both[:, :half], both[:, half:]).astype(bf16)
    cols_ref[...] = cols
    grad = dot_t(cols, w_ref[...])
    keep_ref[...] = jnp.where(first_core, grad[:, :QC], grad[:, QC:])
    send_ref[...] = jnp.where(first_core, grad[:, QC:], grad[:, :QC]).astype(bf16)


def output_weight_grad_kernel(n, rows, small_count, owner_ref, both_ref, cols_ref, small_ref, *refs):
    blocks, grads = refs[:n], refs[n]
    grads[...] = t_dot(both_ref[...], cols_ref[...])
    packed = grads.shape[1] // LANES
    for k in range(n):
        at = pl.ds(pl.multiple_of(owner_ref[k] * rows, rows), rows)
        blocks[k][:rows] = grads[at, :].astype(bf16)
        blocks[k][rows:] = jnp.zeros((blocks[k].shape[0] - rows, grads.shape[1]), bf16)
        for i in range(small_count):
            piece = block_lanes(small_ref, i, owner_ref[k], rows)
            lane = i % packed * LANES
            blocks[k][rows + i // packed : rows + i // packed + 1, lane : lane + LANES] = piece.astype(bf16)


def attention_grad_kernel(place_ref, own_ref, other_ref, q_ref, k_ref, v_ref, lse_ref, att_ref, ag_ref, ag_got_ref, cos_ref, sin_ref, q_pre_ref, kv_own_ref, kv_before_ref):
    cos, sin = cos_ref[...], sin_ref[...]
    low = lane_index((TOK_DEV, LANES)) < HEAD_DIM
    for g, packet_ref in enumerate((own_ref, other_ref)):
        tok = slice(g * TOK_DEV, (g + 1) * TOK_DEV)
        there = slice((1 - g) * TOK_DEV, (2 - g) * TOK_DEV)
        win = slice(2 * g * TOK_DEV, 2 * (g + 1) * TOK_DEV)
        halo = slice(g * HALF, (g + 1) * HALF)
        allowed = allowed_pairs(place_ref[0], packet_ref)
        for pair in range(KC // LANES):
            cols = slice(pair * LANES, (pair + 1) * LANES)
            key_sides, value_sides = apart(k_ref[win, cols]), apart(v_ref[win, cols])
            key_grad = jnp.zeros((2 * TOK_DEV, LANES), f32)
            value_grad = jnp.zeros((2 * TOK_DEV, LANES), f32)
            for one in range(2):
                head = 2 * pair + one
                q_cols = slice(head * LANES, (head + 1) * LANES)
                queries = q_ref[tok, q_cols]
                grads = (ag_ref[tok, q_cols] + ag_got_ref[there, q_cols].astype(f32)).astype(bf16)
                query_sides, grad_sides = apart(queries), apart(grads)
                product = grads.astype(f32) * att_ref[tok, q_cols].astype(f32)
                query_grad = jnp.zeros((TOK_DEV, LANES), f32)
                for side in range(2):
                    k_side, v_side = key_sides[one][side], value_sides[one][side]
                    log_total = lse_ref[tok, 2 * head + side : 2 * head + side + 1]
                    delta = jnp.sum(jnp.where(low == (side == 0), product, 0.0), -1, keepdims=True)
                    scores = dot_t(queries, k_side) * SCORE_SCALE
                    probs = jnp.where(allowed, jnp.exp(scores - log_total), 0.0)
                    prob_grad = dot_t(grads, v_side)
                    score_grad = (probs * (prob_grad - delta) * SCORE_SCALE).astype(bf16)
                    query_grad = query_grad + dot(score_grad, k_side)
                    key_grad = key_grad + t_dot(score_grad, query_sides[side][one])
                    value_grad = value_grad + t_dot(probs.astype(bf16), grad_sides[side][one])
                q_pre_ref[tok, q_cols] = rotate_back(query_grad, cos[TOK_DEV:], sin[TOK_DEV:]).astype(bf16)
            v_cols = slice(KC + pair * LANES, KC + (pair + 1) * LANES)
            key_grad = rotate_back(key_grad, cos, sin)
            kv_own_ref[tok, cols] = key_grad[TOK_DEV:]
            kv_own_ref[tok, v_cols] = value_grad[TOK_DEV:]
            kv_before_ref[halo, cols] = key_grad[HALF:TOK_DEV].astype(bf16)
            kv_before_ref[halo, v_cols] = value_grad[HALF:TOK_DEV].astype(bf16)


def projection_grad_kernel(n, rows, owner_ref, q_pre_ref, kv_own_ref, later_ref, normed_ref, w_ref, own_ref, other_ref, inv_ref, *refs):
    blocks, (aig_own_ref, aig_send_ref, grads, gain_grad) = refs[:n], refs[n:]
    kv, later = kv_own_ref[...], later_ref[...].astype(f32)
    parts = []
    for g in range(2):
        at = g * TOK_DEV
        parts += [kv[at : at + HALF], kv[at + HALF : at + TOK_DEV] + later[g * HALF : (g + 1) * HALF]]
    pre = jnp.concatenate([q_pre_ref[...], jnp.concatenate(parts, 0).astype(bf16)], 1)
    grads[...] = t_dot(normed_ref[...], pre)
    aig = dot_t(pre, w_ref[...])
    values = jnp.concatenate([own_ref[:TOK_DEV], other_ref[:TOK_DEV]], 0).astype(f32)
    gain_grad[...] = jnp.sum(aig * values * inv_ref[...], 0, keepdims=True)
    for k in range(n):
        at = pl.ds(pl.multiple_of(owner_ref[k] * rows, rows), rows)
        blocks[k][:rows] = grads[at, :].astype(bf16)
        blocks[k][rows:] = jnp.zeros((blocks[k].shape[0] - rows, D), bf16)
        blocks[k][rows : rows + 1, :LANES] = block_lanes(gain_grad, 0, owner_ref[k], rows).astype(bf16)
    aig_own_ref[...] = aig[:TOK_DEV]
    aig_send_ref[...] = aig[TOK_DEV:]


def input_grad_kernel(aig_ref, got_ref, own_ref, inv_ref, gain_ref, up_ref, out_ref):
    grad = aig_ref[...] + got_ref[...]
    values, inv = own_ref[:TOK_DEV].astype(f32), inv_ref[:TOK_DEV]
    scaled = grad * gain_ref[...]
    through = inv * scaled - values * (inv * inv * inv) * jnp.mean(scaled * values, -1, keepdims=True)
    out_ref[...] = (up_ref[...].astype(f32) + through).astype(bf16)


def assemble_kernel(place_ref, in_own, in_got, out_own, out_got, wq_ref, wk_ref, wv_ref, wo_ref):
    rows = wq_ref.shape[0]
    half = D // 2
    for core, first, second, low, high in ((0, in_own, in_got, out_own, out_got), (1, in_got, in_own, out_got, out_own)):

        @pl.when(place_ref[1] == core)
        def _(sides=((first, low), (second, high))):
            for c, (into, out) in enumerate(sides):
                wq_ref[:, c * QC : (c + 1) * QC] = into[:rows, :QC]
                wk_ref[:, c * KC : (c + 1) * KC] = into[:rows, QC : QC + KC]
                wv_ref[:, c * KC : (c + 1) * KC] = into[:rows, QC + KC :]
                wo_ref[:, c * half : (c + 1) * half] = out[:rows]


def expert_kernel(size, count, experts, shard_ref, *refs):
    x_refs, up_refs = refs[:count], refs[count : 2 * count]
    chosen_ref, router_ref, wg_ref, wu_ref, wd_ref = refs[2 * count : 2 * count + 5]
    refs = refs[-(2 * count + 6 + 3) :]
    back_refs, mix_refs = refs[:count], refs[count : 2 * count]
    gates_ref, all_x, all_act, all_row, all_gate, all_up = refs[2 * count : 2 * count + 6]
    back_acc, mix_acc, cols_acc = refs[-3:]
    e = pl.program_id(0)
    rows = size * count
    x = jnp.concatenate([ref[...] for ref in x_refs], 0)
    grad = RESIDUAL_SCALE * jnp.concatenate([ref[...] for ref in up_refs], 0).astype(f32)

    @pl.when(e == 0)
    def _():
        chosen = chosen_ref[...] > 0
        logits = jnp.where(chosen, dot_t(x, router_ref[...]), NEG_LARGE)
        raised = jnp.where(chosen, jnp.exp(logits - jnp.max(logits, -1, keepdims=True)), 0.0)
        gates_ref[...] = raised / jnp.sum(raised, -1, keepdims=True)
        all_x[...] = x

    here = lax.broadcasted_iota(jnp.int32, (rows, experts), 1) == shard_ref[0] * EXP_DEV + e
    gate = jnp.sum(jnp.where(here, gates_ref[...], 0.0), -1, keepdims=True)
    gate_pre = dot(x, wg_ref[0])
    up_pre = dot(x, wu_ref[0])
    gate_sig = 1.0 / (1.0 + jnp.exp(-gate_pre))
    silu = gate_pre * gate_sig
    activated = (silu * up_pre).astype(bf16)
    all_act[0] = activated
    expert_out = dot(activated, wd_ref[0]).astype(bf16).astype(f32)
    mix = gate * expert_out
    cols = jnp.where(here, jnp.sum(grad * expert_out, -1, keepdims=True), 0.0)
    row_grad = (gate * grad).astype(bf16)
    all_row[0] = row_grad
    unit = dot_t(row_grad, wd_ref[0])
    gate_grad = (unit * up_pre * gate_sig * (1.0 + gate_pre * (1.0 - gate_sig))).astype(bf16)
    up_grad = (unit * silu).astype(bf16)
    all_gate[0] = gate_grad
    all_up[0] = up_grad
    back = dot_t(gate_grad, wg_ref[0]) + dot_t(up_grad, wu_ref[0])

    @pl.when(e == 0)
    def _():
        back_acc[...] = back
        mix_acc[...] = mix
        cols_acc[...] = cols

    @pl.when(e == EXP_DEV - 1)
    def _():
        whole_back = (back_acc[...] + back).astype(bf16)
        whole_mix = (mix_acc[...] + mix).astype(bf16)
        whole_cols = cols_acc[...] + cols
        high = whole_cols.astype(bf16)
        low = (whole_cols - high.astype(f32)).astype(bf16)
        for k in range(count):
            part = slice(k * size, (k + 1) * size)
            back_refs[k][:, :D] = whole_back[part]
            back_refs[k][:, D:] = jnp.zeros((size, LANES), bf16)
            back_refs[k][:, D : D + experts] = high[part]
            back_refs[k][:, D + experts : D + 2 * experts] = low[part]
            mix_refs[k][...] = whole_mix[part]


def expert_weight_kernel(replicas, place_ref, x_ref, act_ref, row_ref, gate_ref, up_ref, keep_ref, send_ref, wide, tall):
    x = x_ref[...]
    for kind, grads in enumerate((gate_ref, up_ref)):
        tall[...] = t_dot(x, grads[0])
        own = tall.shape[0] // replicas
        for j in range(replicas // 2):
            for target, core in ((keep_ref, place_ref[1]), (send_ref, 1 - place_ref[1])):
                at = pl.ds(pl.multiple_of((2 * j + core) * own, own), own)
                target[kind, j] = tall[at, :].astype(bf16)
    wide[...] = t_dot(act_ref[0], row_ref[0])
    own = wide.shape[0] // replicas
    half = wide.shape[1] // 2
    for j in range(replicas // 2):
        for target, core in ((keep_ref, place_ref[1]), (send_ref, 1 - place_ref[1])):
            at = pl.ds(pl.multiple_of((2 * j + core) * own, own), own)
            target[2, j, :own] = wide[at, :half].astype(bf16)
            target[2, j, own:] = wide[at, half:].astype(bf16)


def expert_weight_grads(replicas, place, held, e):
    group_in, act, row, gate, up = held
    ff = act.shape[2]
    own = D // replicas
    shape = (3, replicas // 2, own, ff)

    def one(width):
        return pl.BlockSpec((1, group_in.shape[0], width), lambda i: (e, 0, 0))

    return pl.pallas_call(
        functools.partial(expert_weight_kernel, replicas),
        grid=(1,),
        in_specs=[
            pl.BlockSpec(memory_space=pltpu.SMEM),
            pl.BlockSpec(group_in.shape, lambda i: (0, 0)),
            one(ff),
            one(D),
            one(ff),
            one(ff),
        ],
        out_specs=[pl.BlockSpec(shape, lambda i: (0, 0, 0, 0))] * 2,
        out_shape=[jax.ShapeDtypeStruct(shape, bf16)] * 2,
        scratch_shapes=[pltpu.VMEM((ff, D), f32), pltpu.VMEM((D, ff), f32)],
        compiler_params=pltpu.CompilerParams(vmem_limit_bytes=32 * 2**20),
        cost_estimate=pl.CostEstimate(flops=2**32, bytes_accessed=2**23, transcendentals=0),
    )(place, group_in, act, row, gate, up)


def expert_sum_kernel(*refs):
    keeps, gots, (gate_ref, up_ref, down_ref) = refs[:EXP_DEV], refs[EXP_DEV : 2 * EXP_DEV], refs[2 * EXP_DEV :]
    own = down_ref.shape[1]
    for e in range(EXP_DEV):
        total = [keeps[e][kind].astype(f32) + gots[e][kind].astype(f32) for kind in range(3)]
        gate_ref[e] = total[0]
        up_ref[e] = total[1]
        down_ref[e, :, : total[2].shape[1]] = total[2][:own]
        down_ref[e, :, total[2].shape[1] :] = total[2][own:]


def replica_split_kernel(place_ref, keep_ref, got_ref, stay_ref, send_ref):
    here = place_ref[2] // 2 % 2
    for kind in range(3):
        for j in range(stay_ref.shape[1]):
            for target, at in ((stay_ref, 2 * j + here), (send_ref, 2 * j + 1 - here)):
                target[kind, j] = (keep_ref[kind, at].astype(f32) + got_ref[kind, at].astype(f32)).astype(bf16)


def run_experts(block, count, total, shard, x, up, chosen, router, w_gate, w_up, w_down, held):
    rows = TOK_DEV * count
    experts = chosen.shape[1]
    ff = w_gate.shape[2]
    at = block // count

    def whole(shape):
        return pl.BlockSpec(shape, lambda e: (0,) * len(shape))

    def one(shape):
        return pl.BlockSpec((1,) + shape, lambda e: (e,) + (0,) * len(shape))

    def filled(width):
        return pl.BlockSpec((1, rows, width), lambda e: (e, at, 0))

    every = TOK_DEV * total
    out_shape = (
        [jax.ShapeDtypeStruct((TOK_DEV, D + LANES), bf16)] * count
        + [jax.ShapeDtypeStruct((TOK_DEV, D), bf16)] * count
        + [jax.ShapeDtypeStruct((rows, experts), f32)]
    )
    held_shape = [
        jax.ShapeDtypeStruct((every, D), bf16),
        jax.ShapeDtypeStruct((EXP_DEV, every, ff), bf16),
        jax.ShapeDtypeStruct((EXP_DEV, every, D), bf16),
        jax.ShapeDtypeStruct((EXP_DEV, every, ff), bf16),
        jax.ShapeDtypeStruct((EXP_DEV, every, ff), bf16),
    ]
    out_specs = (
        [whole((TOK_DEV, D + LANES))] * count
        + [whole((TOK_DEV, D))] * count
        + [whole((rows, experts))]
        + [pl.BlockSpec((rows, D), lambda e: (at, 0))]
        + [filled(ff), filled(D), filled(ff), filled(ff)]
    )
    in_specs = [
        pl.BlockSpec(memory_space=pltpu.SMEM),
        *[whole((TOK_DEV, D))] * (2 * count),
        pl.BlockSpec((rows, experts), lambda e: (at, 0)),
        whole(router.shape),
        one(w_gate.shape[1:]),
        one(w_up.shape[1:]),
        one(w_down.shape[1:]),
    ]
    args = [shard, *x, *up, chosen, router, w_gate, w_up, w_down]
    aliases = {}
    if held is not None:
        aliases = {len(args) + k: len(out_shape) + k for k in range(len(held))}
        in_specs = in_specs + [pl.BlockSpec(memory_space=pl.ANY)] * len(held)
        args = args + list(held)
    flops = 12 * rows * D * ff * EXP_DEV
    outs = pl.pallas_call(
        functools.partial(expert_kernel, TOK_DEV, count, experts),
        grid=(EXP_DEV,),
        in_specs=in_specs,
        out_specs=out_specs,
        out_shape=out_shape + held_shape,
        scratch_shapes=[
            pltpu.VMEM((rows, D), f32),
            pltpu.VMEM((rows, D), f32),
            pltpu.VMEM((rows, experts), f32),
        ],
        input_output_aliases=aliases,
        compiler_params=pltpu.CompilerParams(vmem_limit_bytes=24 * 2**20),
        cost_estimate=pl.CostEstimate(
            flops=flops, bytes_accessed=6 * D * ff * EXP_DEV + 16 * rows * D, transcendentals=rows * ff * EXP_DEV
        ),
    )(*args)
    return outs[:count], outs[count : 2 * count], outs[2 * count], outs[2 * count + 1 :]


def per_device(
    tokens,
    segment_ids,
    expert_ids,
    attn_gain,
    w_query,
    w_key,
    w_value,
    w_output,
    ffn_gain,
    w_router,
    w_gate,
    w_up,
    w_down,
    out_grad,
):
    shard = lax.axis_index("shard")
    core = lax.axis_index("rep") % 2
    ring = Ring()
    n = ring.n
    experts = EXP_DEV * n
    rows = w_query.shape[0]
    half_width = D // 2

    replicas = lax.axis_size("rep")
    place = jnp.stack([shard, core, lax.axis_index("rep")]).astype(jnp.int32)
    owners = ring.row
    cos, sin = rotary_tables()
    shift_up = [(i, i + 1) for i in range(n - 1)]
    shift_down = [(i + 1, i) for i in range(n - 1)]

    in_own, out_own = call(
        split_kernel,
        [vmem((rows + SMALL_ROWS, D), bf16), vmem((rows, half_width), bf16)],
        [place],
        [jnp.stack([attn_gain, ffn_gain]), w_router.T, expert_ids[0].T, w_query, w_key, w_value, w_output],
    )
    in_ring = Gather(ring, in_own)
    in_ring.step()
    seg_row = jnp.pad(segment_ids.astype(bf16), ((0, SEG_ROWS - 1), (0, D - TOK_DEV)))
    before = jnp.concatenate([tokens[0, HALF:], seg_row], axis=0)
    before = lax.ppermute(after(before, in_ring.got[-1]), "shard", shift_up)
    packet = jnp.concatenate([tokens[0], before, seg_row], axis=0)
    in_ring.step()
    packet_other = swap(after(packet, in_ring.got[-2]), 1)
    while in_ring.left:
        in_ring.step()
    out_own, up_own = after((out_own, out_grad[0]), *in_ring.blocks())
    out_ring, up = Gather(ring, out_own), Gather(ring, up_own)
    out_ring.step()
    up.step()
    in_w, small, first_gain, normed, inv_first, queries, keys, values, log_total, att = call(
        functools.partial(attention_kernel, n, rows),
        [
            vmem((D, D), bf16),
            vmem((n, SMALL_ROWS, D), bf16),
            vmem((1, D), f32),
            vmem((2 * TOK_DEV, D), bf16),
            vmem((2 * TOK_DEV, 1), f32),
            vmem((2 * TOK_DEV, QC), bf16),
            vmem((4 * TOK_DEV, KC), bf16),
            vmem((4 * TOK_DEV, KC), bf16),
            vmem((2 * TOK_DEV, LANES), f32),
            vmem((2 * TOK_DEV, QC), bf16),
        ],
        [place, owners],
        [packet, packet_other, cos, sin],
        [pltpu.VMEM((4 * TOK_DEV, D), bf16), pltpu.SemaphoreType.DMA((2 * n,))],
        flops=2**32,
        anywhere=in_ring.blocks(),
    )
    out_ring.got, up.got, att = together(out_ring.got, up.got, att)
    att_got = swap(att, 1)
    out_ring.step()
    up.step()
    while out_ring.left:
        out_ring.step()
    out_blocks, att_got, up.got = together(out_ring.blocks(), att_got, up.got)
    out_w, attended, proj, proj_send = call(
        functools.partial(output_kernel, n, rows),
        [
            vmem((QW, half_width), bf16),
            vmem((2 * TOK_DEV, QW), bf16),
            vmem((TOK_DEV, half_width), f32),
            vmem((TOK_DEV, half_width), f32),
        ],
        [place, owners],
        [att, att_got],
        [pltpu.SemaphoreType.DMA((n,))],
        flops=2**30,
        anywhere=out_blocks,
    )
    second_gain, router, group_chosen, hidden, inv_second, ffn_inputs = call(
        functools.partial(hidden_kernel, n, rows, experts),
        [
            vmem((1, D), f32),
            vmem((experts, D), bf16),
            vmem((n * TOK_DEV, experts), f32),
            vmem((TOK_DEV, D), f32),
            vmem((TOK_DEV, 1), f32),
            vmem((TOK_DEV, D), bf16),
        ],
        [place, owners],
        [proj, swap(proj_send, 1), tokens[0], small],
        [pltpu.VMEM((experts, D), f32)],
        flops=2**28,
    )

    group = Gather(ring, ffn_inputs)
    while group.left:
        group.step()
        if up.left:
            up.step()
    held = None
    back_parts = [None] * n
    own_gates = None
    mix_parts = [None] * n
    runs = [(0, 1)] + [(k, 2) for k in range(2, n, 2)] + [(1, 1)]
    for block, count in runs:
        part = slice(block, block + count)
        backs, mixes, gates, held = run_experts(
            block,
            count,
            n,
            place[:1],
            [group.got[o] for o in ring.offsets[part]],
            [up.got[o] for o in ring.offsets[part]],
            group_chosen,
            router,
            w_gate,
            w_up,
            w_down,
            held,
        )
        back_parts[part] = backs
        mix_parts[part] = mixes
        own_gates = gates if block == 0 else own_gates

    back = Scatter(ring, back_parts)
    stays, crossing = [], []
    while back.left:
        back.step()
        if len(stays) < EXP_DEV:
            held = after(held, back.got)
            keep, send = expert_weight_grads(replicas, place, held, len(stays))
            stay, send = call(
                replica_split_kernel,
                [vmem((3, replicas // 4, *keep.shape[2:]), bf16)] * 2,
                [place],
                [keep, swap(send, 1)],
            )
            stays.append(stay)
            crossing.append(send)
    own_gates, crossing[0] = together(own_gates, crossing[0])
    crossing[0] = swap(crossing[0], 2)

    branch, out_small = call(
        functools.partial(hidden_grad_kernel, experts),
        [vmem((TOK_DEV, D), bf16), vmem((experts + 1, D), f32)],
        [],
        [
            *back.terms(),
            own_gates,
            ffn_inputs,
            hidden,
            inv_second,
            second_gain,
            router,
            out_grad[0],
        ],
        flops=2**28,
    )
    ag_keep, ag_send, branch_cols = call(
        output_grad_kernel,
        [
            vmem((2 * TOK_DEV, QC), f32),
            vmem((2 * TOK_DEV, QC), bf16),
            vmem((2 * TOK_DEV, half_width), bf16),
        ],
        [place],
        [branch, swap(branch, 1), out_w],
        flops=2**29,
    )
    ag_got = swap(ag_send, 1)
    extra = -(-(experts + 1) // (8 * (half_width // LANES))) * 8
    out_blocks = call(
        functools.partial(output_weight_grad_kernel, n, rows, experts + 1),
        [vmem((rows + extra, half_width), bf16)] * n,
        [owners],
        [attended, branch_cols, out_small],
        [pltpu.VMEM((QW, half_width), f32)],
        flops=2**29,
    )
    ag_got, out_blocks = together(ag_got, out_blocks)
    out = Scatter(ring, out_blocks)
    out.step()
    mix = Scatter(ring, after(mix_parts, ag_got))
    q_pre, kv_own, kv_before = call(
        attention_grad_kernel,
        [
            vmem((2 * TOK_DEV, QC), bf16),
            vmem((2 * TOK_DEV, 2 * KC), f32),
            vmem((TOK_DEV, 2 * KC), bf16),
        ],
        [place],
        [packet, packet_other, queries, keys, values, log_total, att, ag_keep, ag_got, cos, sin],
        flops=2**32,
    )
    kv_before, out.got, crossing[0] = together(kv_before, out.got, crossing[0])
    crossing[1] = swap(after(crossing[1], crossing[0]), 2)
    later = lax.ppermute(kv_before, "shard", shift_down)
    out.step()
    mix.step()
    later, out.got = together(later, out.got)
    out.step()
    *in_blocks, aig_own, aig_send = call(
        functools.partial(projection_grad_kernel, n, rows),
        [vmem((rows + 8, D), bf16)] * n + [vmem((TOK_DEV, D), f32)] * 2,
        [owners],
        [q_pre, kv_own, later, normed, in_w, packet, packet_other, inv_first],
        [pltpu.VMEM((D, D), f32), pltpu.VMEM((1, D), f32)],
        flops=2**32,
    )
    in_blocks, out.got, mix.got = together(in_blocks, out.got, mix.got)
    into = Scatter(ring, in_blocks)
    into.step()
    while out.left:
        out.step()
    into.got, out.got = together(into.got, out.got)
    into.step()
    aig_got = swap(after(aig_send, out.got), 1)
    into.got, crossing[1], aig_got = together(into.got, crossing[1], aig_got)
    input_grad = call(
        input_grad_kernel,
        [vmem((TOK_DEV, D), bf16)],
        [],
        [aig_own, aig_got, packet, inv_first, first_gain, out_grad[0]],
    )[0]
    while into.left:
        into.step()
    mix.sums = after(mix.sums, into.got)
    while mix.left:
        mix.step()
    moe_sum = sum(term.astype(f32) for term in mix.terms())

    def owned(sums):
        own, ahead, behind = sums.terms()
        return rep_sum(own.astype(f32) + ahead.astype(f32) + behind.astype(f32))

    in_sum, out_sum = owned(into), owned(out)
    in_got, out_got = swap(in_sum, 1), swap(out_sum, 1)
    g_query, g_key, g_value, g_output = call(
        assemble_kernel,
        [vmem((rows, QW), f32), vmem((rows, KW), f32), vmem((rows, KW), f32), vmem((rows, D), f32)],
        [place],
        [in_sum, in_got, out_sum, out_got],
    )
    mixed = (hidden + RESIDUAL_SCALE * moe_sum).astype(bf16)

    left = replicas // 4
    for bit in list(bits())[2:]:
        left //= 2
        here = (lax.axis_index("rep") // bit) % 2
        for e in range(EXP_DEV):
            total = (stays[e].astype(f32) + crossing[e].astype(f32)).astype(bf16)
            pairs = total.reshape(3, left, 2, *total.shape[2:])
            stays[e] = lax.dynamic_index_in_dim(pairs, here, 2, False)
            crossing[e] = swap(lax.dynamic_index_in_dim(pairs, 1 - here, 2, False), bit)
    ff, own_rows = w_gate.shape[2], D // replicas
    gate_sum, up_sum, down_sum = call(
        expert_sum_kernel,
        [
            vmem((EXP_DEV, own_rows, ff), f32),
            vmem((EXP_DEV, own_rows, ff), f32),
            vmem((EXP_DEV, ff // replicas, D), f32),
        ],
        [],
        [part[:, 0] for part in stays + crossing],
    )

    out_extra = (out_sum[rows:] + out_got[rows:]).reshape(-1, LANES)[: experts + 1, :rows]
    return (
        mixed[None],
        input_grad[None],
        in_sum[rows, :rows] + in_got[rows, :rows],
        g_query,
        g_key,
        g_value,
        g_output,
        out_extra[experts],
        out_extra[:experts].T,
        gate_sum,
        up_sum,
        down_sum,
    )


def solution(mesh):
    return jax.shard_map(
        per_device,
        mesh=mesh,
        in_specs=(
            P("rep", "shard", None),
            P("rep", "shard"),
            P("rep", "shard", None),
            P("shard"),
            P("shard", None),
            P("shard", None),
            P("shard", None),
            P("shard", None),
            P("shard"),
            P("shard", None),
            P("shard", None, None),
            P("shard", None, None),
            P("shard", None, None),
            P("rep", "shard", None),
        ),
        out_specs=(
            P("rep", "shard", None),
            P("rep", "shard", None),
            P("shard"),
            P("shard", None),
            P("shard", None),
            P("shard", None),
            P("shard", None),
            P("shard"),
            P("shard", None),
            P("shard", "rep", None),
            P("shard", "rep", None),
            P("shard", "rep", None),
        ),
        check_vma=False,
    )
```

```python
import functools

import jax
import jax.numpy as jnp
import numpy as np
from jax import lax
from jax.experimental import pallas as pl
from jax.experimental.pallas import tpu as pltpu
from jax.sharding import PartitionSpec as P

D = 1024
HEADS = 16
KV_HEADS = 8
HEAD_DIM = 64
GROUP = HEADS // KV_HEADS
QW = HEADS * HEAD_DIM
KW = KV_HEADS * HEAD_DIM
QC = QW // 2
KC = KW // 2
TOK_DEV = 128
HALF = TOK_DEV // 2
HALO = TOK_DEV + HALF
SEG_ROWS = 16
EXP_DEV = 2
LANES = 128

EPSILON = 1e-06
RESIDUAL_SCALE = 0.22
SCORE_SCALE = 0.015625
ROPE_BASE = 10000.0
NEG_LARGE = -1e30

bf16 = jnp.bfloat16
f32 = jnp.float32


def dot(a, b, contract=((1,), (0,))):
    return lax.dot_general(a, b, (contract, ((), ())), preferred_element_type=f32)


def dot_t(a, b):
    return dot(a, b, ((1,), (1,)))


def t_dot(a, b):
    return dot(a, b, ((0,), (0,)))


def cycle(length):
    rows = 4 if length % 4 == 0 else 1
    cols = length // rows
    if cols == 1:
        return list(range(length))
    order = [z * cols for z in range(rows)]
    for k, z in enumerate(reversed(range(rows))):
        ys = list(range(1, cols))
        order += [z * cols + y for y in (ys if k % 2 == 0 else reversed(ys))]
    return order


class Ring:
    def __init__(self):
        n = self.n = lax.axis_size("shard")
        cyc = self.cyc = cycle(n)
        self.next = [(cyc[i], cyc[(i + 1) % n]) for i in range(n)]
        self.prev = [(b, a) for a, b in self.next]
        self.ahead, self.back = n // 2, (n - 1) // 2
        self.offsets = [0, -self.ahead]
        for s in range(1, self.back + 1):
            self.offsets += [-s, s]
        place = {dev: i for i, dev in enumerate(cyc)}
        table = [[cyc[(place[dev] + o) % n] for o in self.offsets] for dev in range(n)]
        row = lax.dynamic_index_in_dim(jnp.asarray(table, jnp.int32), lax.axis_index("shard"), 0, False)
        self.row = row


class Gather:
    def __init__(self, ring, block, flip=False):
        self.ring, self.got, self.flip = ring, {0: block}, flip
        self.pairs = {-1: ring.next, 1: ring.prev}
        self.steps = {-1: ring.back, 1: ring.ahead} if flip else {-1: ring.ahead, 1: ring.back}
        self.done = {-1: 0, 1: 0}

    @property
    def left(self):
        return max(self.steps[sign] - self.done[sign] for sign in (-1, 1))

    def hop(self, sign):
        s = self.done[sign] = self.done[sign] + 1
        self.got[sign * s] = lax.ppermute(self.got[sign * (s - 1)], "shard", self.pairs[sign])

    def step(self):
        for sign in (-1, 1):
            if self.done[sign] < self.steps[sign]:
                self.hop(sign)

    def blocks(self):
        half = self.ring.ahead
        if self.flip:
            self.got[-half] = self.got[half]
        return [self.got[o] for o in self.ring.offsets]


class Scatter:
    def __init__(self, ring, parts, flip=False):
        self.part = dict(zip(ring.offsets, parts))
        self.pairs = {-1: ring.prev, 1: ring.next}
        self.hops = {-1: ring.back, 1: ring.ahead} if flip else {-1: ring.ahead, 1: ring.back}
        if flip:
            self.part[ring.ahead] = self.part[-ring.ahead]
        self.sums = {sign: self.part[sign * steps] for sign, steps in self.hops.items()}
        self.got = {}

    @property
    def left(self):
        return max(self.hops.values())

    def hop(self, sign):
        if sign in self.got:
            part = self.part[sign * self.hops[sign]].astype(f32)
            self.sums[sign] = (self.got[sign].astype(f32) + part).astype(bf16)
        self.got[sign] = lax.ppermute(self.sums[sign], "shard", self.pairs[sign])
        self.hops[sign] -= 1

    def step(self):
        left = self.left
        for sign in (-1, 1):
            if self.hops[sign] == left:
                self.hop(sign)

    def terms(self):
        return self.part[0], self.got[-1], self.got[1]


def after(value, *earlier):
    return lax.optimization_barrier((value, *earlier))[0] if earlier else value


def together(*values):
    return lax.optimization_barrier(values)


def swap(value, bit):
    size = lax.axis_size("rep")
    return lax.ppermute(value, "rep", [(r, r ^ bit) for r in range(size)])


def bits():
    size, bit = lax.axis_size("rep"), 1
    while bit < size:
        yield bit
        bit *= 2


def rep_sum(value):
    for bit in list(bits())[1:]:
        low = lax.reduce_precision(value, 8, 7)
        value = low + swap(low.astype(bf16), bit).astype(f32)
    return value


def rotary_tables():
    positions = (np.arange(2 * TOK_DEV) + HALF) % TOK_DEV
    inverse = ROPE_BASE ** (-2.0 * np.arange(HEAD_DIM // 2) / HEAD_DIM)
    angles = positions[:, None] * inverse[None, :]
    cos, sin = np.cos(angles), np.sin(angles)
    cos, sin = np.concatenate([cos] * 4, axis=1), np.concatenate([-sin, sin] * 2, axis=1)
    return jnp.asarray(cos, f32), jnp.asarray(sin, f32)


def lane_index(shape):
    return lax.broadcasted_iota(jnp.int32, shape, 1)


def rotate(values, cos, sin):
    first = lane_index(values.shape) % HEAD_DIM < HEAD_DIM // 2
    turned = jnp.where(first, pltpu.roll(values, LANES - 32, 1), pltpu.roll(values, 32, 1))
    return values * cos + turned * sin


def rotate_back(values, cos, sin):
    first = lane_index(values.shape) % HEAD_DIM < HEAD_DIM // 2
    moved = values * sin
    turned = jnp.where(first, pltpu.roll(moved, LANES - 32, 1), pltpu.roll(moved, 32, 1))
    return values * cos + turned


def apart(pair):
    pair = pair.astype(f32)
    turned = pltpu.roll(pair, HEAD_DIM, 1)
    low = lane_index(pair.shape) < HEAD_DIM
    zero = jnp.zeros_like(pair)
    return (
        (jnp.where(low, pair, zero).astype(bf16), jnp.where(low, zero, turned).astype(bf16)),
        (jnp.where(low, turned, zero).astype(bf16), jnp.where(low, zero, pair).astype(bf16)),
    )


def allowed_pairs(shard_index, packet_ref):
    seg_before = packet_ref[HALO : HALO + 1, :LANES].astype(f32)
    seg_own = packet_ref[HALO + SEG_ROWS : HALO + SEG_ROWS + 1, :LANES].astype(f32)
    seg_key = jnp.concatenate([seg_before, seg_own], 1)
    seg_query = jnp.broadcast_to(seg_own, (TOK_DEV, TOK_DEV)).T[:, :1]
    shape = (TOK_DEV, 2 * TOK_DEV)
    query = lax.broadcasted_iota(jnp.int32, shape, 0)
    key = lax.broadcasted_iota(jnp.int32, shape, 1) - TOK_DEV
    allowed = (key <= query) & (key >= -HALF) & ((query >= HALF) == (key >= HALF))
    return allowed & ((key >= 0) | (shard_index > 0)) & (seg_query == seg_key)


def inverse_rms(values):
    return lax.rsqrt(jnp.mean(values * values, axis=-1, keepdims=True) + EPSILON)


def vmem(shape, dtype):
    return jax.ShapeDtypeStruct(shape, dtype)


def call(kernel, out_shape, scalars, arrays, scratch=(), flops=0, limit=20, anywhere=(), out_space=None):
    return pl.pallas_call(
        kernel,
        in_specs=[pl.BlockSpec(memory_space=pltpu.SMEM)] * len(scalars)
        + [pl.BlockSpec()] * len(arrays)
        + [pl.BlockSpec(memory_space=pl.ANY)] * len(anywhere),
        out_specs=[pl.BlockSpec(memory_space=out_space) if out_space else pl.BlockSpec()] * len(out_shape),
        out_shape=out_shape,
        scratch_shapes=list(scratch),
        compiler_params=pltpu.CompilerParams(vmem_limit_bytes=limit * 2**20),
        cost_estimate=pl.CostEstimate(flops=flops, bytes_accessed=2**22, transcendentals=0),
    )(*scalars, *arrays, *anywhere)


SMALL_ROWS = 16


def split_kernel(place_ref, gain_1_ref, gain_2_ref, router_ref, ids_ref, wq_ref, wk_ref, wv_ref, wo_ref, mine, out_mine):
    half = D // 2
    experts, rows = router_ref.shape
    ids = ids_ref[...]
    expert = lax.broadcasted_iota(jnp.int32, (experts, TOK_DEV), 0)
    chosen = jnp.zeros((experts, TOK_DEV), f32)
    for k in range(ids.shape[0]):
        chosen = jnp.where(expert == ids[k : k + 1], 1.0, chosen)
    mine[rows:] = jnp.zeros((SMALL_ROWS, D), bf16)
    mine[rows : rows + 1, :rows] = gain_1_ref[...]
    mine[rows + 1 : rows + 2, :rows] = gain_2_ref[...]
    for t in range(experts // SMALL_ROWS):
        part = slice(t * SMALL_ROWS, (t + 1) * SMALL_ROWS)
        at = (1 + t) * LANES
        mine[rows:, at : at + rows] = router_ref[part]
        at = (1 + t + experts // SMALL_ROWS) * LANES
        mine[rows:, at : at + LANES] = chosen[part].astype(bf16)
    for core in range(2):

        @pl.when(place_ref[1] == core)
        def _(core=core):
            mine[:rows, :QC] = wq_ref[:, core * QC : (core + 1) * QC]
            mine[:rows, QC : QC + KC] = wk_ref[:, core * KC : (core + 1) * KC]
            mine[:rows, QC + KC :] = wv_ref[:, core * KC : (core + 1) * KC]
            out_mine[...] = wo_ref[:, core * half : (core + 1) * half]


def put_lanes(ref, piece, owner, rows):
    start = owner * rows
    at = pl.ds(pl.multiple_of(start // LANES * LANES, LANES), LANES)
    if rows < LANES:
        off = start % LANES
        lane = lane_index(piece.shape)
        piece = pltpu.roll(piece, off, 1)
        piece = jnp.where((lane >= off) & (lane < off + rows), piece, ref[:, at])
    ref[:, at] = piece


def fetch(n, rows, owner_ref, pairs, sems, small=None):
    copies = []
    for blocks, target in pairs:
        for k in range(n):
            at = pl.ds(pl.multiple_of(owner_ref[k] * rows, rows), rows)
            copies.append(pltpu.make_async_copy(blocks[k].at[pl.ds(0, rows)], target.at[at], sems.at[len(copies)]))
    for k in range(n if small is not None else 0):
        source = pairs[0][0][k].at[pl.ds(rows, SMALL_ROWS)]
        copies.append(pltpu.make_async_copy(source, small.at[k], sems.at[len(copies)]))
    for copy in copies:
        copy.start()
    return copies


def attention_kernel(n, rows, place_ref, owner_ref, own_ref, other_ref, cos_ref, sin_ref, *refs):
    blocks = refs[:n]
    w_ref, small_ref, gain_ref, normed_ref, inv_ref, q_ref, k_ref, v_ref, lse_ref, att_ref, window, sems = refs[n:]
    copies = fetch(n, rows, owner_ref, ((blocks, w_ref),), sems, small_ref)
    packets = (own_ref, other_ref)
    scaled = []
    for g, packet in enumerate(packets):
        values = packet[:HALO].astype(f32)
        inv = inverse_rms(values)
        inv_ref[g * TOK_DEV : (g + 1) * TOK_DEV] = inv[:TOK_DEV]
        scaled.append(values * inv)
    for k in range(n):
        copies[n + k].wait()
    for k in range(n):
        put_lanes(gain_ref, small_ref[k, :1, :LANES].astype(f32), owner_ref[k], rows)
    gain = gain_ref[...]
    for g in range(2):
        base = 2 * TOK_DEV * g
        normed = (scaled[g] * gain).astype(bf16)
        window[base : base + HALF] = jnp.zeros((HALF, D), bf16)
        window[base + HALF : base + TOK_DEV] = normed[TOK_DEV:]
        window[base + TOK_DEV : base + 2 * TOK_DEV] = normed[:TOK_DEV]
        normed_ref[g * TOK_DEV : (g + 1) * TOK_DEV] = normed[:TOK_DEV]
    for copy in copies[:n]:
        copy.wait()
    q_both = dot(normed_ref[...], w_ref[:, :QC])
    kv_both = dot(window[...], w_ref[:, QC:])
    cos, sin = cos_ref[...], sin_ref[...]
    lane = lane_index((TOK_DEV, LANES))
    for g in range(2):
        tok = slice(g * TOK_DEV, (g + 1) * TOK_DEV)
        win = slice(2 * g * TOK_DEV, 2 * (g + 1) * TOK_DEV)
        q_lin, kv_lin = q_both[tok], kv_both[win]
        allowed = allowed_pairs(place_ref[0], packets[g])
        v_ref[win] = kv_lin[:, KC:].astype(bf16)
        lse = jnp.zeros((TOK_DEV, LANES), f32)
        for pair in range(KC // LANES):
            cols = slice(pair * LANES, (pair + 1) * LANES)
            keys = rotate(kv_lin[:, cols], cos, sin)
            k_ref[win, cols] = keys.astype(bf16)
            key_sides = apart(keys)
            value_sides = apart(kv_lin[:, KC + pair * LANES : KC + (pair + 1) * LANES])
            for one in range(2):
                head = 2 * pair + one
                q_cols = slice(head * LANES, (head + 1) * LANES)
                queries = rotate(q_lin[:, q_cols], cos[TOK_DEV:], sin[TOK_DEV:]).astype(bf16)
                q_ref[tok, q_cols] = queries
                out = 0.0
                for side in range(2):
                    scores = dot_t(queries, key_sides[one][side]) * SCORE_SCALE
                    scores = jnp.where(allowed, scores, NEG_LARGE)
                    highest = jnp.max(scores, -1, keepdims=True)
                    raised = jnp.exp(scores - highest)
                    log_total = highest + jnp.log(jnp.sum(raised, -1, keepdims=True))
                    lse = jnp.where(lane == 2 * head + side, log_total, lse)
                    probs = jnp.exp(scores - log_total).astype(bf16)
                    out = out + dot(probs, value_sides[one][side])
                att_ref[tok, q_cols] = out.astype(bf16)
        lse_ref[tok] = lse


def both_halves(place_ref, mine, got):
    first_core = place_ref[1] == 0
    mine, got = mine.astype(f32), got.astype(f32)
    return jnp.concatenate([jnp.where(first_core, mine, got), jnp.where(first_core, got, mine)], 1)


def output_kernel(n, rows, place_ref, owner_ref, att_ref, got_ref, *refs):
    blocks, (w_ref, both_ref, own_ref, send_ref, sems) = refs[:n], refs[n:]
    copies = fetch(n, rows, owner_ref, ((blocks, w_ref),), sems)
    own, other = slice(0, TOK_DEV), slice(TOK_DEV, 2 * TOK_DEV)
    both_ref[own] = both_halves(place_ref, att_ref[own], got_ref[other]).astype(bf16)
    both_ref[other] = both_halves(place_ref, att_ref[other], got_ref[own]).astype(bf16)
    for copy in copies:
        copy.wait()
    proj = dot(both_ref[...], w_ref[...])
    own_ref[...] = proj[own]
    send_ref[...] = proj[other]


def hidden_kernel(n, rows, experts, place_ref, owner_ref, own_ref, got_ref, tok_ref, small_ref, gain_ref, router_ref, chosen_ref, hidden_ref, inv_ref, ffn_ref, router):
    for k in range(n):
        tiles = [small_ref[k, :, i * LANES : (i + 1) * LANES].astype(f32) for i in range(1 + 2 * experts // SMALL_ROWS)]
        put_lanes(gain_ref, tiles[0][1:2], owner_ref[k], rows)
        put_lanes(router, jnp.concatenate(tiles[1 : 1 + experts // SMALL_ROWS], 0), owner_ref[k], rows)
        chosen = jnp.concatenate(tiles[1 + experts // SMALL_ROWS :], 0)
        chosen = jnp.concatenate([chosen, jnp.zeros((LANES - experts, LANES), f32)], 0).T
        chosen_ref[k * TOK_DEV : (k + 1) * TOK_DEV] = chosen[:, :experts]
    router_ref[...] = router[...].astype(bf16)
    hidden = tok_ref[...].astype(f32) + RESIDUAL_SCALE * both_halves(place_ref, own_ref[...], got_ref[...])
    hidden_ref[...] = hidden
    inv = inverse_rms(hidden)
    inv_ref[...] = inv
    ffn_ref[...] = (hidden * inv * gain_ref[...]).astype(bf16)


def block_lanes(ref, row, owner, rows):
    start = owner * rows
    piece = ref[row : row + 1, pl.ds(pl.multiple_of(start // LANES * LANES, LANES), LANES)]
    if rows < LANES:
        piece = pltpu.roll(piece, (LANES - start % LANES) % LANES, 1)
    return piece


def hidden_grad_kernel(experts, back0_ref, back1_ref, back2_ref, gates_ref, ffn_ref, hidden_ref, inv_ref, gain_ref, router_ref, up_ref, branch_ref, small_ref):
    back = back0_ref[...].astype(f32) + back1_ref[...].astype(f32) + back2_ref[...].astype(f32)
    gate_grad = back[:, D : D + experts] + back[:, D + experts : D + 2 * experts]
    gates = gates_ref[...]
    logit_grad = (gates * (gate_grad - jnp.sum(gates * gate_grad, -1, keepdims=True))).astype(bf16)
    hidden, inv, gain = hidden_ref[...], inv_ref[...], gain_ref[...]
    grad = back[:, :D] + dot(logit_grad, router_ref[...])
    scaled = grad * gain
    through = inv * scaled - hidden * (inv * inv * inv) * jnp.mean(scaled * hidden, -1, keepdims=True)
    hidden_grad = up_ref[...].astype(f32) + through
    branch_ref[...] = (RESIDUAL_SCALE * hidden_grad).astype(bf16)
    small_ref[:experts] = t_dot(logit_grad, ffn_ref[...])
    small_ref[experts : experts + 1] = jnp.sum(grad * hidden * inv, 0, keepdims=True)


def output_grad_kernel(place_ref, own_ref, got_ref, w_ref, keep_ref, send_ref, cols_ref):
    half = D // 2
    first_core = place_ref[1] == 0
    both = jnp.concatenate([own_ref[...], got_ref[...]], 0).astype(f32)
    cols = jnp.where(first_core, both[:, :half], both[:, half:]).astype(bf16)
    cols_ref[...] = cols
    grad = dot_t(cols, w_ref[...])
    keep_ref[...] = jnp.where(first_core, grad[:, :QC], grad[:, QC:])
    send_ref[...] = jnp.where(first_core, grad[:, QC:], grad[:, :QC]).astype(bf16)


def output_weight_grad_kernel(n, rows, small_count, owner_ref, both_ref, cols_ref, small_ref, *refs):
    blocks, grads = refs[:n], refs[n]
    grads[...] = t_dot(both_ref[...], cols_ref[...])
    packed = grads.shape[1] // LANES
    for k in range(n):
        at = pl.ds(pl.multiple_of(owner_ref[k] * rows, rows), rows)
        blocks[k][:rows] = grads[at, :].astype(bf16)
        blocks[k][rows:] = jnp.zeros((blocks[k].shape[0] - rows, grads.shape[1]), bf16)
        for i in range(small_count):
            piece = block_lanes(small_ref, i, owner_ref[k], rows)
            lane = i % packed * LANES
            blocks[k][rows + i // packed : rows + i // packed + 1, lane : lane + LANES] = piece.astype(bf16)


def attention_grad_kernel(place_ref, own_ref, other_ref, q_ref, k_ref, v_ref, lse_ref, att_ref, ag_ref, ag_got_ref, cos_ref, sin_ref, q_pre_ref, kv_own_ref, kv_before_ref):
    cos, sin = cos_ref[...], sin_ref[...]
    low = lane_index((TOK_DEV, LANES)) < HEAD_DIM
    for g, packet_ref in enumerate((own_ref, other_ref)):
        tok = slice(g * TOK_DEV, (g + 1) * TOK_DEV)
        there = slice((1 - g) * TOK_DEV, (2 - g) * TOK_DEV)
        win = slice(2 * g * TOK_DEV, 2 * (g + 1) * TOK_DEV)
        halo = slice(g * HALF, (g + 1) * HALF)
        allowed = allowed_pairs(place_ref[0], packet_ref)
        for pair in range(KC // LANES):
            cols = slice(pair * LANES, (pair + 1) * LANES)
            key_sides, value_sides = apart(k_ref[win, cols]), apart(v_ref[win, cols])
            key_grad = jnp.zeros((2 * TOK_DEV, LANES), f32)
            value_grad = jnp.zeros((2 * TOK_DEV, LANES), f32)
            for one in range(2):
                head = 2 * pair + one
                q_cols = slice(head * LANES, (head + 1) * LANES)
                queries = q_ref[tok, q_cols]
                grads = (ag_ref[tok, q_cols] + ag_got_ref[there, q_cols].astype(f32)).astype(bf16)
                query_sides, grad_sides = apart(queries), apart(grads)
                product = grads.astype(f32) * att_ref[tok, q_cols].astype(f32)
                query_grad = jnp.zeros((TOK_DEV, LANES), f32)
                for side in range(2):
                    k_side, v_side = key_sides[one][side], value_sides[one][side]
                    log_total = lse_ref[tok, 2 * head + side : 2 * head + side + 1]
                    delta = jnp.sum(jnp.where(low == (side == 0), product, 0.0), -1, keepdims=True)
                    scores = dot_t(queries, k_side) * SCORE_SCALE
                    probs = jnp.where(allowed, jnp.exp(scores - log_total), 0.0)
                    prob_grad = dot_t(grads, v_side)
                    score_grad = (probs * (prob_grad - delta) * SCORE_SCALE).astype(bf16)
                    query_grad = query_grad + dot(score_grad, k_side)
                    key_grad = key_grad + t_dot(score_grad, query_sides[side][one])
                    value_grad = value_grad + t_dot(probs.astype(bf16), grad_sides[side][one])
                q_pre_ref[tok, q_cols] = rotate_back(query_grad, cos[TOK_DEV:], sin[TOK_DEV:]).astype(bf16)
            v_cols = slice(KC + pair * LANES, KC + (pair + 1) * LANES)
            key_grad = rotate_back(key_grad, cos, sin)
            kv_own_ref[tok, cols] = key_grad[TOK_DEV:]
            kv_own_ref[tok, v_cols] = value_grad[TOK_DEV:]
            kv_before_ref[halo, cols] = key_grad[HALF:TOK_DEV].astype(bf16)
            kv_before_ref[halo, v_cols] = value_grad[HALF:TOK_DEV].astype(bf16)


def projection_grad_kernel(n, rows, owner_ref, q_pre_ref, kv_own_ref, later_ref, normed_ref, w_ref, own_ref, other_ref, inv_ref, *refs):
    blocks, (aig_own_ref, aig_send_ref, grads, gain_grad) = refs[:n], refs[n:]
    kv, later = kv_own_ref[...], later_ref[...].astype(f32)
    parts = []
    for g in range(2):
        at = g * TOK_DEV
        parts += [kv[at : at + HALF], kv[at + HALF : at + TOK_DEV] + later[g * HALF : (g + 1) * HALF]]
    pre = jnp.concatenate([q_pre_ref[...], jnp.concatenate(parts, 0).astype(bf16)], 1)
    grads[...] = t_dot(normed_ref[...], pre)
    aig = dot_t(pre, w_ref[...])
    values = jnp.concatenate([own_ref[:TOK_DEV], other_ref[:TOK_DEV]], 0).astype(f32)
    gain_grad[...] = jnp.sum(aig * values * inv_ref[...], 0, keepdims=True)
    for k in range(n):
        at = pl.ds(pl.multiple_of(owner_ref[k] * rows, rows), rows)
        blocks[k][:rows] = grads[at, :].astype(bf16)
        blocks[k][rows:] = jnp.zeros((blocks[k].shape[0] - rows, D), bf16)
        blocks[k][rows : rows + 1, :LANES] = block_lanes(gain_grad, 0, owner_ref[k], rows).astype(bf16)
    aig_own_ref[...] = aig[:TOK_DEV]
    aig_send_ref[...] = aig[TOK_DEV:]


def input_grad_kernel(aig_ref, got_ref, own_ref, inv_ref, gain_ref, up_ref, out_ref):
    grad = aig_ref[...] + got_ref[...]
    values, inv = own_ref[:TOK_DEV].astype(f32), inv_ref[:TOK_DEV]
    scaled = grad * gain_ref[...]
    through = inv * scaled - values * (inv * inv * inv) * jnp.mean(scaled * values, -1, keepdims=True)
    out_ref[...] = (up_ref[...].astype(f32) + through).astype(bf16)


def assemble_kernel(experts, place_ref, in_own, in_got, out_own, out_got, wq_ref, wk_ref, wv_ref, wo_ref, gain_1_ref, gain_2_ref, router_ref):
    rows = wq_ref.shape[0]
    half = D // 2
    for core, first, second, low, high in ((0, in_own, in_got, out_own, out_got), (1, in_got, in_own, out_got, out_own)):

        @pl.when(place_ref[1] == core)
        def _(sides=((first, low), (second, high))):
            for c, (into, out) in enumerate(sides):
                wq_ref[:, c * QC : (c + 1) * QC] = into[:rows, :QC]
                wk_ref[:, c * KC : (c + 1) * KC] = into[:rows, QC : QC + KC]
                wv_ref[:, c * KC : (c + 1) * KC] = into[:rows, QC + KC :]
                wo_ref[:, c * half : (c + 1) * half] = out[:rows]

    gain_1_ref[...] = in_own[rows : rows + 1, :rows] + in_got[rows : rows + 1, :rows]
    small = out_own[rows:] + out_got[rows:]
    packed = half // LANES
    for i in range(experts + 1):
        piece = small[i // packed : i // packed + 1, i % packed * LANES : i % packed * LANES + rows]
        if i < experts:
            router_ref[i : i + 1] = piece
        else:
            gain_2_ref[...] = piece


def expert_kernel(size, count, experts, shard_ref, *refs):
    x_refs, up_refs = refs[:count], refs[count : 2 * count]
    chosen_ref, router_ref, wg_ref, wu_ref, wd_ref = refs[2 * count : 2 * count + 5]
    refs = refs[-(2 * count + 6 + 3) :]
    back_refs, mix_refs = refs[:count], refs[count : 2 * count]
    gates_ref, all_x, all_act, all_row, all_gate, all_up = refs[2 * count : 2 * count + 6]
    back_acc, mix_acc, cols_acc = refs[-3:]
    e = pl.program_id(0)
    rows = size * count
    x = jnp.concatenate([ref[...] for ref in x_refs], 0)
    grad = RESIDUAL_SCALE * jnp.concatenate([ref[...] for ref in up_refs], 0).astype(f32)

    @pl.when(e == 0)
    def _():
        chosen = chosen_ref[...] > 0
        logits = jnp.where(chosen, dot_t(x, router_ref[...]), NEG_LARGE)
        raised = jnp.where(chosen, jnp.exp(logits - jnp.max(logits, -1, keepdims=True)), 0.0)
        gates_ref[...] = raised / jnp.sum(raised, -1, keepdims=True)
        all_x[...] = x

    here = lax.broadcasted_iota(jnp.int32, (rows, experts), 1) == shard_ref[0] * EXP_DEV + e
    gate = jnp.sum(jnp.where(here, gates_ref[...], 0.0), -1, keepdims=True)
    gate_pre = dot(x, wg_ref[0])
    up_pre = dot(x, wu_ref[0])
    gate_sig = 1.0 / (1.0 + jnp.exp(-gate_pre))
    silu = gate_pre * gate_sig
    activated = (silu * up_pre).astype(bf16)
    all_act[0] = activated
    expert_out = dot(activated, wd_ref[0]).astype(bf16).astype(f32)
    mix = gate * expert_out
    cols = jnp.where(here, jnp.sum(grad * expert_out, -1, keepdims=True), 0.0)
    row_grad = (gate * grad).astype(bf16)
    all_row[0] = row_grad
    unit = dot_t(row_grad, wd_ref[0])
    gate_grad = (unit * up_pre * gate_sig * (1.0 + gate_pre * (1.0 - gate_sig))).astype(bf16)
    up_grad = (unit * silu).astype(bf16)
    all_gate[0] = gate_grad
    all_up[0] = up_grad
    back = dot_t(gate_grad, wg_ref[0]) + dot_t(up_grad, wu_ref[0])

    @pl.when(e == 0)
    def _():
        back_acc[...] = back
        mix_acc[...] = mix
        cols_acc[...] = cols

    @pl.when(e == EXP_DEV - 1)
    def _():
        whole_back = (back_acc[...] + back).astype(bf16)
        whole_mix = (mix_acc[...] + mix).astype(bf16)
        whole_cols = cols_acc[...] + cols
        high = whole_cols.astype(bf16)
        low = (whole_cols - high.astype(f32)).astype(bf16)
        for k in range(count):
            part = slice(k * size, (k + 1) * size)
            back_refs[k][:, :D] = whole_back[part]
            back_refs[k][:, D:] = jnp.zeros((size, LANES), bf16)
            back_refs[k][:, D : D + experts] = high[part]
            back_refs[k][:, D + experts : D + 2 * experts] = low[part]
            mix_refs[k][...] = whole_mix[part]


def expert_weight_kernel(replicas, place_ref, x_ref, act_ref, row_ref, gate_ref, up_ref, keep_ref, send_ref, wide, tall):
    x = x_ref[...]
    for kind, grads in enumerate((gate_ref, up_ref)):
        tall[...] = t_dot(x, grads[0])
        own = tall.shape[0] // replicas
        for j in range(replicas // 2):
            for target, core in ((keep_ref, place_ref[1]), (send_ref, 1 - place_ref[1])):
                at = pl.ds(pl.multiple_of((2 * j + core) * own, own), own)
                target[kind, j] = tall[at, :].astype(bf16)
    wide[...] = t_dot(act_ref[0], row_ref[0])
    own = wide.shape[0] // replicas
    half = wide.shape[1] // 2
    for j in range(replicas // 2):
        for target, core in ((keep_ref, place_ref[1]), (send_ref, 1 - place_ref[1])):
            at = pl.ds(pl.multiple_of((2 * j + core) * own, own), own)
            target[2, j, :own] = wide[at, :half].astype(bf16)
            target[2, j, own:] = wide[at, half:].astype(bf16)


def expert_weight_grads(replicas, place, held, e):
    group_in, act, row, gate, up = held
    ff = act.shape[2]
    own = D // replicas
    shape = (3, replicas // 2, own, ff)

    def one(width):
        return pl.BlockSpec((1, group_in.shape[0], width), lambda i: (e, 0, 0))

    return pl.pallas_call(
        functools.partial(expert_weight_kernel, replicas),
        grid=(1,),
        in_specs=[
            pl.BlockSpec(memory_space=pltpu.SMEM),
            pl.BlockSpec(group_in.shape, lambda i: (0, 0)),
            one(ff),
            one(D),
            one(ff),
            one(ff),
        ],
        out_specs=[pl.BlockSpec(shape, lambda i: (0, 0, 0, 0))] * 2,
        out_shape=[jax.ShapeDtypeStruct(shape, bf16)] * 2,
        scratch_shapes=[pltpu.VMEM((ff, D), f32), pltpu.VMEM((D, ff), f32)],
        compiler_params=pltpu.CompilerParams(vmem_limit_bytes=32 * 2**20),
        cost_estimate=pl.CostEstimate(flops=2**32, bytes_accessed=2**23, transcendentals=0),
    )(place, group_in, act, row, gate, up)


def expert_sum_kernel(*refs):
    keeps, gots, (gate_ref, up_ref, down_ref) = refs[:EXP_DEV], refs[EXP_DEV : 2 * EXP_DEV], refs[2 * EXP_DEV :]
    own = down_ref.shape[1]
    for e in range(EXP_DEV):
        total = [keeps[e][kind].astype(f32) + gots[e][kind].astype(f32) for kind in range(3)]
        gate_ref[e] = total[0]
        up_ref[e] = total[1]
        down_ref[e, :, : total[2].shape[1]] = total[2][:own]
        down_ref[e, :, total[2].shape[1] :] = total[2][own:]


def replica_split_kernel(place_ref, keep_ref, got_ref, stay_ref, send_ref):
    here = place_ref[2] // 2 % 2
    for kind in range(3):
        for j in range(stay_ref.shape[1]):
            for target, at in ((stay_ref, 2 * j + here), (send_ref, 2 * j + 1 - here)):
                target[kind, j] = (keep_ref[kind, at].astype(f32) + got_ref[kind, at].astype(f32)).astype(bf16)


def run_experts(block, count, total, shard, x, up, chosen, router, w_gate, w_up, w_down, held):
    rows = TOK_DEV * count
    experts = chosen.shape[1]
    ff = w_gate.shape[2]
    at = block // count

    def whole(shape):
        return pl.BlockSpec(shape, lambda e: (0,) * len(shape))

    def one(shape):
        return pl.BlockSpec((1,) + shape, lambda e: (e,) + (0,) * len(shape))

    def filled(width):
        return pl.BlockSpec((1, rows, width), lambda e: (e, at, 0))

    every = TOK_DEV * total
    out_shape = (
        [jax.ShapeDtypeStruct((TOK_DEV, D + LANES), bf16)] * count
        + [jax.ShapeDtypeStruct((TOK_DEV, D), bf16)] * count
        + [jax.ShapeDtypeStruct((rows, experts), f32)]
    )
    held_shape = [
        jax.ShapeDtypeStruct((every, D), bf16),
        jax.ShapeDtypeStruct((EXP_DEV, every, ff), bf16),
        jax.ShapeDtypeStruct((EXP_DEV, every, D), bf16),
        jax.ShapeDtypeStruct((EXP_DEV, every, ff), bf16),
        jax.ShapeDtypeStruct((EXP_DEV, every, ff), bf16),
    ]
    out_specs = (
        [whole((TOK_DEV, D + LANES))] * count
        + [whole((TOK_DEV, D))] * count
        + [whole((rows, experts))]
        + [pl.BlockSpec((rows, D), lambda e: (at, 0))]
        + [filled(ff), filled(D), filled(ff), filled(ff)]
    )
    in_specs = [
        pl.BlockSpec(memory_space=pltpu.SMEM),
        *[whole((TOK_DEV, D))] * (2 * count),
        pl.BlockSpec((rows, experts), lambda e: (at, 0)),
        whole(router.shape),
        one(w_gate.shape[1:]),
        one(w_up.shape[1:]),
        one(w_down.shape[1:]),
    ]
    args = [shard, *x, *up, chosen, router, w_gate, w_up, w_down]
    aliases = {}
    if held is not None:
        aliases = {len(args) + k: len(out_shape) + k for k in range(len(held))}
        in_specs = in_specs + [pl.BlockSpec(memory_space=pl.ANY)] * len(held)
        args = args + list(held)
    flops = 12 * rows * D * ff * EXP_DEV
    outs = pl.pallas_call(
        functools.partial(expert_kernel, TOK_DEV, count, experts),
        grid=(EXP_DEV,),
        in_specs=in_specs,
        out_specs=out_specs,
        out_shape=out_shape + held_shape,
        scratch_shapes=[
            pltpu.VMEM((rows, D), f32),
            pltpu.VMEM((rows, D), f32),
            pltpu.VMEM((rows, experts), f32),
        ],
        input_output_aliases=aliases,
        compiler_params=pltpu.CompilerParams(vmem_limit_bytes=24 * 2**20),
        cost_estimate=pl.CostEstimate(
            flops=flops, bytes_accessed=6 * D * ff * EXP_DEV + 16 * rows * D, transcendentals=rows * ff * EXP_DEV
        ),
    )(*args)
    return outs[:count], outs[count : 2 * count], outs[2 * count], outs[2 * count + 1 :]


def per_device(
    tokens,
    segment_ids,
    expert_ids,
    attn_gain,
    w_query,
    w_key,
    w_value,
    w_output,
    ffn_gain,
    w_router,
    w_gate,
    w_up,
    w_down,
    out_grad,
):
    shard = lax.axis_index("shard")
    core = lax.axis_index("rep") % 2
    ring = Ring()
    n = ring.n
    experts = EXP_DEV * n
    rows = w_query.shape[0]
    half_width = D // 2

    replicas = lax.axis_size("rep")
    place = jnp.stack([shard, core, lax.axis_index("rep")]).astype(jnp.int32)
    owners = ring.row
    cos, sin = rotary_tables()
    shift_up = [(i, i + 1) for i in range(n - 1)]
    shift_down = [(i + 1, i) for i in range(n - 1)]

    in_own, out_own = call(
        split_kernel,
        [vmem((rows + SMALL_ROWS, D), bf16), vmem((rows, half_width), bf16)],
        [place],
        [attn_gain[None], ffn_gain[None], w_router.T, expert_ids[0].T, w_query, w_key, w_value, w_output],
        limit=60,
    )
    in_ring = Gather(ring, in_own)
    in_ring.step()
    seg_row = jnp.pad(segment_ids.astype(bf16), ((0, SEG_ROWS - 1), (0, D - TOK_DEV)))
    before = jnp.concatenate([tokens[0, HALF:], seg_row], axis=0)
    before = lax.ppermute(after(before, in_ring.got[-1]), "shard", shift_up)
    packet = jnp.concatenate([tokens[0], before, seg_row], axis=0)
    in_ring.step()
    packet_other = swap(after(packet, in_ring.got[-2]), 1)
    while in_ring.left > 1:
        in_ring.step()
    out_ring = Gather(ring, after(out_own, in_ring.got[-in_ring.done[-1]]), flip=True)
    in_ring.step()
    out_ring.hop(1)
    out_ring.got, up_own = after((out_ring.got, out_grad[0]), *in_ring.blocks())
    up = Gather(ring, up_own)
    out_ring.step()
    up.step()
    in_w, small, first_gain, normed, inv_first, queries, keys, values, log_total, att = call(
        functools.partial(attention_kernel, n, rows),
        [
            vmem((D, D), bf16),
            vmem((n, SMALL_ROWS, D), bf16),
            vmem((1, D), f32),
            vmem((2 * TOK_DEV, D), bf16),
            vmem((2 * TOK_DEV, 1), f32),
            vmem((2 * TOK_DEV, QC), bf16),
            vmem((4 * TOK_DEV, KC), bf16),
            vmem((4 * TOK_DEV, KC), bf16),
            vmem((2 * TOK_DEV, LANES), f32),
            vmem((2 * TOK_DEV, QC), bf16),
        ],
        [place, owners],
        [packet, packet_other, cos, sin],
        [pltpu.VMEM((4 * TOK_DEV, D), bf16), pltpu.SemaphoreType.DMA((2 * n,))],
        flops=2**32,
        anywhere=in_ring.blocks(),
    )
    out_ring.got, up.got, att = together(out_ring.got, up.got, att)
    att_got = swap(att, 1)
    out_ring.step()
    up.step()
    while out_ring.left:
        out_ring.step()
    out_blocks, att_got, up.got = together(out_ring.blocks(), att_got, up.got)
    out_w, attended, proj, proj_send = call(
        functools.partial(output_kernel, n, rows),
        [
            vmem((QW, half_width), bf16),
            vmem((2 * TOK_DEV, QW), bf16),
            vmem((TOK_DEV, half_width), f32),
            vmem((TOK_DEV, half_width), f32),
        ],
        [place, owners],
        [att, att_got],
        [pltpu.SemaphoreType.DMA((n,))],
        flops=2**30,
        anywhere=out_blocks,
    )
    second_gain, router, group_chosen, hidden, inv_second, ffn_inputs = call(
        functools.partial(hidden_kernel, n, rows, experts),
        [
            vmem((1, D), f32),
            vmem((experts, D), bf16),
            vmem((n * TOK_DEV, experts), f32),
            vmem((TOK_DEV, D), f32),
            vmem((TOK_DEV, 1), f32),
            vmem((TOK_DEV, D), bf16),
        ],
        [place, owners],
        [proj, swap(proj_send, 1), tokens[0], small],
        [pltpu.VMEM((experts, D), f32)],
        flops=2**28,
    )


    group = Gather(ring, ffn_inputs)
    while group.left:
        group.step()
        if up.left:
            up.step()
    held = None
    back_parts = [None] * n
    own_gates = None
    mix_parts = [None] * n
    runs = [(0, 1)] + [(k, 2) for k in range(2, n, 2)] + [(1, 1)]
    for block, count in runs:
        part = slice(block, block + count)
        backs, mixes, gates, held = run_experts(
            block,
            count,
            n,
            place[:1],
            [group.got[o] for o in ring.offsets[part]],
            [up.got[o] for o in ring.offsets[part]],
            group_chosen,
            router,
            w_gate,
            w_up,
            w_down,
            held,
        )
        back_parts[part] = backs
        mix_parts[part] = mixes
        own_gates = gates if block == 0 else own_gates

    back, mix = Scatter(ring, back_parts), Scatter(ring, mix_parts, flip=True)
    stays, crossing, made = [], [], []
    while back.left:
        if back.left == 1:
            back.got = after(back.got, made)
            mix.sums = after(mix.sums, back.got)
            mix.hop(1)
        back.step()
        if len(stays) < EXP_DEV:
            held = after(held, back.got)
            keep, send = expert_weight_grads(replicas, place, held, len(stays))
            made.append(send)
            stay, send = call(
                replica_split_kernel,
                [vmem((3, replicas // 4, *keep.shape[2:]), bf16)] * 2,
                [place],
                [keep, swap(send, 1)],
            )
            stays.append(stay)
            crossing.append(send)
    own_gates, crossing[0] = together(own_gates, crossing[0])
    crossing[0] = swap(crossing[0], 2)

    branch, out_small = call(
        functools.partial(hidden_grad_kernel, experts),
        [vmem((TOK_DEV, D), bf16), vmem((experts + 1, D), f32)],
        [],
        [
            *back.terms(),
            own_gates,
            ffn_inputs,
            hidden,
            inv_second,
            second_gain,
            router,
            out_grad[0],
        ],
        flops=2**28,
    )
    ag_keep, ag_send, branch_cols = call(
        output_grad_kernel,
        [
            vmem((2 * TOK_DEV, QC), f32),
            vmem((2 * TOK_DEV, QC), bf16),
            vmem((2 * TOK_DEV, half_width), bf16),
        ],
        [place],
        [branch, swap(branch, 1), out_w],
        flops=2**29,
    )
    mix.got, mix.sums = after((mix.got, mix.sums), *back.terms())
    mix.step()
    ag_got = swap(ag_send, 1)
    extra = -(-(experts + 1) // (8 * (half_width // LANES))) * 8
    out_blocks = call(
        functools.partial(output_weight_grad_kernel, n, rows, experts + 1),
        [vmem((rows + extra, half_width), bf16)] * n,
        [owners],
        [attended, branch_cols, out_small],
        [pltpu.VMEM((QW, half_width), f32)],
        flops=2**29,
    )
    ag_got, out_blocks = together(ag_got, out_blocks)
    out = Scatter(ring, out_blocks)
    out.step()
    q_pre, kv_own, kv_before = call(
        attention_grad_kernel,
        [
            vmem((2 * TOK_DEV, QC), bf16),
            vmem((2 * TOK_DEV, 2 * KC), f32),
            vmem((TOK_DEV, 2 * KC), bf16),
        ],
        [place],
        [packet, packet_other, queries, keys, values, log_total, att, ag_keep, ag_got, cos, sin],
        flops=2**32,
    )
    kv_before, out.got, mix.got = together(kv_before, out.got, mix.got)
    later = lax.ppermute(kv_before, "shard", shift_down)
    out.got = after(out.got, later)
    out.step()
    *in_blocks, aig_own, aig_send = call(
        functools.partial(projection_grad_kernel, n, rows),
        [vmem((rows + 8, D), bf16)] * n + [vmem((TOK_DEV, D), f32)] * 2,
        [owners],
        [q_pre, kv_own, later, normed, in_w, packet, packet_other, inv_first],
        [pltpu.VMEM((D, D), f32), pltpu.VMEM((1, D), f32)],
        flops=2**32,
    )
    in_blocks, out.got, crossing[0] = together(in_blocks, out.got, crossing[0])
    crossing[1] = swap(after(crossing[1], crossing[0]), 2)

    def owned(sums):
        own, ahead, behind = sums.terms()
        return rep_sum(own.astype(f32) + ahead.astype(f32) + behind.astype(f32))

    into = Scatter(ring, in_blocks)
    into.step()
    while out.left > 1:
        out.step()
    into.got, out.got = together(into.got, out.got)
    into.step()
    out.step()
    aig_got = swap(aig_send, 1)
    into.got, out.got, aig_got = together(into.got, out.got, aig_got)
    input_grad = call(
        input_grad_kernel,
        [vmem((TOK_DEV, D), bf16)],
        [],
        [aig_own, aig_got, packet, inv_first, first_gain, out_grad[0]],
    )[0]
    into.step()
    into.got, input_grad = together(into.got, input_grad)
    while into.left:
        into.step()
    into.got, crossing[1], out.got = together(into.got, crossing[1], out.got)
    out_sum = owned(out)
    out_got = swap(out_sum, 1)
    left = replicas // 4
    for bit in list(bits())[2:]:
        left //= 2
        here = (lax.axis_index("rep") // bit) % 2
        for e in range(EXP_DEV):
            total = (stays[e].astype(f32) + crossing[e].astype(f32)).astype(bf16)
            pairs = total.reshape(3, left, 2, *total.shape[2:])
            stays[e] = lax.dynamic_index_in_dim(pairs, here, 2, False)
            crossing[e] = swap(lax.dynamic_index_in_dim(pairs, 1 - here, 2, False), bit)
    ff, own_rows = w_gate.shape[2], D // replicas
    gate_sum, up_sum, down_sum = call(
        expert_sum_kernel,
        [
            vmem((EXP_DEV, own_rows, ff), f32),
            vmem((EXP_DEV, own_rows, ff), f32),
            vmem((EXP_DEV, ff // replicas, D), f32),
        ],
        [],
        [part[:, 0] for part in stays + crossing],
    )
    mix.got = after(mix.got, into.got)
    while mix.left:
        mix.step()
    moe_sum = sum(term.astype(f32) for term in mix.terms())

    in_sum = owned(into)
    in_got = swap(in_sum, 1)
    g_query, g_key, g_value, g_output, gain_1, gain_2, g_router = call(
        functools.partial(assemble_kernel, experts),
        [
            vmem((rows, QW), f32),
            vmem((rows, KW), f32),
            vmem((rows, KW), f32),
            vmem((rows, D), f32),
            vmem((1, rows), f32),
            vmem((1, rows), f32),
            vmem((experts, rows), f32),
        ],
        [place],
        [in_sum, in_got, out_sum, out_got],
    )
    mixed = (hidden + RESIDUAL_SCALE * moe_sum).astype(bf16)
    return (
        mixed[None],
        input_grad[None],
        gain_1[0],
        g_query,
        g_key,
        g_value,
        g_output,
        gain_2[0],
        g_router.T,
        gate_sum,
        up_sum,
        down_sum,
    )


def solution(mesh):
    return jax.shard_map(
        per_device,
        mesh=mesh,
        in_specs=(
            P("rep", "shard", None),
            P("rep", "shard"),
            P("rep", "shard", None),
            P("shard"),
            P("shard", None),
            P("shard", None),
            P("shard", None),
            P("shard", None),
            P("shard"),
            P("shard", None),
            P("shard", None, None),
            P("shard", None, None),
            P("shard", None, None),
            P("rep", "shard", None),
        ),
        out_specs=(
            P("rep", "shard", None),
            P("rep", "shard", None),
            P("shard"),
            P("shard", None),
            P("shard", None),
            P("shard", None),
            P("shard", None),
            P("shard"),
            P("shard", None),
            P("shard", "rep", None),
            P("shard", "rep", None),
            P("shard", "rep", None),
        ),
        check_vma=False,
    )
```

```python
import functools

import jax
import jax.numpy as jnp
import numpy as np
from jax import lax
from jax.experimental import pallas as pl
from jax.experimental.pallas import tpu as pltpu
from jax.sharding import PartitionSpec as P

D = 1024
HEADS = 16
KV_HEADS = 8
HEAD_DIM = 64
GROUP = HEADS // KV_HEADS
QW = HEADS * HEAD_DIM
KW = KV_HEADS * HEAD_DIM
QC = QW // 2
KC = KW // 2
ALONE = 384
SHARED = D - 2 * ALONE
WIDE = ALONE + SHARED
TOK_DEV = 128
HALF = TOK_DEV // 2
HALO = TOK_DEV + HALF
SEG_ROWS = 16
EXP_DEV = 2
LANES = 128

EPSILON = 1e-06
RESIDUAL_SCALE = 0.22
SCORE_SCALE = 0.015625
ROPE_BASE = 10000.0
NEG_LARGE = -1e30

bf16 = jnp.bfloat16
f32 = jnp.float32


def dot(a, b, contract=((1,), (0,))):
    return lax.dot_general(a, b, (contract, ((), ())), preferred_element_type=f32)


def dot_t(a, b):
    return dot(a, b, ((1,), (1,)))


def t_dot(a, b):
    return dot(a, b, ((0,), (0,)))


def cycle(length):
    rows = 4 if length % 4 == 0 else 1
    cols = length // rows
    if cols == 1:
        return list(range(length))
    order = [z * cols for z in range(rows)]
    for k, z in enumerate(reversed(range(rows))):
        ys = list(range(1, cols))
        order += [z * cols + y for y in (ys if k % 2 == 0 else reversed(ys))]
    return order


class Ring:
    def __init__(self):
        n = self.n = lax.axis_size("shard")
        cyc = self.cyc = cycle(n)
        self.next = [(cyc[i], cyc[(i + 1) % n]) for i in range(n)]
        self.prev = [(b, a) for a, b in self.next]
        self.ahead, self.back = n // 2, (n - 1) // 2
        self.offsets = [0, -self.ahead]
        for s in range(1, self.back + 1):
            self.offsets += [-s, s]
        place = {dev: i for i, dev in enumerate(cyc)}
        table = [[cyc[(place[dev] + o) % n] for o in self.offsets] for dev in range(n)]
        row = lax.dynamic_index_in_dim(jnp.asarray(table, jnp.int32), lax.axis_index("shard"), 0, False)
        self.row = row


class Gather:
    def __init__(self, ring, block, flip=False):
        self.ring, self.got, self.flip = ring, {0: block}, flip
        self.pairs = {-1: ring.next, 1: ring.prev}
        self.steps = {-1: ring.back, 1: ring.ahead} if flip else {-1: ring.ahead, 1: ring.back}
        self.done = {-1: 0, 1: 0}

    @property
    def left(self):
        return max(self.steps[sign] - self.done[sign] for sign in (-1, 1))

    def hop(self, sign):
        s = self.done[sign] = self.done[sign] + 1
        self.got[sign * s] = lax.ppermute(self.got[sign * (s - 1)], "shard", self.pairs[sign])

    def step(self):
        self.new = []
        for sign in (-1, 1):
            if self.done[sign] < self.steps[sign]:
                self.hop(sign)
                self.new.append(sign * self.done[sign])

    def blocks(self):
        half = self.ring.ahead
        if self.flip:
            self.got[-half] = self.got[half]
        return [self.got[o] for o in self.ring.offsets]


class Scatter:
    def __init__(self, ring, parts, flip=False):
        self.part = dict(zip(ring.offsets, parts))
        self.pairs = {-1: ring.prev, 1: ring.next}
        self.hops = {-1: ring.back, 1: ring.ahead} if flip else {-1: ring.ahead, 1: ring.back}
        if flip:
            self.part[ring.ahead] = self.part[-ring.ahead]
        self.sums = {sign: self.part[sign * steps] for sign, steps in self.hops.items()}
        self.got = {}

    @property
    def left(self):
        return max(self.hops.values())

    def hop(self, sign):
        if sign in self.got:
            part = self.part[sign * self.hops[sign]].astype(f32)
            self.sums[sign] = (self.got[sign].astype(f32) + part).astype(bf16)
        self.got[sign] = lax.ppermute(self.sums[sign], "shard", self.pairs[sign])
        self.hops[sign] -= 1

    def step(self):
        left = self.left
        for sign in (-1, 1):
            if self.hops[sign] == left:
                self.hop(sign)

    def terms(self):
        return self.part[0], self.got[-1], self.got[1]


def after(value, *earlier):
    return lax.optimization_barrier((value, *earlier))[0] if earlier else value


def together(*values):
    return lax.optimization_barrier(values)


def swap(value, bit):
    size = lax.axis_size("rep")
    return lax.ppermute(value, "rep", [(r, r ^ bit) for r in range(size)])


def bits():
    size, bit = lax.axis_size("rep"), 1
    while bit < size:
        yield bit
        bit *= 2


def rep_sum(value):
    for bit in list(bits())[1:]:
        low = lax.reduce_precision(value, 8, 7)
        value = low + swap(low.astype(bf16), bit).astype(f32)
    return value


def rotary_tables():
    positions = (np.arange(2 * TOK_DEV) + HALF) % TOK_DEV
    inverse = ROPE_BASE ** (-2.0 * np.arange(HEAD_DIM // 2) / HEAD_DIM)
    angles = positions[:, None] * inverse[None, :]
    cos, sin = np.cos(angles), np.sin(angles)
    cos, sin = np.concatenate([cos] * 4, axis=1), np.concatenate([-sin, sin] * 2, axis=1)
    return jnp.asarray(cos, f32), jnp.asarray(sin, f32)


def lane_index(shape):
    return lax.broadcasted_iota(jnp.int32, shape, 1)


def rotate(values, cos, sin):
    first = lane_index(values.shape) % HEAD_DIM < HEAD_DIM // 2
    turned = jnp.where(first, pltpu.roll(values, LANES - 32, 1), pltpu.roll(values, 32, 1))
    return values * cos + turned * sin


def rotate_back(values, cos, sin):
    first = lane_index(values.shape) % HEAD_DIM < HEAD_DIM // 2
    moved = values * sin
    turned = jnp.where(first, pltpu.roll(moved, LANES - 32, 1), pltpu.roll(moved, 32, 1))
    return values * cos + turned


def apart(pair):
    pair = pair.astype(f32)
    turned = pltpu.roll(pair, HEAD_DIM, 1)
    low = lane_index(pair.shape) < HEAD_DIM
    zero = jnp.zeros_like(pair)
    return (
        (jnp.where(low, pair, zero).astype(bf16), jnp.where(low, zero, turned).astype(bf16)),
        (jnp.where(low, turned, zero).astype(bf16), jnp.where(low, zero, pair).astype(bf16)),
    )


def allowed_pairs(shard_index, packet_ref):
    seg_before = packet_ref[HALO : HALO + 1, :LANES].astype(f32)
    seg_own = packet_ref[HALO + SEG_ROWS : HALO + SEG_ROWS + 1, :LANES].astype(f32)
    seg_key = jnp.concatenate([seg_before, seg_own], 1)
    seg_query = jnp.broadcast_to(seg_own, (TOK_DEV, TOK_DEV)).T[:, :1]
    shape = (TOK_DEV, 2 * TOK_DEV)
    query = lax.broadcasted_iota(jnp.int32, shape, 0)
    key = lax.broadcasted_iota(jnp.int32, shape, 1) - TOK_DEV
    allowed = (key <= query) & (key >= -HALF) & ((query >= HALF) == (key >= HALF))
    return allowed & ((key >= 0) | (shard_index > 0)) & (seg_query == seg_key)


def inverse_rms(values):
    return lax.rsqrt(jnp.mean(values * values, axis=-1, keepdims=True) + EPSILON)


def vmem(shape, dtype):
    return jax.ShapeDtypeStruct(shape, dtype)


def call(kernel, out_shape, scalars, arrays, scratch=(), flops=0, limit=20, anywhere=(), out_space=None):
    return pl.pallas_call(
        kernel,
        in_specs=[pl.BlockSpec(memory_space=pltpu.SMEM)] * len(scalars)
        + [pl.BlockSpec()] * len(arrays)
        + [pl.BlockSpec(memory_space=pl.ANY)] * len(anywhere),
        out_specs=[pl.BlockSpec(memory_space=out_space) if out_space else pl.BlockSpec()] * len(out_shape),
        out_shape=out_shape,
        scratch_shapes=list(scratch),
        compiler_params=pltpu.CompilerParams(vmem_limit_bytes=limit * 2**20),
        cost_estimate=pl.CostEstimate(flops=flops, bytes_accessed=2**22, transcendentals=0),
    )(*scalars, *arrays, *anywhere)


SMALL_ROWS = 16


def split_kernel(place_ref, gain_1_ref, gain_2_ref, router_ref, ids_ref, wq_ref, wk_ref, wv_ref, wo_ref, mine, theirs, out_mine):
    half = D // 2
    experts, rows = router_ref.shape
    ids = ids_ref[...]
    expert = lax.broadcasted_iota(jnp.int32, (experts, TOK_DEV), 0)
    chosen = jnp.zeros((experts, TOK_DEV), f32)
    for k in range(ids.shape[0]):
        chosen = jnp.where(expert == ids[k : k + 1], 1.0, chosen)
    mine[rows:] = jnp.zeros((SMALL_ROWS, WIDE), bf16)
    mine[rows : rows + 1, :rows] = gain_1_ref[...]
    mine[rows + 1 : rows + 2, :rows] = gain_2_ref[...]
    for t in range(experts // SMALL_ROWS):
        part = slice(t * SMALL_ROWS, (t + 1) * SMALL_ROWS)
        at = (1 + t) * LANES
        mine[rows:, at : at + rows] = router_ref[part]
        at = (1 + t + experts // SMALL_ROWS) * LANES
        mine[rows:, at : at + LANES] = chosen[part].astype(bf16)
    for core in range(2):

        @pl.when(place_ref[1] == core)
        def _(core=core):
            cols = [wq_ref[:, core * QC : (core + 1) * QC]]
            cols += [ref[:, core * KC : (core + 1) * KC] for ref in (wk_ref, wv_ref)]
            cols = jnp.concatenate(cols, 1)
            first_x = place_ref[2] // 2 % 2 == 0
            low, high = cols[:, :ALONE].astype(f32), cols[:, ALONE + SHARED :].astype(f32)
            mine[:rows, :ALONE] = jnp.where(first_x, low, high).astype(bf16)
            mine[:rows, ALONE:] = cols[:, ALONE : ALONE + SHARED]
            theirs[...] = jnp.where(first_x, high, low).astype(bf16)
            out_mine[...] = wo_ref[:, core * half : (core + 1) * half]


def put_lanes(ref, piece, owner, rows):
    start = owner * rows
    at = pl.ds(pl.multiple_of(start // LANES * LANES, LANES), LANES)
    if rows < LANES:
        off = start % LANES
        lane = lane_index(piece.shape)
        piece = pltpu.roll(piece, off, 1)
        piece = jnp.where((lane >= off) & (lane < off + rows), piece, ref[:, at])
    ref[:, at] = piece


def fetch(n, rows, owner_ref, pairs, sems):
    copies = []
    for blocks, target in pairs:
        for k in range(n):
            at = pl.ds(pl.multiple_of(owner_ref[k] * rows, rows), rows)
            copies.append(pltpu.make_async_copy(blocks[k].at[pl.ds(0, rows)], target.at[at], sems.at[len(copies)]))
    for copy in copies:
        copy.start()
    return copies


def attention_kernel(n, rows, place_ref, owner_ref, own_ref, other_ref, cos_ref, sin_ref, *refs):
    blocks, theirs = refs[:n], refs[n : n + n // 2 + 1]
    w_ref, small_ref, gain_ref, normed_ref, inv_ref, q_ref, k_ref, v_ref, lse_ref, att_ref, window, sems = refs[n + n // 2 + 1 :]
    first_x = place_ref[2] // 2 % 2 == 0
    ours_at = pl.ds(pl.multiple_of(jnp.where(first_x, 0, ALONE + SHARED), LANES), ALONE)
    theirs_at = pl.ds(pl.multiple_of(jnp.where(first_x, ALONE + SHARED, 0), LANES), ALONE)
    other_x = [theirs[0], theirs[n // 2]]
    for k in range(1, n // 2):
        other_x += [theirs[k].at[pl.ds(0, rows)], theirs[k].at[pl.ds(rows, rows)]]
    copies = []
    for k in range(n):
        source = blocks[k].at[pl.ds(rows, SMALL_ROWS)]
        copies.append(pltpu.make_async_copy(source, small_ref.at[k], sems.at[k]))
    for k in range(n):
        at = pl.ds(pl.multiple_of(owner_ref[k] * rows, rows), rows)
        block = blocks[k].at[pl.ds(0, rows)]
        for source, target in (
            (block.at[:, pl.ds(0, ALONE)], w_ref.at[at, ours_at]),
            (block.at[:, pl.ds(ALONE, SHARED)], w_ref.at[at, pl.ds(ALONE, SHARED)]),
            (other_x[k], w_ref.at[at, theirs_at]),
        ):
            copies.append(pltpu.make_async_copy(source, target, sems.at[len(copies)]))
    for copy in copies:
        copy.start()
    packets = (own_ref, other_ref)
    scaled = []
    for g, packet in enumerate(packets):
        values = packet[:HALO].astype(f32)
        inv = inverse_rms(values)
        inv_ref[g * TOK_DEV : (g + 1) * TOK_DEV] = inv[:TOK_DEV]
        scaled.append(values * inv)
    for k in range(n):
        copies[k].wait()
    for k in range(n):
        put_lanes(gain_ref, small_ref[k, :1, :LANES].astype(f32), owner_ref[k], rows)
    gain = gain_ref[...]
    for g in range(2):
        base = 2 * TOK_DEV * g
        normed = (scaled[g] * gain).astype(bf16)
        window[base : base + HALF] = jnp.zeros((HALF, D), bf16)
        window[base + HALF : base + TOK_DEV] = normed[TOK_DEV:]
        window[base + TOK_DEV : base + 2 * TOK_DEV] = normed[:TOK_DEV]
        normed_ref[g * TOK_DEV : (g + 1) * TOK_DEV] = normed[:TOK_DEV]
    for copy in copies[n:]:
        copy.wait()
    q_both = dot(normed_ref[...], w_ref[:, :QC])
    kv_both = dot(window[...], w_ref[:, QC:])
    cos, sin = cos_ref[...], sin_ref[...]
    lane = lane_index((TOK_DEV, LANES))
    for g in range(2):
        tok = slice(g * TOK_DEV, (g + 1) * TOK_DEV)
        win = slice(2 * g * TOK_DEV, 2 * (g + 1) * TOK_DEV)
        q_lin, kv_lin = q_both[tok], kv_both[win]
        allowed = allowed_pairs(place_ref[0], packets[g])
        v_ref[win] = kv_lin[:, KC:].astype(bf16)
        lse = jnp.zeros((TOK_DEV, LANES), f32)
        for pair in range(KC // LANES):
            cols = slice(pair * LANES, (pair + 1) * LANES)
            keys = rotate(kv_lin[:, cols], cos, sin)
            k_ref[win, cols] = keys.astype(bf16)
            key_sides = apart(keys)
            value_sides = apart(kv_lin[:, KC + pair * LANES : KC + (pair + 1) * LANES])
            for one in range(2):
                head = 2 * pair + one
                q_cols = slice(head * LANES, (head + 1) * LANES)
                queries = rotate(q_lin[:, q_cols], cos[TOK_DEV:], sin[TOK_DEV:]).astype(bf16)
                q_ref[tok, q_cols] = queries
                out = 0.0
                for side in range(2):
                    scores = dot_t(queries, key_sides[one][side]) * SCORE_SCALE
                    scores = jnp.where(allowed, scores, NEG_LARGE)
                    highest = jnp.max(scores, -1, keepdims=True)
                    raised = jnp.exp(scores - highest)
                    log_total = highest + jnp.log(jnp.sum(raised, -1, keepdims=True))
                    lse = jnp.where(lane == 2 * head + side, log_total, lse)
                    probs = jnp.exp(scores - log_total).astype(bf16)
                    out = out + dot(probs, value_sides[one][side])
                att_ref[tok, q_cols] = out.astype(bf16)
        lse_ref[tok] = lse


def both_halves(place_ref, mine, got):
    first_core = place_ref[1] == 0
    mine, got = mine.astype(f32), got.astype(f32)
    return jnp.concatenate([jnp.where(first_core, mine, got), jnp.where(first_core, got, mine)], 1)


def output_kernel(n, rows, place_ref, owner_ref, att_ref, got_ref, *refs):
    blocks, (w_ref, both_ref, own_ref, send_ref, sems) = refs[:n], refs[n:]
    copies = fetch(n, rows, owner_ref, ((blocks, w_ref),), sems)
    own, other = slice(0, TOK_DEV), slice(TOK_DEV, 2 * TOK_DEV)
    both_ref[own] = both_halves(place_ref, att_ref[own], got_ref[other]).astype(bf16)
    both_ref[other] = both_halves(place_ref, att_ref[other], got_ref[own]).astype(bf16)
    for copy in copies:
        copy.wait()
    proj = dot(both_ref[...], w_ref[...])
    own_ref[...] = proj[own]
    send_ref[...] = proj[other]


def hidden_kernel(n, rows, experts, place_ref, owner_ref, own_ref, got_ref, tok_ref, small_ref, gain_ref, router_ref, chosen_ref, hidden_ref, inv_ref, ffn_ref, router):
    for k in range(n):
        tiles = [small_ref[k, :, i * LANES : (i + 1) * LANES].astype(f32) for i in range(1 + 2 * experts // SMALL_ROWS)]
        put_lanes(gain_ref, tiles[0][1:2], owner_ref[k], rows)
        put_lanes(router, jnp.concatenate(tiles[1 : 1 + experts // SMALL_ROWS], 0), owner_ref[k], rows)
        chosen = jnp.concatenate(tiles[1 + experts // SMALL_ROWS :], 0)
        chosen = jnp.concatenate([chosen, jnp.zeros((LANES - experts, LANES), f32)], 0).T
        chosen_ref[k * TOK_DEV : (k + 1) * TOK_DEV] = chosen[:, :experts]
    router_ref[...] = router[...].astype(bf16)
    hidden = tok_ref[...].astype(f32) + RESIDUAL_SCALE * both_halves(place_ref, own_ref[...], got_ref[...])
    hidden_ref[...] = hidden
    inv = inverse_rms(hidden)
    inv_ref[...] = inv
    ffn_ref[...] = (hidden * inv * gain_ref[...]).astype(bf16)


def block_lanes(ref, row, owner, rows):
    start = owner * rows
    piece = ref[row : row + 1, pl.ds(pl.multiple_of(start // LANES * LANES, LANES), LANES)]
    if rows < LANES:
        piece = pltpu.roll(piece, (LANES - start % LANES) % LANES, 1)
    return piece


def hidden_grad_kernel(experts, back0_ref, back1_ref, back2_ref, gates_ref, ffn_ref, hidden_ref, inv_ref, gain_ref, router_ref, up_ref, branch_ref, small_ref):
    back = back0_ref[...].astype(f32) + back1_ref[...].astype(f32) + back2_ref[...].astype(f32)
    gate_grad = back[:, D : D + experts] + back[:, D + experts : D + 2 * experts]
    gates = gates_ref[...]
    logit_grad = (gates * (gate_grad - jnp.sum(gates * gate_grad, -1, keepdims=True))).astype(bf16)
    hidden, inv, gain = hidden_ref[...], inv_ref[...], gain_ref[...]
    grad = back[:, :D] + dot(logit_grad, router_ref[...])
    scaled = grad * gain
    through = inv * scaled - hidden * (inv * inv * inv) * jnp.mean(scaled * hidden, -1, keepdims=True)
    hidden_grad = up_ref[...].astype(f32) + through
    branch_ref[...] = (RESIDUAL_SCALE * hidden_grad).astype(bf16)
    small_ref[:experts] = t_dot(logit_grad, ffn_ref[...])
    small_ref[experts : experts + 1] = jnp.sum(grad * hidden * inv, 0, keepdims=True)


def output_grad_kernel(place_ref, own_ref, got_ref, w_ref, keep_ref, send_ref, cols_ref):
    half = D // 2
    first_core = place_ref[1] == 0
    both = jnp.concatenate([own_ref[...], got_ref[...]], 0).astype(f32)
    cols = jnp.where(first_core, both[:, :half], both[:, half:]).astype(bf16)
    cols_ref[...] = cols
    grad = dot_t(cols, w_ref[...])
    keep_ref[...] = jnp.where(first_core, grad[:, :QC], grad[:, QC:])
    send_ref[...] = jnp.where(first_core, grad[:, QC:], grad[:, :QC]).astype(bf16)


def output_weight_grad_kernel(n, rows, small_count, owner_ref, both_ref, cols_ref, small_ref, *refs):
    blocks, grads = refs[:n], refs[n]
    grads[...] = t_dot(both_ref[...], cols_ref[...])
    packed = grads.shape[1] // LANES
    for k in range(n):
        at = pl.ds(pl.multiple_of(owner_ref[k] * rows, rows), rows)
        blocks[k][:rows] = grads[at, :].astype(bf16)
        blocks[k][rows:] = jnp.zeros((blocks[k].shape[0] - rows, grads.shape[1]), bf16)
        for i in range(small_count):
            piece = block_lanes(small_ref, i, owner_ref[k], rows)
            lane = i % packed * LANES
            blocks[k][rows + i // packed : rows + i // packed + 1, lane : lane + LANES] = piece.astype(bf16)


def attention_grad_kernel(place_ref, own_ref, other_ref, q_ref, k_ref, v_ref, lse_ref, att_ref, ag_ref, ag_got_ref, cos_ref, sin_ref, q_pre_ref, kv_own_ref, kv_before_ref):
    cos, sin = cos_ref[...], sin_ref[...]
    low = lane_index((TOK_DEV, LANES)) < HEAD_DIM
    for g, packet_ref in enumerate((own_ref, other_ref)):
        tok = slice(g * TOK_DEV, (g + 1) * TOK_DEV)
        there = slice((1 - g) * TOK_DEV, (2 - g) * TOK_DEV)
        win = slice(2 * g * TOK_DEV, 2 * (g + 1) * TOK_DEV)
        halo = slice(g * HALF, (g + 1) * HALF)
        allowed = allowed_pairs(place_ref[0], packet_ref)
        for pair in range(KC // LANES):
            cols = slice(pair * LANES, (pair + 1) * LANES)
            key_sides, value_sides = apart(k_ref[win, cols]), apart(v_ref[win, cols])
            key_grad = jnp.zeros((2 * TOK_DEV, LANES), f32)
            value_grad = jnp.zeros((2 * TOK_DEV, LANES), f32)
            for one in range(2):
                head = 2 * pair + one
                q_cols = slice(head * LANES, (head + 1) * LANES)
                queries = q_ref[tok, q_cols]
                grads = (ag_ref[tok, q_cols] + ag_got_ref[there, q_cols].astype(f32)).astype(bf16)
                query_sides, grad_sides = apart(queries), apart(grads)
                product = grads.astype(f32) * att_ref[tok, q_cols].astype(f32)
                query_grad = jnp.zeros((TOK_DEV, LANES), f32)
                for side in range(2):
                    k_side, v_side = key_sides[one][side], value_sides[one][side]
                    log_total = lse_ref[tok, 2 * head + side : 2 * head + side + 1]
                    delta = jnp.sum(jnp.where(low == (side == 0), product, 0.0), -1, keepdims=True)
                    scores = dot_t(queries, k_side) * SCORE_SCALE
                    probs = jnp.where(allowed, jnp.exp(scores - log_total), 0.0)
                    prob_grad = dot_t(grads, v_side)
                    score_grad = (probs * (prob_grad - delta) * SCORE_SCALE).astype(bf16)
                    query_grad = query_grad + dot(score_grad, k_side)
                    key_grad = key_grad + t_dot(score_grad, query_sides[side][one])
                    value_grad = value_grad + t_dot(probs.astype(bf16), grad_sides[side][one])
                q_pre_ref[tok, q_cols] = rotate_back(query_grad, cos[TOK_DEV:], sin[TOK_DEV:]).astype(bf16)
            v_cols = slice(KC + pair * LANES, KC + (pair + 1) * LANES)
            key_grad = rotate_back(key_grad, cos, sin)
            kv_own_ref[tok, cols] = key_grad[TOK_DEV:]
            kv_own_ref[tok, v_cols] = value_grad[TOK_DEV:]
            kv_before_ref[halo, cols] = key_grad[HALF:TOK_DEV].astype(bf16)
            kv_before_ref[halo, v_cols] = value_grad[HALF:TOK_DEV].astype(bf16)


def projection_grad_kernel(n, rows, owner_ref, q_pre_ref, kv_own_ref, later_ref, normed_ref, w_ref, own_ref, other_ref, inv_ref, *refs):
    blocks, (aig_own_ref, aig_send_ref, grads, gain_grad) = refs[:n], refs[n:]
    kv, later = kv_own_ref[...], later_ref[...].astype(f32)
    parts = []
    for g in range(2):
        at = g * TOK_DEV
        parts += [kv[at : at + HALF], kv[at + HALF : at + TOK_DEV] + later[g * HALF : (g + 1) * HALF]]
    pre = jnp.concatenate([q_pre_ref[...], jnp.concatenate(parts, 0).astype(bf16)], 1)
    grads[...] = t_dot(normed_ref[...], pre)
    aig = dot_t(pre, w_ref[...])
    values = jnp.concatenate([own_ref[:TOK_DEV], other_ref[:TOK_DEV]], 0).astype(f32)
    gain_grad[...] = jnp.sum(aig * values * inv_ref[...], 0, keepdims=True)
    for k in range(n):
        at = pl.ds(pl.multiple_of(owner_ref[k] * rows, rows), rows)
        blocks[k][:rows] = grads[at, :].astype(bf16)
        blocks[k][rows:] = jnp.zeros((blocks[k].shape[0] - rows, D), bf16)
        blocks[k][rows : rows + 1, :LANES] = block_lanes(gain_grad, 0, owner_ref[k], rows).astype(bf16)
    aig_own_ref[...] = aig[:TOK_DEV]
    aig_send_ref[...] = aig[TOK_DEV:]


def input_grad_kernel(aig_ref, got_ref, own_ref, inv_ref, gain_ref, up_ref, out_ref):
    grad = aig_ref[...] + got_ref[...]
    values, inv = own_ref[:TOK_DEV].astype(f32), inv_ref[:TOK_DEV]
    scaled = grad * gain_ref[...]
    through = inv * scaled - values * (inv * inv * inv) * jnp.mean(scaled * values, -1, keepdims=True)
    out_ref[...] = (up_ref[...].astype(f32) + through).astype(bf16)


def assemble_kernel(experts, place_ref, in_own, in_got, out_own, out_got, wq_ref, wk_ref, wv_ref, wo_ref, gain_1_ref, gain_2_ref, router_ref):
    rows = wq_ref.shape[0]
    half = D // 2
    for core, first, second, low, high in ((0, in_own, in_got, out_own, out_got), (1, in_got, in_own, out_got, out_own)):

        @pl.when(place_ref[1] == core)
        def _(sides=((first, low), (second, high))):
            for c, (into, out) in enumerate(sides):
                wq_ref[:, c * QC : (c + 1) * QC] = into[:rows, :QC]
                wk_ref[:, c * KC : (c + 1) * KC] = into[:rows, QC : QC + KC]
                wv_ref[:, c * KC : (c + 1) * KC] = into[:rows, QC + KC :]
                wo_ref[:, c * half : (c + 1) * half] = out[:rows]

    gain_1_ref[...] = in_own[rows : rows + 1, :rows] + in_got[rows : rows + 1, :rows]
    small = out_own[rows:] + out_got[rows:]
    packed = half // LANES
    for i in range(experts + 1):
        piece = small[i // packed : i // packed + 1, i % packed * LANES : i % packed * LANES + rows]
        if i < experts:
            router_ref[i : i + 1] = piece
        else:
            gain_2_ref[...] = piece


def expert_kernel(size, count, experts, shard_ref, *refs):
    x_refs, up_refs = refs[:count], refs[count : 2 * count]
    chosen_ref, router_ref, wg_ref, wu_ref, wd_ref = refs[2 * count : 2 * count + 5]
    refs = refs[-(2 * count + 6 + 3) :]
    back_refs, mix_refs = refs[:count], refs[count : 2 * count]
    gates_ref, all_x, all_act, all_row, all_gate, all_up = refs[2 * count : 2 * count + 6]
    back_acc, mix_acc, cols_acc = refs[-3:]
    e = pl.program_id(0)
    rows = size * count
    x = jnp.concatenate([ref[...] for ref in x_refs], 0)
    grad = RESIDUAL_SCALE * jnp.concatenate([ref[...] for ref in up_refs], 0).astype(f32)

    @pl.when(e == 0)
    def _():
        chosen = chosen_ref[...] > 0
        logits = jnp.where(chosen, dot_t(x, router_ref[...]), NEG_LARGE)
        raised = jnp.where(chosen, jnp.exp(logits - jnp.max(logits, -1, keepdims=True)), 0.0)
        gates_ref[...] = raised / jnp.sum(raised, -1, keepdims=True)
        all_x[...] = x

    here = lax.broadcasted_iota(jnp.int32, (rows, experts), 1) == shard_ref[0] * EXP_DEV + e
    gate = jnp.sum(jnp.where(here, gates_ref[...], 0.0), -1, keepdims=True)
    gate_pre = dot(x, wg_ref[0])
    up_pre = dot(x, wu_ref[0])
    gate_sig = 1.0 / (1.0 + jnp.exp(-gate_pre))
    silu = gate_pre * gate_sig
    activated = (silu * up_pre).astype(bf16)
    all_act[0] = activated
    expert_out = dot(activated, wd_ref[0]).astype(bf16).astype(f32)
    mix = gate * expert_out
    cols = jnp.where(here, jnp.sum(grad * expert_out, -1, keepdims=True), 0.0)
    row_grad = (gate * grad).astype(bf16)
    all_row[0] = row_grad
    unit = dot_t(row_grad, wd_ref[0])
    gate_grad = (unit * up_pre * gate_sig * (1.0 + gate_pre * (1.0 - gate_sig))).astype(bf16)
    up_grad = (unit * silu).astype(bf16)
    all_gate[0] = gate_grad
    all_up[0] = up_grad
    back = dot_t(gate_grad, wg_ref[0]) + dot_t(up_grad, wu_ref[0])

    @pl.when(e == 0)
    def _():
        back_acc[...] = back
        mix_acc[...] = mix
        cols_acc[...] = cols

    @pl.when(e == EXP_DEV - 1)
    def _():
        whole_back = (back_acc[...] + back).astype(bf16)
        whole_mix = (mix_acc[...] + mix).astype(bf16)
        whole_cols = cols_acc[...] + cols
        high = whole_cols.astype(bf16)
        low = (whole_cols - high.astype(f32)).astype(bf16)
        for k in range(count):
            part = slice(k * size, (k + 1) * size)
            back_refs[k][:, :D] = whole_back[part]
            back_refs[k][:, D:] = jnp.zeros((size, LANES), bf16)
            back_refs[k][:, D : D + experts] = high[part]
            back_refs[k][:, D + experts : D + 2 * experts] = low[part]
            mix_refs[k][...] = whole_mix[part]


def expert_weight_kernel(replicas, place_ref, x_ref, act_ref, row_ref, gate_ref, up_ref, keep_ref, send_ref, wide, tall):
    x = x_ref[...]
    for kind, grads in enumerate((gate_ref, up_ref)):
        tall[...] = t_dot(x, grads[0])
        own = tall.shape[0] // replicas
        for j in range(replicas // 2):
            for target, core in ((keep_ref, place_ref[1]), (send_ref, 1 - place_ref[1])):
                at = pl.ds(pl.multiple_of((2 * j + core) * own, own), own)
                target[kind, j] = tall[at, :].astype(bf16)
    wide[...] = t_dot(act_ref[0], row_ref[0])
    own = wide.shape[0] // replicas
    half = wide.shape[1] // 2
    for j in range(replicas // 2):
        for target, core in ((keep_ref, place_ref[1]), (send_ref, 1 - place_ref[1])):
            at = pl.ds(pl.multiple_of((2 * j + core) * own, own), own)
            target[2, j, :own] = wide[at, :half].astype(bf16)
            target[2, j, own:] = wide[at, half:].astype(bf16)


def expert_weight_grads(replicas, place, held, e):
    group_in, act, row, gate, up = held
    ff = act.shape[2]
    own = D // replicas
    shape = (3, replicas // 2, own, ff)

    def one(width):
        return pl.BlockSpec((1, group_in.shape[0], width), lambda i: (e, 0, 0))

    return pl.pallas_call(
        functools.partial(expert_weight_kernel, replicas),
        grid=(1,),
        in_specs=[
            pl.BlockSpec(memory_space=pltpu.SMEM),
            pl.BlockSpec(group_in.shape, lambda i: (0, 0)),
            one(ff),
            one(D),
            one(ff),
            one(ff),
        ],
        out_specs=[pl.BlockSpec(shape, lambda i: (0, 0, 0, 0))] * 2,
        out_shape=[jax.ShapeDtypeStruct(shape, bf16)] * 2,
        scratch_shapes=[pltpu.VMEM((ff, D), f32), pltpu.VMEM((D, ff), f32)],
        compiler_params=pltpu.CompilerParams(vmem_limit_bytes=32 * 2**20),
        cost_estimate=pl.CostEstimate(flops=2**32, bytes_accessed=2**23, transcendentals=0),
    )(place, group_in, act, row, gate, up)


def expert_sum_kernel(*refs):
    keeps, gots, (gate_ref, up_ref, down_ref) = refs[:EXP_DEV], refs[EXP_DEV : 2 * EXP_DEV], refs[2 * EXP_DEV :]
    own = down_ref.shape[1]
    for e in range(EXP_DEV):
        total = [keeps[e][kind].astype(f32) + gots[e][kind].astype(f32) for kind in range(3)]
        gate_ref[e] = total[0]
        up_ref[e] = total[1]
        down_ref[e, :, : total[2].shape[1]] = total[2][:own]
        down_ref[e, :, total[2].shape[1] :] = total[2][own:]


def replica_split_kernel(place_ref, keep_ref, got_ref, stay_ref, send_ref):
    here = place_ref[2] // 2 % 2
    for kind in range(3):
        for j in range(stay_ref.shape[1]):
            for target, at in ((stay_ref, 2 * j + here), (send_ref, 2 * j + 1 - here)):
                target[kind, j] = (keep_ref[kind, at].astype(f32) + got_ref[kind, at].astype(f32)).astype(bf16)


def run_experts(block, count, total, shard, x, up, chosen, router, w_gate, w_up, w_down, held):
    rows = TOK_DEV * count
    experts = chosen.shape[1]
    ff = w_gate.shape[2]
    at = block // count

    def whole(shape):
        return pl.BlockSpec(shape, lambda e: (0,) * len(shape))

    def one(shape):
        return pl.BlockSpec((1,) + shape, lambda e: (e,) + (0,) * len(shape))

    def filled(width):
        return pl.BlockSpec((1, rows, width), lambda e: (e, at, 0))

    every = TOK_DEV * total
    out_shape = (
        [jax.ShapeDtypeStruct((TOK_DEV, D + LANES), bf16)] * count
        + [jax.ShapeDtypeStruct((TOK_DEV, D), bf16)] * count
        + [jax.ShapeDtypeStruct((rows, experts), f32)]
    )
    held_shape = [
        jax.ShapeDtypeStruct((every, D), bf16),
        jax.ShapeDtypeStruct((EXP_DEV, every, ff), bf16),
        jax.ShapeDtypeStruct((EXP_DEV, every, D), bf16),
        jax.ShapeDtypeStruct((EXP_DEV, every, ff), bf16),
        jax.ShapeDtypeStruct((EXP_DEV, every, ff), bf16),
    ]
    out_specs = (
        [whole((TOK_DEV, D + LANES))] * count
        + [whole((TOK_DEV, D))] * count
        + [whole((rows, experts))]
        + [pl.BlockSpec((rows, D), lambda e: (at, 0))]
        + [filled(ff), filled(D), filled(ff), filled(ff)]
    )
    in_specs = [
        pl.BlockSpec(memory_space=pltpu.SMEM),
        *[whole((TOK_DEV, D))] * (2 * count),
        pl.BlockSpec((rows, experts), lambda e: (at, 0)),
        whole(router.shape),
        one(w_gate.shape[1:]),
        one(w_up.shape[1:]),
        one(w_down.shape[1:]),
    ]
    args = [shard, *x, *up, chosen, router, w_gate, w_up, w_down]
    aliases = {}
    if held is not None:
        aliases = {len(args) + k: len(out_shape) + k for k in range(len(held))}
        in_specs = in_specs + [pl.BlockSpec(memory_space=pl.ANY)] * len(held)
        args = args + list(held)
    flops = 12 * rows * D * ff * EXP_DEV
    outs = pl.pallas_call(
        functools.partial(expert_kernel, TOK_DEV, count, experts),
        grid=(EXP_DEV,),
        in_specs=in_specs,
        out_specs=out_specs,
        out_shape=out_shape + held_shape,
        scratch_shapes=[
            pltpu.VMEM((rows, D), f32),
            pltpu.VMEM((rows, D), f32),
            pltpu.VMEM((rows, experts), f32),
        ],
        input_output_aliases=aliases,
        compiler_params=pltpu.CompilerParams(vmem_limit_bytes=24 * 2**20),
        cost_estimate=pl.CostEstimate(
            flops=flops, bytes_accessed=6 * D * ff * EXP_DEV + 16 * rows * D, transcendentals=rows * ff * EXP_DEV
        ),
    )(*args)
    return outs[:count], outs[count : 2 * count], outs[2 * count], outs[2 * count + 1 :]


def per_device(
    tokens,
    segment_ids,
    expert_ids,
    attn_gain,
    w_query,
    w_key,
    w_value,
    w_output,
    ffn_gain,
    w_router,
    w_gate,
    w_up,
    w_down,
    out_grad,
):
    shard = lax.axis_index("shard")
    core = lax.axis_index("rep") % 2
    ring = Ring()
    n = ring.n
    experts = EXP_DEV * n
    rows = w_query.shape[0]
    half_width = D // 2

    replicas = lax.axis_size("rep")
    place = jnp.stack([shard, core, lax.axis_index("rep")]).astype(jnp.int32)
    owners = ring.row
    cos, sin = rotary_tables()
    shift_up = [(i, i + 1) for i in range(n - 1)]
    shift_down = [(i + 1, i) for i in range(n - 1)]

    in_own, in_theirs, out_own = call(
        split_kernel,
        [vmem((rows + SMALL_ROWS, WIDE), bf16), vmem((rows, ALONE), bf16), vmem((rows, half_width), bf16)],
        [place],
        [attn_gain[None], ffn_gain[None], w_router.T, expert_ids[0].T, w_query, w_key, w_value, w_output],
        limit=60,
    )
    in_ring, theirs = Gather(ring, in_own), [in_theirs]

    def cross_in():
        if len(theirs) > 2:
            in_ring.got, theirs[-2] = together(in_ring.got, theirs[-2])
        theirs.append(swap(jnp.concatenate([in_ring.got[o][:rows, :ALONE] for o in in_ring.new], axis=0), 2))

    in_ring.step()
    cross_in()
    seg_row = jnp.pad(segment_ids.astype(bf16), ((0, SEG_ROWS - 1), (0, D - TOK_DEV)))
    before = jnp.concatenate([tokens[0, HALF:], seg_row], axis=0)
    before = lax.ppermute(after(before, in_ring.got[-1]), "shard", shift_up)
    packet = jnp.concatenate([tokens[0], before, seg_row], axis=0)
    in_ring.step()
    cross_in()
    packet_other = swap(after(packet, in_ring.got[-2]), 1)
    while in_ring.left > 1:
        in_ring.step()
        cross_in()
    out_ring = Gather(ring, after(out_own, in_ring.got[-in_ring.done[-1]]), flip=True)
    in_ring.step()
    cross_in()
    out_ring.hop(1)
    out_ring.got, up_own = after((out_ring.got, out_grad[0]), *in_ring.blocks())
    up = Gather(ring, up_own)
    out_ring.step()
    up.step()
    in_w, small, first_gain, normed, inv_first, queries, keys, values, log_total, att = call(
        functools.partial(attention_kernel, n, rows),
        [
            vmem((D, D), bf16),
            vmem((n, SMALL_ROWS, WIDE), bf16),
            vmem((1, D), f32),
            vmem((2 * TOK_DEV, D), bf16),
            vmem((2 * TOK_DEV, 1), f32),
            vmem((2 * TOK_DEV, QC), bf16),
            vmem((4 * TOK_DEV, KC), bf16),
            vmem((4 * TOK_DEV, KC), bf16),
            vmem((2 * TOK_DEV, LANES), f32),
            vmem((2 * TOK_DEV, QC), bf16),
        ],
        [place, owners],
        [packet, packet_other, cos, sin],
        [pltpu.VMEM((4 * TOK_DEV, D), bf16), pltpu.SemaphoreType.DMA((4 * n,))],
        flops=2**32,
        anywhere=[*in_ring.blocks(), *theirs],
    )
    out_ring.got, up.got, att = together(out_ring.got, up.got, att)
    att_got = swap(att, 1)
    out_ring.step()
    up.step()
    while out_ring.left:
        out_ring.step()
    out_blocks, att_got, up.got = together(out_ring.blocks(), att_got, up.got)
    out_w, attended, proj, proj_send = call(
        functools.partial(output_kernel, n, rows),
        [
            vmem((QW, half_width), bf16),
            vmem((2 * TOK_DEV, QW), bf16),
            vmem((TOK_DEV, half_width), f32),
            vmem((TOK_DEV, half_width), f32),
        ],
        [place, owners],
        [att, att_got],
        [pltpu.SemaphoreType.DMA((n,))],
        flops=2**30,
        anywhere=out_blocks,
    )
    second_gain, router, group_chosen, hidden, inv_second, ffn_inputs = call(
        functools.partial(hidden_kernel, n, rows, experts),
        [
            vmem((1, D), f32),
            vmem((experts, D), bf16),
            vmem((n * TOK_DEV, experts), f32),
            vmem((TOK_DEV, D), f32),
            vmem((TOK_DEV, 1), f32),
            vmem((TOK_DEV, D), bf16),
        ],
        [place, owners],
        [proj, swap(proj_send, 1), tokens[0], small],
        [pltpu.VMEM((experts, D), f32)],
        flops=2**28,
    )


    group = Gather(ring, ffn_inputs)
    while group.left:
        group.step()
        if up.left:
            up.step()
    held = None
    back_parts = [None] * n
    own_gates = None
    mix_parts = [None] * n
    runs = [(0, 1)] + [(k, 2) for k in range(2, n, 2)] + [(1, 1)]
    for block, count in runs:
        part = slice(block, block + count)
        backs, mixes, gates, held = run_experts(
            block,
            count,
            n,
            place[:1],
            [group.got[o] for o in ring.offsets[part]],
            [up.got[o] for o in ring.offsets[part]],
            group_chosen,
            router,
            w_gate,
            w_up,
            w_down,
            held,
        )
        back_parts[part] = backs
        mix_parts[part] = mixes
        own_gates = gates if block == 0 else own_gates

    back, mix = Scatter(ring, back_parts), Scatter(ring, mix_parts, flip=True)
    stays, crossing, made = [], [], []
    while back.left:
        if back.left == 1:
            back.got = after(back.got, made)
            mix.sums = after(mix.sums, back.got)
            mix.hop(1)
        back.step()
        if len(stays) < EXP_DEV:
            held = after(held, back.got)
            keep, send = expert_weight_grads(replicas, place, held, len(stays))
            made.append(send)
            stay, send = call(
                replica_split_kernel,
                [vmem((3, replicas // 4, *keep.shape[2:]), bf16)] * 2,
                [place],
                [keep, swap(send, 1)],
            )
            stays.append(stay)
            crossing.append(send)
    own_gates, crossing[0] = together(own_gates, crossing[0])
    crossing[0] = swap(crossing[0], 2)

    branch, out_small = call(
        functools.partial(hidden_grad_kernel, experts),
        [vmem((TOK_DEV, D), bf16), vmem((experts + 1, D), f32)],
        [],
        [
            *back.terms(),
            own_gates,
            ffn_inputs,
            hidden,
            inv_second,
            second_gain,
            router,
            out_grad[0],
        ],
        flops=2**28,
    )
    ag_keep, ag_send, branch_cols = call(
        output_grad_kernel,
        [
            vmem((2 * TOK_DEV, QC), f32),
            vmem((2 * TOK_DEV, QC), bf16),
            vmem((2 * TOK_DEV, half_width), bf16),
        ],
        [place],
        [branch, swap(branch, 1), out_w],
        flops=2**29,
    )
    mix.got, mix.sums = after((mix.got, mix.sums), *back.terms())
    mix.step()
    ag_got = swap(ag_send, 1)
    extra = -(-(experts + 1) // (8 * (half_width // LANES))) * 8
    out_blocks = call(
        functools.partial(output_weight_grad_kernel, n, rows, experts + 1),
        [vmem((rows + extra, half_width), bf16)] * n,
        [owners],
        [attended, branch_cols, out_small],
        [pltpu.VMEM((QW, half_width), f32)],
        flops=2**29,
    )
    ag_got, out_blocks = together(ag_got, out_blocks)
    q_pre, kv_own, kv_before = call(
        attention_grad_kernel,
        [
            vmem((2 * TOK_DEV, QC), bf16),
            vmem((2 * TOK_DEV, 2 * KC), f32),
            vmem((TOK_DEV, 2 * KC), bf16),
        ],
        [place],
        [packet, packet_other, queries, keys, values, log_total, att, ag_keep, ag_got, cos, sin],
        flops=2**32,
    )
    later = lax.ppermute(kv_before, "shard", shift_down)
    mix.got = after(mix.got, kv_before)
    if mix.left > 1:
        mix.step()
    later, out_blocks = together(later, out_blocks)
    out = Scatter(ring, out_blocks)
    out.step()
    *in_blocks, aig_own, aig_send = call(
        functools.partial(projection_grad_kernel, n, rows),
        [vmem((rows + 8, D), bf16)] * n + [vmem((TOK_DEV, D), f32)] * 2,
        [owners],
        [q_pre, kv_own, later, normed, in_w, packet, packet_other, inv_first],
        [pltpu.VMEM((D, D), f32), pltpu.VMEM((1, D), f32)],
        flops=2**32,
    )
    in_blocks, crossing[0], mix.got = together(in_blocks, crossing[0], mix.got)
    crossing[1] = swap(after(crossing[1], crossing[0]), 2)

    def owned(sums):
        own, ahead, behind = sums.terms()
        return rep_sum(own.astype(f32) + ahead.astype(f32) + behind.astype(f32))

    into = Scatter(ring, in_blocks)
    into.step()
    out.step()
    into.got, out.got = together(into.got, out.got)
    into.step()
    out.step()
    into.got, out.got, crossing[1] = together(into.got, out.got, crossing[1])
    into.step()
    while out.left:
        out.step()
    aig_got = swap(aig_send, 1)
    into.got, out.got, aig_got = together(into.got, out.got, aig_got)
    input_grad = call(
        input_grad_kernel,
        [vmem((TOK_DEV, D), bf16)],
        [],
        [aig_own, aig_got, packet, inv_first, first_gain, out_grad[0]],
    )[0]
    out_sum = owned(out)
    while into.left:
        into.step()
    into.got, out_sum = together(into.got, out_sum)
    out_got = swap(out_sum, 1)
    left = replicas // 4
    for bit in list(bits())[2:]:
        left //= 2
        here = (lax.axis_index("rep") // bit) % 2
        for e in range(EXP_DEV):
            total = (stays[e].astype(f32) + crossing[e].astype(f32)).astype(bf16)
            pairs = total.reshape(3, left, 2, *total.shape[2:])
            stays[e] = lax.dynamic_index_in_dim(pairs, here, 2, False)
            crossing[e] = swap(lax.dynamic_index_in_dim(pairs, 1 - here, 2, False), bit)
    ff, own_rows = w_gate.shape[2], D // replicas
    gate_sum, up_sum, down_sum = call(
        expert_sum_kernel,
        [
            vmem((EXP_DEV, own_rows, ff), f32),
            vmem((EXP_DEV, own_rows, ff), f32),
            vmem((EXP_DEV, ff // replicas, D), f32),
        ],
        [],
        [part[:, 0] for part in stays + crossing],
    )
    mix.got = after(mix.got, into.got)
    while mix.left:
        mix.step()
    moe_sum = sum(term.astype(f32) for term in mix.terms())

    in_sum = owned(into)
    in_got = swap(in_sum, 1)
    g_query, g_key, g_value, g_output, gain_1, gain_2, g_router = call(
        functools.partial(assemble_kernel, experts),
        [
            vmem((rows, QW), f32),
            vmem((rows, KW), f32),
            vmem((rows, KW), f32),
            vmem((rows, D), f32),
            vmem((1, rows), f32),
            vmem((1, rows), f32),
            vmem((experts, rows), f32),
        ],
        [place],
        [in_sum, in_got, out_sum, out_got],
    )
    mixed = (hidden + RESIDUAL_SCALE * moe_sum).astype(bf16)
    return (
        mixed[None],
        input_grad[None],
        gain_1[0],
        g_query,
        g_key,
        g_value,
        g_output,
        gain_2[0],
        g_router.T,
        gate_sum,
        up_sum,
        down_sum,
    )


def solution(mesh):
    return jax.shard_map(
        per_device,
        mesh=mesh,
        in_specs=(
            P("rep", "shard", None),
            P("rep", "shard"),
            P("rep", "shard", None),
            P("shard"),
            P("shard", None),
            P("shard", None),
            P("shard", None),
            P("shard", None),
            P("shard"),
            P("shard", None),
            P("shard", None, None),
            P("shard", None, None),
            P("shard", None, None),
            P("rep", "shard", None),
        ),
        out_specs=(
            P("rep", "shard", None),
            P("rep", "shard", None),
            P("shard"),
            P("shard", None),
            P("shard", None),
            P("shard", None),
            P("shard", None),
            P("shard"),
            P("shard", None),
            P("shard", "rep", None),
            P("shard", "rep", None),
            P("shard", "rep", None),
        ),
        check_vma=False,
    )
```

```python
import functools

import jax
import jax.numpy as jnp
import numpy as np
from jax import lax
from jax.experimental import pallas as pl
from jax.experimental.pallas import tpu as pltpu
from jax.sharding import PartitionSpec as P

D = 1024
HEADS = 16
KV_HEADS = 8
HEAD_DIM = 64
GROUP = HEADS // KV_HEADS
QW = HEADS * HEAD_DIM
KW = KV_HEADS * HEAD_DIM
QC = QW // 2
KC = KW // 2
ALONE = 384
SHARED = D - 2 * ALONE
WIDE = ALONE + SHARED
TOK_DEV = 128
HALF = TOK_DEV // 2
HALO = TOK_DEV + HALF
SEG_ROWS = 16
EXP_DEV = 2
LANES = 128

EPSILON = 1e-06
RESIDUAL_SCALE = 0.22
SCORE_SCALE = 0.015625
ROPE_BASE = 10000.0
NEG_LARGE = -1e30

bf16 = jnp.bfloat16
f32 = jnp.float32


def dot(a, b, contract=((1,), (0,))):
    return lax.dot_general(a, b, (contract, ((), ())), preferred_element_type=f32)


def dot_t(a, b):
    return dot(a, b, ((1,), (1,)))


def t_dot(a, b):
    return dot(a, b, ((0,), (0,)))


def cycle(length):
    rows = 4 if length % 4 == 0 else 1
    cols = length // rows
    if cols == 1:
        return list(range(length))
    order = [z * cols for z in range(rows)]
    for k, z in enumerate(reversed(range(rows))):
        ys = list(range(1, cols))
        order += [z * cols + y for y in (ys if k % 2 == 0 else reversed(ys))]
    return order


class Ring:
    def __init__(self):
        n = self.n = lax.axis_size("shard")
        cyc = self.cyc = cycle(n)
        self.next = [(cyc[i], cyc[(i + 1) % n]) for i in range(n)]
        self.prev = [(b, a) for a, b in self.next]
        self.ahead, self.back = n // 2, (n - 1) // 2
        self.offsets = [0, -self.ahead]
        for s in range(1, self.back + 1):
            self.offsets += [-s, s]
        place = {dev: i for i, dev in enumerate(cyc)}
        table = [[cyc[(place[dev] + o) % n] for o in self.offsets] for dev in range(n)]
        row = lax.dynamic_index_in_dim(jnp.asarray(table, jnp.int32), lax.axis_index("shard"), 0, False)
        self.row = row


class Gather:
    def __init__(self, ring, block, flip=False):
        self.ring, self.got, self.flip = ring, {0: block}, flip
        self.pairs = {-1: ring.next, 1: ring.prev}
        self.steps = {-1: ring.back, 1: ring.ahead} if flip else {-1: ring.ahead, 1: ring.back}
        self.done = {-1: 0, 1: 0}

    @property
    def left(self):
        return max(self.steps[sign] - self.done[sign] for sign in (-1, 1))

    def hop(self, sign):
        s = self.done[sign] = self.done[sign] + 1
        self.got[sign * s] = lax.ppermute(self.got[sign * (s - 1)], "shard", self.pairs[sign])

    def step(self):
        self.new = []
        for sign in (-1, 1):
            if self.done[sign] < self.steps[sign]:
                self.hop(sign)
                self.new.append(sign * self.done[sign])

    def blocks(self):
        half = self.ring.ahead
        if self.flip:
            self.got[-half] = self.got[half]
        return [self.got[o] for o in self.ring.offsets]


class Scatter:
    def __init__(self, ring, parts, flip=False):
        self.part = dict(zip(ring.offsets, parts))
        self.pairs = {-1: ring.prev, 1: ring.next}
        self.hops = {-1: ring.back, 1: ring.ahead} if flip else {-1: ring.ahead, 1: ring.back}
        if flip:
            self.part[ring.ahead] = self.part[-ring.ahead]
        self.sums = {sign: self.part[sign * steps] for sign, steps in self.hops.items()}
        self.got = {}

    @property
    def left(self):
        return max(self.hops.values())

    def hop(self, sign):
        if sign in self.got:
            part = self.part[sign * self.hops[sign]].astype(f32)
            self.sums[sign] = (self.got[sign].astype(f32) + part).astype(bf16)
        self.got[sign] = lax.ppermute(self.sums[sign], "shard", self.pairs[sign])
        self.hops[sign] -= 1

    def step(self):
        left = self.left
        for sign in (-1, 1):
            if self.hops[sign] == left:
                self.hop(sign)

    def terms(self):
        return self.part[0], self.got[-1], self.got[1]


def after(value, *earlier):
    return lax.optimization_barrier((value, *earlier))[0] if earlier else value


def together(*values):
    return lax.optimization_barrier(values)


def swap(value, bit):
    size = lax.axis_size("rep")
    return lax.ppermute(value, "rep", [(r, r ^ bit) for r in range(size)])


def bits():
    size, bit = lax.axis_size("rep"), 1
    while bit < size:
        yield bit
        bit *= 2


def rep_sum(value):
    for bit in list(bits())[1:]:
        low = lax.reduce_precision(value, 8, 7)
        value = low + swap(low.astype(bf16), bit).astype(f32)
    return value


def rotary_tables():
    positions = (np.arange(2 * TOK_DEV) + HALF) % TOK_DEV
    inverse = ROPE_BASE ** (-2.0 * np.arange(HEAD_DIM // 2) / HEAD_DIM)
    angles = positions[:, None] * inverse[None, :]
    cos, sin = np.cos(angles), np.sin(angles)
    cos, sin = np.concatenate([cos] * 4, axis=1), np.concatenate([-sin, sin] * 2, axis=1)
    return jnp.asarray(cos, f32), jnp.asarray(sin, f32)


def lane_index(shape):
    return lax.broadcasted_iota(jnp.int32, shape, 1)


def rotate(values, cos, sin):
    first = lane_index(values.shape) % HEAD_DIM < HEAD_DIM // 2
    turned = jnp.where(first, pltpu.roll(values, LANES - 32, 1), pltpu.roll(values, 32, 1))
    return values * cos + turned * sin


def rotate_back(values, cos, sin):
    first = lane_index(values.shape) % HEAD_DIM < HEAD_DIM // 2
    moved = values * sin
    turned = jnp.where(first, pltpu.roll(moved, LANES - 32, 1), pltpu.roll(moved, 32, 1))
    return values * cos + turned


def apart(pair):
    pair = pair.astype(f32)
    turned = pltpu.roll(pair, HEAD_DIM, 1)
    low = lane_index(pair.shape) < HEAD_DIM
    zero = jnp.zeros_like(pair)
    return (
        (jnp.where(low, pair, zero).astype(bf16), jnp.where(low, zero, turned).astype(bf16)),
        (jnp.where(low, turned, zero).astype(bf16), jnp.where(low, zero, pair).astype(bf16)),
    )


def allowed_pairs(shard_index, packet_ref):
    seg_before = packet_ref[HALO : HALO + 1, :LANES].astype(f32)
    seg_own = packet_ref[HALO + SEG_ROWS : HALO + SEG_ROWS + 1, :LANES].astype(f32)
    seg_key = jnp.concatenate([seg_before, seg_own], 1)
    seg_query = jnp.broadcast_to(seg_own, (TOK_DEV, TOK_DEV)).T[:, :1]
    shape = (TOK_DEV, 2 * TOK_DEV)
    query = lax.broadcasted_iota(jnp.int32, shape, 0)
    key = lax.broadcasted_iota(jnp.int32, shape, 1) - TOK_DEV
    allowed = (key <= query) & (key >= -HALF) & ((query >= HALF) == (key >= HALF))
    return allowed & ((key >= 0) | (shard_index > 0)) & (seg_query == seg_key)


def inverse_rms(values):
    return lax.rsqrt(jnp.mean(values * values, axis=-1, keepdims=True) + EPSILON)


def vmem(shape, dtype):
    return jax.ShapeDtypeStruct(shape, dtype)


def call(kernel, out_shape, scalars, arrays, scratch=(), flops=0, limit=20, anywhere=(), out_space=None):
    return pl.pallas_call(
        kernel,
        in_specs=[pl.BlockSpec(memory_space=pltpu.SMEM)] * len(scalars)
        + [pl.BlockSpec()] * len(arrays)
        + [pl.BlockSpec(memory_space=pl.ANY)] * len(anywhere),
        out_specs=[pl.BlockSpec(memory_space=out_space) if out_space else pl.BlockSpec()] * len(out_shape),
        out_shape=out_shape,
        scratch_shapes=list(scratch),
        compiler_params=pltpu.CompilerParams(vmem_limit_bytes=limit * 2**20),
        cost_estimate=pl.CostEstimate(flops=flops, bytes_accessed=2**22, transcendentals=0),
    )(*scalars, *arrays, *anywhere)


SMALL_ROWS = 16


def split_kernel(place_ref, gain_1_ref, gain_2_ref, router_ref, ids_ref, wq_ref, wk_ref, wv_ref, wo_ref, mine, theirs, out_mine):
    half = D // 2
    experts, rows = router_ref.shape
    ids = ids_ref[...]
    expert = lax.broadcasted_iota(jnp.int32, (experts, TOK_DEV), 0)
    chosen = jnp.zeros((experts, TOK_DEV), f32)
    for k in range(ids.shape[0]):
        chosen = jnp.where(expert == ids[k : k + 1], 1.0, chosen)
    mine[rows:] = jnp.zeros((SMALL_ROWS, WIDE), bf16)
    mine[rows : rows + 1, :rows] = gain_1_ref[...]
    mine[rows + 1 : rows + 2, :rows] = gain_2_ref[...]
    for t in range(experts // SMALL_ROWS):
        part = slice(t * SMALL_ROWS, (t + 1) * SMALL_ROWS)
        at = (1 + t) * LANES
        mine[rows:, at : at + rows] = router_ref[part]
        at = (1 + t + experts // SMALL_ROWS) * LANES
        mine[rows:, at : at + LANES] = chosen[part].astype(bf16)
    for core in range(2):

        @pl.when(place_ref[1] == core)
        def _(core=core):
            cols = [wq_ref[:, core * QC : (core + 1) * QC]]
            cols += [ref[:, core * KC : (core + 1) * KC] for ref in (wk_ref, wv_ref)]
            cols = jnp.concatenate(cols, 1)
            first_x = place_ref[2] // 2 % 2 == 0
            low, high = cols[:, :ALONE].astype(f32), cols[:, ALONE + SHARED :].astype(f32)
            mine[:rows, :ALONE] = jnp.where(first_x, low, high).astype(bf16)
            mine[:rows, ALONE:] = cols[:, ALONE : ALONE + SHARED]
            theirs[...] = jnp.where(first_x, high, low).astype(bf16)
            out_mine[...] = wo_ref[:, core * half : (core + 1) * half]


def put_lanes(ref, piece, owner, rows):
    start = owner * rows
    at = pl.ds(pl.multiple_of(start // LANES * LANES, LANES), LANES)
    if rows < LANES:
        off = start % LANES
        lane = lane_index(piece.shape)
        piece = pltpu.roll(piece, off, 1)
        piece = jnp.where((lane >= off) & (lane < off + rows), piece, ref[:, at])
    ref[:, at] = piece


def fetch(n, rows, owner_ref, pairs, sems):
    copies = []
    for blocks, target in pairs:
        for k in range(n):
            at = pl.ds(pl.multiple_of(owner_ref[k] * rows, rows), rows)
            copies.append(pltpu.make_async_copy(blocks[k].at[pl.ds(0, rows)], target.at[at], sems.at[len(copies)]))
    for copy in copies:
        copy.start()
    return copies


def attention_kernel(n, rows, place_ref, owner_ref, own_ref, other_ref, cos_ref, sin_ref, *refs):
    blocks, theirs = refs[:n], refs[n : n + n // 2 + 1]
    w_ref, small_ref, gain_ref, normed_ref, inv_ref, q_ref, k_ref, v_ref, lse_ref, att_ref, window, sems = refs[n + n // 2 + 1 :]
    first_x = place_ref[2] // 2 % 2 == 0
    ours_at = pl.ds(pl.multiple_of(jnp.where(first_x, 0, ALONE + SHARED), LANES), ALONE)
    theirs_at = pl.ds(pl.multiple_of(jnp.where(first_x, ALONE + SHARED, 0), LANES), ALONE)
    other_x = [theirs[0], theirs[n // 2]]
    for k in range(1, n // 2):
        other_x += [theirs[k].at[pl.ds(0, rows)], theirs[k].at[pl.ds(rows, rows)]]
    copies = []
    for k in range(n):
        source = blocks[k].at[pl.ds(rows, SMALL_ROWS)]
        copies.append(pltpu.make_async_copy(source, small_ref.at[k], sems.at[k]))
    for k in range(n):
        at = pl.ds(pl.multiple_of(owner_ref[k] * rows, rows), rows)
        block = blocks[k].at[pl.ds(0, rows)]
        for source, target in (
            (block.at[:, pl.ds(0, ALONE)], w_ref.at[at, ours_at]),
            (block.at[:, pl.ds(ALONE, SHARED)], w_ref.at[at, pl.ds(ALONE, SHARED)]),
            (other_x[k], w_ref.at[at, theirs_at]),
        ):
            copies.append(pltpu.make_async_copy(source, target, sems.at[len(copies)]))
    for copy in copies:
        copy.start()
    packets = (own_ref, other_ref)
    scaled = []
    for g, packet in enumerate(packets):
        values = packet[:HALO].astype(f32)
        inv = inverse_rms(values)
        inv_ref[g * TOK_DEV : (g + 1) * TOK_DEV] = inv[:TOK_DEV]
        scaled.append(values * inv)
    for k in range(n):
        copies[k].wait()
    for k in range(n):
        put_lanes(gain_ref, small_ref[k, :1, :LANES].astype(f32), owner_ref[k], rows)
    gain = gain_ref[...]
    for g in range(2):
        base = 2 * TOK_DEV * g
        normed = (scaled[g] * gain).astype(bf16)
        window[base : base + HALF] = jnp.zeros((HALF, D), bf16)
        window[base + HALF : base + TOK_DEV] = normed[TOK_DEV:]
        window[base + TOK_DEV : base + 2 * TOK_DEV] = normed[:TOK_DEV]
        normed_ref[g * TOK_DEV : (g + 1) * TOK_DEV] = normed[:TOK_DEV]
    for copy in copies[n:]:
        copy.wait()
    q_both = dot(normed_ref[...], w_ref[:, :QC])
    kv_both = dot(window[...], w_ref[:, QC:])
    cos, sin = cos_ref[...], sin_ref[...]
    lane = lane_index((TOK_DEV, LANES))
    for g in range(2):
        tok = slice(g * TOK_DEV, (g + 1) * TOK_DEV)
        win = slice(2 * g * TOK_DEV, 2 * (g + 1) * TOK_DEV)
        q_lin, kv_lin = q_both[tok], kv_both[win]
        allowed = allowed_pairs(place_ref[0], packets[g])
        v_ref[win] = kv_lin[:, KC:].astype(bf16)
        lse = jnp.zeros((TOK_DEV, LANES), f32)
        for pair in range(KC // LANES):
            cols = slice(pair * LANES, (pair + 1) * LANES)
            keys = rotate(kv_lin[:, cols], cos, sin)
            k_ref[win, cols] = keys.astype(bf16)
            key_sides = apart(keys)
            value_sides = apart(kv_lin[:, KC + pair * LANES : KC + (pair + 1) * LANES])
            for one in range(2):
                head = 2 * pair + one
                q_cols = slice(head * LANES, (head + 1) * LANES)
                queries = rotate(q_lin[:, q_cols], cos[TOK_DEV:], sin[TOK_DEV:]).astype(bf16)
                q_ref[tok, q_cols] = queries
                out = 0.0
                for side in range(2):
                    scores = dot_t(queries, key_sides[one][side]) * SCORE_SCALE
                    scores = jnp.where(allowed, scores, NEG_LARGE)
                    highest = jnp.max(scores, -1, keepdims=True)
                    raised = jnp.exp(scores - highest)
                    log_total = highest + jnp.log(jnp.sum(raised, -1, keepdims=True))
                    lse = jnp.where(lane == 2 * head + side, log_total, lse)
                    probs = jnp.exp(scores - log_total).astype(bf16)
                    out = out + dot(probs, value_sides[one][side])
                att_ref[tok, q_cols] = out.astype(bf16)
        lse_ref[tok] = lse


def both_halves(place_ref, mine, got):
    first_core = place_ref[1] == 0
    mine, got = mine.astype(f32), got.astype(f32)
    return jnp.concatenate([jnp.where(first_core, mine, got), jnp.where(first_core, got, mine)], 1)


def output_kernel(n, rows, place_ref, owner_ref, att_ref, got_ref, *refs):
    blocks, (w_ref, both_ref, own_ref, send_ref, sems) = refs[:n], refs[n:]
    copies = fetch(n, rows, owner_ref, ((blocks, w_ref),), sems)
    own, other = slice(0, TOK_DEV), slice(TOK_DEV, 2 * TOK_DEV)
    both_ref[own] = both_halves(place_ref, att_ref[own], got_ref[other]).astype(bf16)
    both_ref[other] = both_halves(place_ref, att_ref[other], got_ref[own]).astype(bf16)
    for copy in copies:
        copy.wait()
    proj = dot(both_ref[...], w_ref[...])
    own_ref[...] = proj[own]
    send_ref[...] = proj[other]


def hidden_kernel(n, rows, experts, place_ref, owner_ref, own_ref, got_ref, tok_ref, small_ref, gain_ref, router_ref, chosen_ref, hidden_ref, inv_ref, ffn_ref, router):
    for k in range(n):
        tiles = [small_ref[k, :, i * LANES : (i + 1) * LANES].astype(f32) for i in range(1 + 2 * experts // SMALL_ROWS)]
        put_lanes(gain_ref, tiles[0][1:2], owner_ref[k], rows)
        put_lanes(router, jnp.concatenate(tiles[1 : 1 + experts // SMALL_ROWS], 0), owner_ref[k], rows)
        chosen = jnp.concatenate(tiles[1 + experts // SMALL_ROWS :], 0)
        chosen = jnp.concatenate([chosen, jnp.zeros((LANES - experts, LANES), f32)], 0).T
        chosen_ref[k * TOK_DEV : (k + 1) * TOK_DEV] = chosen[:, :experts]
    router_ref[...] = router[...].astype(bf16)
    hidden = tok_ref[...].astype(f32) + RESIDUAL_SCALE * both_halves(place_ref, own_ref[...], got_ref[...])
    hidden_ref[...] = hidden
    inv = inverse_rms(hidden)
    inv_ref[...] = inv
    ffn_ref[...] = (hidden * inv * gain_ref[...]).astype(bf16)


def block_lanes(ref, row, owner, rows):
    start = owner * rows
    piece = ref[row : row + 1, pl.ds(pl.multiple_of(start // LANES * LANES, LANES), LANES)]
    if rows < LANES:
        piece = pltpu.roll(piece, (LANES - start % LANES) % LANES, 1)
    return piece


def hidden_grad_kernel(experts, back0_ref, back1_ref, back2_ref, gates_ref, ffn_ref, hidden_ref, inv_ref, gain_ref, router_ref, up_ref, branch_ref, small_ref):
    back = back0_ref[...].astype(f32) + back1_ref[...].astype(f32) + back2_ref[...].astype(f32)
    gate_grad = back[:, D : D + experts] + back[:, D + experts : D + 2 * experts]
    gates = gates_ref[...]
    logit_grad = (gates * (gate_grad - jnp.sum(gates * gate_grad, -1, keepdims=True))).astype(bf16)
    hidden, inv, gain = hidden_ref[...], inv_ref[...], gain_ref[...]
    grad = back[:, :D] + dot(logit_grad, router_ref[...])
    scaled = grad * gain
    through = inv * scaled - hidden * (inv * inv * inv) * jnp.mean(scaled * hidden, -1, keepdims=True)
    hidden_grad = up_ref[...].astype(f32) + through
    branch_ref[...] = (RESIDUAL_SCALE * hidden_grad).astype(bf16)
    small_ref[:experts] = t_dot(logit_grad, ffn_ref[...])
    small_ref[experts : experts + 1] = jnp.sum(grad * hidden * inv, 0, keepdims=True)


def output_grad_kernel(place_ref, own_ref, got_ref, w_ref, keep_ref, send_ref, cols_ref):
    half = D // 2
    first_core = place_ref[1] == 0
    both = jnp.concatenate([own_ref[...], got_ref[...]], 0).astype(f32)
    cols = jnp.where(first_core, both[:, :half], both[:, half:]).astype(bf16)
    cols_ref[...] = cols
    grad = dot_t(cols, w_ref[...])
    keep_ref[...] = jnp.where(first_core, grad[:, :QC], grad[:, QC:])
    send_ref[...] = jnp.where(first_core, grad[:, QC:], grad[:, :QC]).astype(bf16)


def output_weight_grad_kernel(n, rows, small_count, owner_ref, both_ref, cols_ref, small_ref, *refs):
    blocks, grads = refs[:n], refs[n]
    grads[...] = t_dot(both_ref[...], cols_ref[...])
    packed = grads.shape[1] // LANES
    for k in range(n):
        at = pl.ds(pl.multiple_of(owner_ref[k] * rows, rows), rows)
        blocks[k][:rows] = grads[at, :].astype(bf16)
        blocks[k][rows:] = jnp.zeros((blocks[k].shape[0] - rows, grads.shape[1]), bf16)
        for i in range(small_count):
            piece = block_lanes(small_ref, i, owner_ref[k], rows)
            lane = i % packed * LANES
            blocks[k][rows + i // packed : rows + i // packed + 1, lane : lane + LANES] = piece.astype(bf16)


def attention_grad_kernel(place_ref, own_ref, other_ref, q_ref, k_ref, v_ref, lse_ref, att_ref, ag_ref, ag_got_ref, cos_ref, sin_ref, q_pre_ref, kv_own_ref, kv_before_ref):
    cos, sin = cos_ref[...], sin_ref[...]
    low = lane_index((TOK_DEV, LANES)) < HEAD_DIM
    for g, packet_ref in enumerate((own_ref, other_ref)):
        tok = slice(g * TOK_DEV, (g + 1) * TOK_DEV)
        there = slice((1 - g) * TOK_DEV, (2 - g) * TOK_DEV)
        win = slice(2 * g * TOK_DEV, 2 * (g + 1) * TOK_DEV)
        halo = slice(g * HALF, (g + 1) * HALF)
        allowed = allowed_pairs(place_ref[0], packet_ref)
        for pair in range(KC // LANES):
            cols = slice(pair * LANES, (pair + 1) * LANES)
            key_sides, value_sides = apart(k_ref[win, cols]), apart(v_ref[win, cols])
            key_grad = jnp.zeros((2 * TOK_DEV, LANES), f32)
            value_grad = jnp.zeros((2 * TOK_DEV, LANES), f32)
            for one in range(2):
                head = 2 * pair + one
                q_cols = slice(head * LANES, (head + 1) * LANES)
                queries = q_ref[tok, q_cols]
                grads = (ag_ref[tok, q_cols] + ag_got_ref[there, q_cols].astype(f32)).astype(bf16)
                query_sides, grad_sides = apart(queries), apart(grads)
                product = grads.astype(f32) * att_ref[tok, q_cols].astype(f32)
                query_grad = jnp.zeros((TOK_DEV, LANES), f32)
                for side in range(2):
                    k_side, v_side = key_sides[one][side], value_sides[one][side]
                    log_total = lse_ref[tok, 2 * head + side : 2 * head + side + 1]
                    delta = jnp.sum(jnp.where(low == (side == 0), product, 0.0), -1, keepdims=True)
                    scores = dot_t(queries, k_side) * SCORE_SCALE
                    probs = jnp.where(allowed, jnp.exp(scores - log_total), 0.0)
                    prob_grad = dot_t(grads, v_side)
                    score_grad = (probs * (prob_grad - delta) * SCORE_SCALE).astype(bf16)
                    query_grad = query_grad + dot(score_grad, k_side)
                    key_grad = key_grad + t_dot(score_grad, query_sides[side][one])
                    value_grad = value_grad + t_dot(probs.astype(bf16), grad_sides[side][one])
                q_pre_ref[tok, q_cols] = rotate_back(query_grad, cos[TOK_DEV:], sin[TOK_DEV:]).astype(bf16)
            v_cols = slice(KC + pair * LANES, KC + (pair + 1) * LANES)
            key_grad = rotate_back(key_grad, cos, sin)
            kv_own_ref[tok, cols] = key_grad[TOK_DEV:]
            kv_own_ref[tok, v_cols] = value_grad[TOK_DEV:]
            kv_before_ref[halo, cols] = key_grad[HALF:TOK_DEV].astype(bf16)
            kv_before_ref[halo, v_cols] = value_grad[HALF:TOK_DEV].astype(bf16)


def projection_grad_kernel(n, rows, owner_ref, q_pre_ref, kv_own_ref, later_ref, normed_ref, w_ref, own_ref, other_ref, inv_ref, *refs):
    blocks, (aig_own_ref, aig_send_ref, grads, gain_grad) = refs[:n], refs[n:]
    kv, later = kv_own_ref[...], later_ref[...].astype(f32)
    parts = []
    for g in range(2):
        at = g * TOK_DEV
        parts += [kv[at : at + HALF], kv[at + HALF : at + TOK_DEV] + later[g * HALF : (g + 1) * HALF]]
    pre = jnp.concatenate([q_pre_ref[...], jnp.concatenate(parts, 0).astype(bf16)], 1)
    grads[...] = t_dot(normed_ref[...], pre)
    aig = dot_t(pre, w_ref[...])
    values = jnp.concatenate([own_ref[:TOK_DEV], other_ref[:TOK_DEV]], 0).astype(f32)
    gain_grad[...] = jnp.sum(aig * values * inv_ref[...], 0, keepdims=True)
    for k in range(n):
        at = pl.ds(pl.multiple_of(owner_ref[k] * rows, rows), rows)
        blocks[k][:rows] = grads[at, :].astype(bf16)
        blocks[k][rows:] = jnp.zeros((blocks[k].shape[0] - rows, D), bf16)
        blocks[k][rows : rows + 1, :LANES] = block_lanes(gain_grad, 0, owner_ref[k], rows).astype(bf16)
    aig_own_ref[...] = aig[:TOK_DEV]
    aig_send_ref[...] = aig[TOK_DEV:]


def input_grad_kernel(aig_ref, got_ref, own_ref, inv_ref, gain_ref, up_ref, out_ref):
    grad = aig_ref[...] + got_ref[...]
    values, inv = own_ref[:TOK_DEV].astype(f32), inv_ref[:TOK_DEV]
    scaled = grad * gain_ref[...]
    through = inv * scaled - values * (inv * inv * inv) * jnp.mean(scaled * values, -1, keepdims=True)
    out_ref[...] = (up_ref[...].astype(f32) + through).astype(bf16)


def assemble_kernel(experts, place_ref, in_own, in_got, out_own, out_got, wq_ref, wk_ref, wv_ref, wo_ref, gain_1_ref, gain_2_ref, router_ref):
    rows = wq_ref.shape[0]
    half = D // 2
    for core, first, second, low, high in ((0, in_own, in_got, out_own, out_got), (1, in_got, in_own, out_got, out_own)):

        @pl.when(place_ref[1] == core)
        def _(sides=((first, low), (second, high))):
            for c, (into, out) in enumerate(sides):
                wq_ref[:, c * QC : (c + 1) * QC] = into[:rows, :QC]
                wk_ref[:, c * KC : (c + 1) * KC] = into[:rows, QC : QC + KC]
                wv_ref[:, c * KC : (c + 1) * KC] = into[:rows, QC + KC :]
                wo_ref[:, c * half : (c + 1) * half] = out[:rows]

    gain_1_ref[...] = in_own[rows : rows + 1, :rows] + in_got[rows : rows + 1, :rows]
    small = out_own[rows:] + out_got[rows:]
    packed = half // LANES
    for i in range(experts + 1):
        piece = small[i // packed : i // packed + 1, i % packed * LANES : i % packed * LANES + rows]
        if i < experts:
            router_ref[i : i + 1] = piece
        else:
            gain_2_ref[...] = piece


def expert_kernel(size, count, experts, shard_ref, *refs):
    x_refs, up_refs = refs[:count], refs[count : 2 * count]
    chosen_ref, router_ref, wg_ref, wu_ref, wd_ref = refs[2 * count : 2 * count + 5]
    refs = refs[-(2 * count + 6 + 3) :]
    back_refs, mix_refs = refs[:count], refs[count : 2 * count]
    gates_ref, all_x, all_act, all_row, all_gate, all_up = refs[2 * count : 2 * count + 6]
    back_acc, mix_acc, cols_acc = refs[-3:]
    e = pl.program_id(0)
    rows = size * count
    x = jnp.concatenate([ref[...] for ref in x_refs], 0)
    grad = RESIDUAL_SCALE * jnp.concatenate([ref[...] for ref in up_refs], 0).astype(f32)

    @pl.when(e == 0)
    def _():
        chosen = chosen_ref[...] > 0
        logits = jnp.where(chosen, dot_t(x, router_ref[...]), NEG_LARGE)
        raised = jnp.where(chosen, jnp.exp(logits - jnp.max(logits, -1, keepdims=True)), 0.0)
        gates_ref[...] = raised / jnp.sum(raised, -1, keepdims=True)
        all_x[...] = x

    here = lax.broadcasted_iota(jnp.int32, (rows, experts), 1) == shard_ref[0] * EXP_DEV + e
    gate = jnp.sum(jnp.where(here, gates_ref[...], 0.0), -1, keepdims=True)
    gate_pre = dot(x, wg_ref[0])
    up_pre = dot(x, wu_ref[0])
    gate_sig = 1.0 / (1.0 + jnp.exp(-gate_pre))
    silu = gate_pre * gate_sig
    activated = (silu * up_pre).astype(bf16)
    all_act[0] = activated
    expert_out = dot(activated, wd_ref[0]).astype(bf16).astype(f32)
    mix = gate * expert_out
    cols = jnp.where(here, jnp.sum(grad * expert_out, -1, keepdims=True), 0.0)
    row_grad = (gate * grad).astype(bf16)
    all_row[0] = row_grad
    unit = dot_t(row_grad, wd_ref[0])
    gate_grad = (unit * up_pre * gate_sig * (1.0 + gate_pre * (1.0 - gate_sig))).astype(bf16)
    up_grad = (unit * silu).astype(bf16)
    all_gate[0] = gate_grad
    all_up[0] = up_grad
    back = dot_t(gate_grad, wg_ref[0]) + dot_t(up_grad, wu_ref[0])

    @pl.when(e == 0)
    def _():
        back_acc[...] = back
        mix_acc[...] = mix
        cols_acc[...] = cols

    @pl.when(e == EXP_DEV - 1)
    def _():
        whole_back = (back_acc[...] + back).astype(bf16)
        whole_mix = (mix_acc[...] + mix).astype(bf16)
        whole_cols = cols_acc[...] + cols
        high = whole_cols.astype(bf16)
        low = (whole_cols - high.astype(f32)).astype(bf16)
        for k in range(count):
            part = slice(k * size, (k + 1) * size)
            back_refs[k][:, :D] = whole_back[part]
            back_refs[k][:, D:] = jnp.zeros((size, LANES), bf16)
            back_refs[k][:, D : D + experts] = high[part]
            back_refs[k][:, D + experts : D + 2 * experts] = low[part]
            mix_refs[k][...] = whole_mix[part]


def expert_weight_kernel(replicas, place_ref, x_ref, act_ref, row_ref, gate_ref, up_ref, keep_ref, send_ref, wide, tall):
    x = x_ref[...]
    for kind, grads in enumerate((gate_ref, up_ref)):
        tall[...] = t_dot(x, grads[0])
        own = tall.shape[0] // replicas
        for j in range(replicas // 2):
            for target, core in ((keep_ref, place_ref[1]), (send_ref, 1 - place_ref[1])):
                at = pl.ds(pl.multiple_of((2 * j + core) * own, own), own)
                target[kind, j] = tall[at, :].astype(bf16)
    wide[...] = t_dot(act_ref[0], row_ref[0])
    own = wide.shape[0] // replicas
    half = wide.shape[1] // 2
    for j in range(replicas // 2):
        for target, core in ((keep_ref, place_ref[1]), (send_ref, 1 - place_ref[1])):
            at = pl.ds(pl.multiple_of((2 * j + core) * own, own), own)
            target[2, j, :own] = wide[at, :half].astype(bf16)
            target[2, j, own:] = wide[at, half:].astype(bf16)


def expert_weight_grads(replicas, place, held, e):
    group_in, act, row, gate, up = held
    ff = act.shape[2]
    own = D // replicas
    shape = (3, replicas // 2, own, ff)

    def one(width):
        return pl.BlockSpec((1, group_in.shape[0], width), lambda i: (e, 0, 0))

    return pl.pallas_call(
        functools.partial(expert_weight_kernel, replicas),
        grid=(1,),
        in_specs=[
            pl.BlockSpec(memory_space=pltpu.SMEM),
            pl.BlockSpec(group_in.shape, lambda i: (0, 0)),
            one(ff),
            one(D),
            one(ff),
            one(ff),
        ],
        out_specs=[pl.BlockSpec(shape, lambda i: (0, 0, 0, 0))] * 2,
        out_shape=[jax.ShapeDtypeStruct(shape, bf16)] * 2,
        scratch_shapes=[pltpu.VMEM((ff, D), f32), pltpu.VMEM((D, ff), f32)],
        compiler_params=pltpu.CompilerParams(vmem_limit_bytes=32 * 2**20),
        cost_estimate=pl.CostEstimate(flops=2**32, bytes_accessed=2**23, transcendentals=0),
    )(place, group_in, act, row, gate, up)


def expert_sum_kernel(*refs):
    keeps, gots, (gate_ref, up_ref, down_ref) = refs[:EXP_DEV], refs[EXP_DEV : 2 * EXP_DEV], refs[2 * EXP_DEV :]
    own = down_ref.shape[1]
    for e in range(EXP_DEV):
        total = [keeps[e][kind].astype(f32) + gots[e][kind].astype(f32) for kind in range(3)]
        gate_ref[e] = total[0]
        up_ref[e] = total[1]
        down_ref[e, :, : total[2].shape[1]] = total[2][:own]
        down_ref[e, :, total[2].shape[1] :] = total[2][own:]


def replica_split_kernel(place_ref, keep_ref, got_ref, stay_ref, send_ref):
    here = place_ref[2] // 2 % 2
    for kind in range(3):
        for j in range(stay_ref.shape[1]):
            for target, at in ((stay_ref, 2 * j + here), (send_ref, 2 * j + 1 - here)):
                target[kind, j] = (keep_ref[kind, at].astype(f32) + got_ref[kind, at].astype(f32)).astype(bf16)


def run_experts(block, count, total, shard, x, up, chosen, router, w_gate, w_up, w_down, held):
    rows = TOK_DEV * count
    experts = chosen.shape[1]
    ff = w_gate.shape[2]
    at = block // count

    def whole(shape):
        return pl.BlockSpec(shape, lambda e: (0,) * len(shape))

    def one(shape):
        return pl.BlockSpec((1,) + shape, lambda e: (e,) + (0,) * len(shape))

    def filled(width):
        return pl.BlockSpec((1, rows, width), lambda e: (e, at, 0))

    every = TOK_DEV * total
    out_shape = (
        [jax.ShapeDtypeStruct((TOK_DEV, D + LANES), bf16)] * count
        + [jax.ShapeDtypeStruct((TOK_DEV, D), bf16)] * count
        + [jax.ShapeDtypeStruct((rows, experts), f32)]
    )
    held_shape = [
        jax.ShapeDtypeStruct((every, D), bf16),
        jax.ShapeDtypeStruct((EXP_DEV, every, ff), bf16),
        jax.ShapeDtypeStruct((EXP_DEV, every, D), bf16),
        jax.ShapeDtypeStruct((EXP_DEV, every, ff), bf16),
        jax.ShapeDtypeStruct((EXP_DEV, every, ff), bf16),
    ]
    out_specs = (
        [whole((TOK_DEV, D + LANES))] * count
        + [whole((TOK_DEV, D))] * count
        + [whole((rows, experts))]
        + [pl.BlockSpec((rows, D), lambda e: (at, 0))]
        + [filled(ff), filled(D), filled(ff), filled(ff)]
    )
    in_specs = [
        pl.BlockSpec(memory_space=pltpu.SMEM),
        *[whole((TOK_DEV, D))] * (2 * count),
        pl.BlockSpec((rows, experts), lambda e: (at, 0)),
        whole(router.shape),
        one(w_gate.shape[1:]),
        one(w_up.shape[1:]),
        one(w_down.shape[1:]),
    ]
    args = [shard, *x, *up, chosen, router, w_gate, w_up, w_down]
    aliases = {}
    if held is not None:
        aliases = {len(args) + k: len(out_shape) + k for k in range(len(held))}
        in_specs = in_specs + [pl.BlockSpec(memory_space=pl.ANY)] * len(held)
        args = args + list(held)
    flops = 12 * rows * D * ff * EXP_DEV
    outs = pl.pallas_call(
        functools.partial(expert_kernel, TOK_DEV, count, experts),
        grid=(EXP_DEV,),
        in_specs=in_specs,
        out_specs=out_specs,
        out_shape=out_shape + held_shape,
        scratch_shapes=[
            pltpu.VMEM((rows, D), f32),
            pltpu.VMEM((rows, D), f32),
            pltpu.VMEM((rows, experts), f32),
        ],
        input_output_aliases=aliases,
        compiler_params=pltpu.CompilerParams(vmem_limit_bytes=24 * 2**20),
        cost_estimate=pl.CostEstimate(
            flops=flops, bytes_accessed=6 * D * ff * EXP_DEV + 16 * rows * D, transcendentals=rows * ff * EXP_DEV
        ),
    )(*args)
    return outs[:count], outs[count : 2 * count], outs[2 * count], outs[2 * count + 1 :]


def per_device(
    tokens,
    segment_ids,
    expert_ids,
    attn_gain,
    w_query,
    w_key,
    w_value,
    w_output,
    ffn_gain,
    w_router,
    w_gate,
    w_up,
    w_down,
    out_grad,
):
    shard = lax.axis_index("shard")
    core = lax.axis_index("rep") % 2
    ring = Ring()
    n = ring.n
    experts = EXP_DEV * n
    rows = w_query.shape[0]
    half_width = D // 2

    replicas = lax.axis_size("rep")
    place = jnp.stack([shard, core, lax.axis_index("rep")]).astype(jnp.int32)
    owners = ring.row
    cos, sin = rotary_tables()
    shift_up = [(i, i + 1) for i in range(n - 1)]
    shift_down = [(i + 1, i) for i in range(n - 1)]

    in_own, in_theirs, out_own = call(
        split_kernel,
        [vmem((rows + SMALL_ROWS, WIDE), bf16), vmem((rows, ALONE), bf16), vmem((rows, half_width), bf16)],
        [place],
        [attn_gain[None], ffn_gain[None], w_router.T, expert_ids[0].T, w_query, w_key, w_value, w_output],
        limit=60,
    )
    in_ring, theirs = Gather(ring, in_own), [in_theirs]

    def cross_in():
        if len(theirs) > 2:
            in_ring.got, theirs[-2] = together(in_ring.got, theirs[-2])
        theirs.append(swap(jnp.concatenate([in_ring.got[o][:rows, :ALONE] for o in in_ring.new], axis=0), 2))

    in_ring.step()
    cross_in()
    seg_row = jnp.pad(segment_ids.astype(bf16), ((0, SEG_ROWS - 1), (0, D - TOK_DEV)))
    before = jnp.concatenate([tokens[0, HALF:], seg_row], axis=0)
    before = lax.ppermute(after(before, in_ring.got[-1]), "shard", shift_up)
    packet = jnp.concatenate([tokens[0], before, seg_row], axis=0)
    in_ring.step()
    cross_in()
    packet_other = swap(after(packet, in_ring.got[-2]), 1)
    while in_ring.left > 1:
        in_ring.step()
        cross_in()
    out_ring = Gather(ring, after(out_own, in_ring.got[-in_ring.done[-1]]), flip=True)
    in_ring.step()
    cross_in()
    out_ring.hop(1)
    out_ring.got, up_own = after((out_ring.got, out_grad[0]), *in_ring.blocks())
    up = Gather(ring, up_own, flip=True)
    out_ring.step()
    up.step()
    in_w, small, first_gain, normed, inv_first, queries, keys, values, log_total, att = call(
        functools.partial(attention_kernel, n, rows),
        [
            vmem((D, D), bf16),
            vmem((n, SMALL_ROWS, WIDE), bf16),
            vmem((1, D), f32),
            vmem((2 * TOK_DEV, D), bf16),
            vmem((2 * TOK_DEV, 1), f32),
            vmem((2 * TOK_DEV, QC), bf16),
            vmem((4 * TOK_DEV, KC), bf16),
            vmem((4 * TOK_DEV, KC), bf16),
            vmem((2 * TOK_DEV, LANES), f32),
            vmem((2 * TOK_DEV, QC), bf16),
        ],
        [place, owners],
        [packet, packet_other, cos, sin],
        [pltpu.VMEM((4 * TOK_DEV, D), bf16), pltpu.SemaphoreType.DMA((4 * n,))],
        flops=2**32,
        anywhere=[*in_ring.blocks(), *theirs],
    )
    out_ring.got, up.got, att = together(out_ring.got, up.got, att)
    att_got = swap(att, 1)
    while out_ring.left:
        out_ring.step()
    out_blocks, att_got, up.got = together(out_ring.blocks(), att_got, up.got)
    if up.left > 1:
        up.step()
    out_w, attended, proj, proj_send = call(
        functools.partial(output_kernel, n, rows),
        [
            vmem((QW, half_width), bf16),
            vmem((2 * TOK_DEV, QW), bf16),
            vmem((TOK_DEV, half_width), f32),
            vmem((TOK_DEV, half_width), f32),
        ],
        [place, owners],
        [att, att_got],
        [pltpu.SemaphoreType.DMA((n,))],
        flops=2**30,
        anywhere=out_blocks,
    )
    second_gain, router, group_chosen, hidden, inv_second, ffn_inputs = call(
        functools.partial(hidden_kernel, n, rows, experts),
        [
            vmem((1, D), f32),
            vmem((experts, D), bf16),
            vmem((n * TOK_DEV, experts), f32),
            vmem((TOK_DEV, D), f32),
            vmem((TOK_DEV, 1), f32),
            vmem((TOK_DEV, D), bf16),
        ],
        [place, owners],
        [proj, swap(proj_send, 1), tokens[0], small],
        [pltpu.VMEM((experts, D), f32)],
        flops=2**28,
    )


    group = Gather(ring, ffn_inputs)
    while group.left:
        group.step()
        if up.left:
            up.step()
    held = None
    back_parts = [None] * n
    own_gates = None
    mix_parts = [None] * n
    runs = [(0, 1)] + [(k, 2) for k in range(2, n, 2)] + [(1, 1)]
    for block, count in runs:
        part = slice(block, block + count)
        backs, mixes, gates, held = run_experts(
            block,
            count,
            n,
            place[:1],
            [group.got[o] for o in ring.offsets[part]],
            up.blocks()[part],
            group_chosen,
            router,
            w_gate,
            w_up,
            w_down,
            held,
        )
        back_parts[part] = backs
        mix_parts[part] = mixes
        own_gates = gates if block == 0 else own_gates

    back, mix = Scatter(ring, back_parts), Scatter(ring, mix_parts, flip=True)
    stays, crossing, made = [], [], []
    while back.left:
        if back.left == 1:
            back.got = after(back.got, made)
            mix.sums = after(mix.sums, back.got)
            mix.hop(1)
        back.step()
        if len(stays) < EXP_DEV:
            held = after(held, back.got)
            keep, send = expert_weight_grads(replicas, place, held, len(stays))
            made.append(send)
            stay, send = call(
                replica_split_kernel,
                [vmem((3, replicas // 4, *keep.shape[2:]), bf16)] * 2,
                [place],
                [keep, swap(send, 1)],
            )
            stays.append(stay)
            crossing.append(send)
    own_gates, crossing[0] = together(own_gates, crossing[0])
    crossing[0] = swap(crossing[0], 2)

    branch, out_small = call(
        functools.partial(hidden_grad_kernel, experts),
        [vmem((TOK_DEV, D), bf16), vmem((experts + 1, D), f32)],
        [],
        [
            *back.terms(),
            own_gates,
            ffn_inputs,
            hidden,
            inv_second,
            second_gain,
            router,
            out_grad[0],
        ],
        flops=2**28,
    )
    ag_keep, ag_send, branch_cols = call(
        output_grad_kernel,
        [
            vmem((2 * TOK_DEV, QC), f32),
            vmem((2 * TOK_DEV, QC), bf16),
            vmem((2 * TOK_DEV, half_width), bf16),
        ],
        [place],
        [branch, swap(branch, 1), out_w],
        flops=2**29,
    )
    mix.got, mix.sums = after((mix.got, mix.sums), *back.terms())
    mix.step()
    ag_got = swap(ag_send, 1)
    extra = -(-(experts + 1) // (8 * (half_width // LANES))) * 8
    out_blocks = call(
        functools.partial(output_weight_grad_kernel, n, rows, experts + 1),
        [vmem((rows + extra, half_width), bf16)] * n,
        [owners],
        [attended, branch_cols, out_small],
        [pltpu.VMEM((QW, half_width), f32)],
        flops=2**29,
    )
    ag_got, out_blocks = together(ag_got, out_blocks)
    q_pre, kv_own, kv_before = call(
        attention_grad_kernel,
        [
            vmem((2 * TOK_DEV, QC), bf16),
            vmem((2 * TOK_DEV, 2 * KC), f32),
            vmem((TOK_DEV, 2 * KC), bf16),
        ],
        [place],
        [packet, packet_other, queries, keys, values, log_total, att, ag_keep, ag_got, cos, sin],
        flops=2**32,
    )
    later = lax.ppermute(kv_before, "shard", shift_down)
    mix.got = after(mix.got, kv_before)
    if mix.left > 1:
        mix.step()
    later, out_blocks = together(later, out_blocks)
    out = Scatter(ring, out_blocks, flip=True)
    out.step()
    *in_blocks, aig_own, aig_send = call(
        functools.partial(projection_grad_kernel, n, rows),
        [vmem((rows + 8, D), bf16)] * n + [vmem((TOK_DEV, D), f32)] * 2,
        [owners],
        [q_pre, kv_own, later, normed, in_w, packet, packet_other, inv_first],
        [pltpu.VMEM((D, D), f32), pltpu.VMEM((1, D), f32)],
        flops=2**32,
    )
    in_blocks, crossing[0], mix.got = together(in_blocks, crossing[0], mix.got)
    crossing[1] = swap(after(crossing[1], crossing[0]), 2)

    def owned(sums):
        own, ahead, behind = sums.terms()
        return rep_sum(own.astype(f32) + ahead.astype(f32) + behind.astype(f32))

    into = Scatter(ring, in_blocks)
    into.step()
    out.step()
    into.got, out.got = together(into.got, out.got)
    into.step()
    out.step()
    into.got, out.got, crossing[1] = together(into.got, out.got, crossing[1])
    into.step()
    while out.left:
        out.step()
    aig_got = swap(aig_send, 1)
    into.got, out.got, aig_got = together(into.got, out.got, aig_got)
    input_grad = call(
        input_grad_kernel,
        [vmem((TOK_DEV, D), bf16)],
        [],
        [aig_own, aig_got, packet, inv_first, first_gain, out_grad[0]],
    )[0]
    out_sum = owned(out)
    mix.got = after(mix.got, into.got)
    if mix.left:
        mix.hop(1)
    while into.left:
        into.step()
    into.got, out_sum, mix.got = together(into.got, out_sum, mix.got)
    out_got = swap(out_sum, 1)
    left = replicas // 4
    for bit in list(bits())[2:]:
        left //= 2
        here = (lax.axis_index("rep") // bit) % 2
        for e in range(EXP_DEV):
            total = (stays[e].astype(f32) + crossing[e].astype(f32)).astype(bf16)
            pairs = total.reshape(3, left, 2, *total.shape[2:])
            stays[e] = lax.dynamic_index_in_dim(pairs, here, 2, False)
            crossing[e] = swap(lax.dynamic_index_in_dim(pairs, 1 - here, 2, False), bit)
    ff, own_rows = w_gate.shape[2], D // replicas
    gate_sum, up_sum, down_sum = call(
        expert_sum_kernel,
        [
            vmem((EXP_DEV, own_rows, ff), f32),
            vmem((EXP_DEV, own_rows, ff), f32),
            vmem((EXP_DEV, ff // replicas, D), f32),
        ],
        [],
        [part[:, 0] for part in stays + crossing],
    )
    mix.got = after(mix.got, into.got)
    while mix.left:
        mix.step()

    in_sum = owned(into)
    in_sum, mix.got = together(in_sum, mix.got)
    moe_sum = sum(term.astype(f32) for term in mix.terms())
    in_got = swap(in_sum, 1)
    g_query, g_key, g_value, g_output, gain_1, gain_2, g_router = call(
        functools.partial(assemble_kernel, experts),
        [
            vmem((rows, QW), f32),
            vmem((rows, KW), f32),
            vmem((rows, KW), f32),
            vmem((rows, D), f32),
            vmem((1, rows), f32),
            vmem((1, rows), f32),
            vmem((experts, rows), f32),
        ],
        [place],
        [in_sum, in_got, out_sum, out_got],
    )
    mixed = (hidden + RESIDUAL_SCALE * moe_sum).astype(bf16)
    return (
        mixed[None],
        input_grad[None],
        gain_1[0],
        g_query,
        g_key,
        g_value,
        g_output,
        gain_2[0],
        g_router.T,
        gate_sum,
        up_sum,
        down_sum,
    )


def solution(mesh):
    return jax.shard_map(
        per_device,
        mesh=mesh,
        in_specs=(
            P("rep", "shard", None),
            P("rep", "shard"),
            P("rep", "shard", None),
            P("shard"),
            P("shard", None),
            P("shard", None),
            P("shard", None),
            P("shard", None),
            P("shard"),
            P("shard", None),
            P("shard", None, None),
            P("shard", None, None),
            P("shard", None, None),
            P("rep", "shard", None),
        ),
        out_specs=(
            P("rep", "shard", None),
            P("rep", "shard", None),
            P("shard"),
            P("shard", None),
            P("shard", None),
            P("shard", None),
            P("shard", None),
            P("shard"),
            P("shard", None),
            P("shard", "rep", None),
            P("shard", "rep", None),
            P("shard", "rep", None),
        ),
        check_vma=False,
    )
```

```python
import functools

import jax
import jax.numpy as jnp
import numpy as np
from jax import lax
from jax.experimental import pallas as pl
from jax.experimental.pallas import tpu as pltpu
from jax.sharding import PartitionSpec as P

D = 1024
HEADS = 16
KV_HEADS = 8
HEAD_DIM = 64
GROUP = HEADS // KV_HEADS
QW = HEADS * HEAD_DIM
KW = KV_HEADS * HEAD_DIM
QC = QW // 2
KC = KW // 2
ALONE = 384
SHARED = D - 2 * ALONE
WIDE = ALONE + SHARED
TOK_DEV = 128
HALF = TOK_DEV // 2
HALO = TOK_DEV + HALF
SEG_ROWS = 16
EXP_DEV = 2
LANES = 128

EPSILON = 1e-06
RESIDUAL_SCALE = 0.22
SCORE_SCALE = 0.015625
ROPE_BASE = 10000.0
NEG_LARGE = -1e30

bf16 = jnp.bfloat16
f32 = jnp.float32


def dot(a, b, contract=((1,), (0,))):
    return lax.dot_general(a, b, (contract, ((), ())), preferred_element_type=f32)


def dot_t(a, b):
    return dot(a, b, ((1,), (1,)))


def t_dot(a, b):
    return dot(a, b, ((0,), (0,)))


def cycle(length):
    rows = 4 if length % 4 == 0 else 1
    cols = length // rows
    if cols == 1:
        return list(range(length))
    order = [z * cols for z in range(rows)]
    for k, z in enumerate(reversed(range(rows))):
        ys = list(range(1, cols))
        order += [z * cols + y for y in (ys if k % 2 == 0 else reversed(ys))]
    return order


class Ring:
    def __init__(self):
        n = self.n = lax.axis_size("shard")
        cyc = self.cyc = cycle(n)
        self.next = [(cyc[i], cyc[(i + 1) % n]) for i in range(n)]
        self.prev = [(b, a) for a, b in self.next]
        self.ahead, self.back = n // 2, (n - 1) // 2
        self.offsets = [0, -self.ahead]
        for s in range(1, self.back + 1):
            self.offsets += [-s, s]
        place = {dev: i for i, dev in enumerate(cyc)}
        table = [[cyc[(place[dev] + o) % n] for o in self.offsets] for dev in range(n)]
        row = lax.dynamic_index_in_dim(jnp.asarray(table, jnp.int32), lax.axis_index("shard"), 0, False)
        self.row = row


class Gather:
    def __init__(self, ring, block, flip=False):
        self.ring, self.got, self.flip = ring, {0: block}, flip
        self.pairs = {-1: ring.next, 1: ring.prev}
        self.steps = {-1: ring.back, 1: ring.ahead} if flip else {-1: ring.ahead, 1: ring.back}
        self.done = {-1: 0, 1: 0}

    @property
    def left(self):
        return max(self.steps[sign] - self.done[sign] for sign in (-1, 1))

    def hop(self, sign):
        s = self.done[sign] = self.done[sign] + 1
        self.got[sign * s] = lax.ppermute(self.got[sign * (s - 1)], "shard", self.pairs[sign])

    def step(self):
        self.new = []
        for sign in (-1, 1):
            if self.done[sign] < self.steps[sign]:
                self.hop(sign)
                self.new.append(sign * self.done[sign])

    def blocks(self):
        half = self.ring.ahead
        if self.flip:
            self.got[-half] = self.got[half]
        return [self.got[o] for o in self.ring.offsets]


class Scatter:
    def __init__(self, ring, parts, flip=False):
        self.part = dict(zip(ring.offsets, parts))
        self.pairs = {-1: ring.prev, 1: ring.next}
        self.hops = {-1: ring.back, 1: ring.ahead} if flip else {-1: ring.ahead, 1: ring.back}
        if flip:
            self.part[ring.ahead] = self.part[-ring.ahead]
        self.sums = {sign: self.part[sign * steps] for sign, steps in self.hops.items()}
        self.got = {}

    @property
    def left(self):
        return max(self.hops.values())

    def hop(self, sign):
        if sign in self.got:
            part = self.part[sign * self.hops[sign]].astype(f32)
            self.sums[sign] = (self.got[sign].astype(f32) + part).astype(bf16)
        self.got[sign] = lax.ppermute(self.sums[sign], "shard", self.pairs[sign])
        self.hops[sign] -= 1

    def step(self):
        left = self.left
        for sign in (-1, 1):
            if self.hops[sign] == left:
                self.hop(sign)

    def terms(self):
        return self.part[0], self.got[-1], self.got[1]


def after(value, *earlier):
    return lax.optimization_barrier((value, *earlier))[0] if earlier else value


def together(*values):
    return lax.optimization_barrier(values)


def swap(value, bit):
    size = lax.axis_size("rep")
    return lax.ppermute(value, "rep", [(r, r ^ bit) for r in range(size)])


def bits():
    size, bit = lax.axis_size("rep"), 1
    while bit < size:
        yield bit
        bit *= 2


def rep_sum(value):
    for bit in list(bits())[1:]:
        low = lax.reduce_precision(value, 8, 7)
        value = low + swap(low.astype(bf16), bit).astype(f32)
    return value


def rotary_tables():
    positions = (np.arange(2 * TOK_DEV) + HALF) % TOK_DEV
    inverse = ROPE_BASE ** (-2.0 * np.arange(HEAD_DIM // 2) / HEAD_DIM)
    angles = positions[:, None] * inverse[None, :]
    cos, sin = np.cos(angles), np.sin(angles)
    cos, sin = np.concatenate([cos] * 4, axis=1), np.concatenate([-sin, sin] * 2, axis=1)
    return jnp.asarray(cos, f32), jnp.asarray(sin, f32)


def lane_index(shape):
    return lax.broadcasted_iota(jnp.int32, shape, 1)


def rotate(values, cos, sin):
    first = lane_index(values.shape) % HEAD_DIM < HEAD_DIM // 2
    turned = jnp.where(first, pltpu.roll(values, LANES - 32, 1), pltpu.roll(values, 32, 1))
    return values * cos + turned * sin


def rotate_back(values, cos, sin):
    first = lane_index(values.shape) % HEAD_DIM < HEAD_DIM // 2
    moved = values * sin
    turned = jnp.where(first, pltpu.roll(moved, LANES - 32, 1), pltpu.roll(moved, 32, 1))
    return values * cos + turned


def apart(pair):
    pair = pair.astype(f32)
    turned = pltpu.roll(pair, HEAD_DIM, 1)
    low = lane_index(pair.shape) < HEAD_DIM
    zero = jnp.zeros_like(pair)
    return (
        (jnp.where(low, pair, zero).astype(bf16), jnp.where(low, zero, turned).astype(bf16)),
        (jnp.where(low, turned, zero).astype(bf16), jnp.where(low, zero, pair).astype(bf16)),
    )


def allowed_pairs(shard_index, packet_ref):
    seg_before = packet_ref[HALO : HALO + 1, :LANES].astype(f32)
    seg_own = packet_ref[HALO + SEG_ROWS : HALO + SEG_ROWS + 1, :LANES].astype(f32)
    seg_key = jnp.concatenate([seg_before, seg_own], 1)
    seg_query = jnp.broadcast_to(seg_own, (TOK_DEV, TOK_DEV)).T[:, :1]
    shape = (TOK_DEV, 2 * TOK_DEV)
    query = lax.broadcasted_iota(jnp.int32, shape, 0)
    key = lax.broadcasted_iota(jnp.int32, shape, 1) - TOK_DEV
    allowed = (key <= query) & (key >= -HALF) & ((query >= HALF) == (key >= HALF))
    return allowed & ((key >= 0) | (shard_index > 0)) & (seg_query == seg_key)


def inverse_rms(values):
    return lax.rsqrt(jnp.mean(values * values, axis=-1, keepdims=True) + EPSILON)


def vmem(shape, dtype):
    return jax.ShapeDtypeStruct(shape, dtype)


def call(kernel, out_shape, scalars, arrays, scratch=(), flops=0, limit=30, anywhere=(), out_space=None):
    return pl.pallas_call(
        kernel,
        in_specs=[pl.BlockSpec(memory_space=pltpu.SMEM)] * len(scalars)
        + [pl.BlockSpec()] * len(arrays)
        + [pl.BlockSpec(memory_space=pl.ANY)] * len(anywhere),
        out_specs=[pl.BlockSpec(memory_space=out_space) if out_space else pl.BlockSpec()] * len(out_shape),
        out_shape=out_shape,
        scratch_shapes=list(scratch),
        compiler_params=pltpu.CompilerParams(vmem_limit_bytes=limit * 2**20),
        cost_estimate=pl.CostEstimate(flops=flops, bytes_accessed=2**22, transcendentals=0),
    )(*scalars, *arrays, *anywhere)


SMALL_ROWS = 16


def split_kernel(place_ref, gain_1_ref, gain_2_ref, router_ref, ids_ref, wq_ref, wk_ref, wv_ref, wo_ref, mine, theirs, out_mine):
    half = D // 2
    experts, rows = router_ref.shape
    ids = ids_ref[...]
    expert = lax.broadcasted_iota(jnp.int32, (experts, TOK_DEV), 0)
    chosen = jnp.zeros((experts, TOK_DEV), f32)
    for k in range(ids.shape[0]):
        chosen = jnp.where(expert == ids[k : k + 1], 1.0, chosen)
    mine[rows:] = jnp.zeros((SMALL_ROWS, WIDE), bf16)
    mine[rows : rows + 1, :rows] = gain_1_ref[...]
    mine[rows + 1 : rows + 2, :rows] = gain_2_ref[...]
    for t in range(experts // SMALL_ROWS):
        part = slice(t * SMALL_ROWS, (t + 1) * SMALL_ROWS)
        at = (1 + t) * LANES
        mine[rows:, at : at + rows] = router_ref[part]
        at = (1 + t + experts // SMALL_ROWS) * LANES
        mine[rows:, at : at + LANES] = chosen[part].astype(bf16)
    for core in range(2):

        @pl.when(place_ref[1] == core)
        def _(core=core):
            cols = [wq_ref[:, core * QC : (core + 1) * QC]]
            cols += [ref[:, core * KC : (core + 1) * KC] for ref in (wk_ref, wv_ref)]
            cols = jnp.concatenate(cols, 1)
            first_x = place_ref[2] // 2 % 2 == 0
            low, high = cols[:, :ALONE].astype(f32), cols[:, ALONE + SHARED :].astype(f32)
            mine[:rows, :ALONE] = jnp.where(first_x, low, high).astype(bf16)
            mine[:rows, ALONE:] = cols[:, ALONE : ALONE + SHARED]
            theirs[...] = jnp.where(first_x, high, low).astype(bf16)
            out_mine[...] = wo_ref[:, core * half : (core + 1) * half]


def put_lanes(ref, piece, owner, rows):
    start = owner * rows
    at = pl.ds(pl.multiple_of(start // LANES * LANES, LANES), LANES)
    if rows < LANES:
        off = start % LANES
        lane = lane_index(piece.shape)
        piece = pltpu.roll(piece, off, 1)
        piece = jnp.where((lane >= off) & (lane < off + rows), piece, ref[:, at])
    ref[:, at] = piece


def fetch(n, rows, owner_ref, pairs, sems):
    copies = []
    for blocks, target in pairs:
        for k in range(n):
            at = pl.ds(pl.multiple_of(owner_ref[k] * rows, rows), rows)
            copies.append(pltpu.make_async_copy(blocks[k].at[pl.ds(0, rows)], target.at[at], sems.at[len(copies)]))
    for copy in copies:
        copy.start()
    return copies


def attention_kernel(n, rows, place_ref, owner_ref, own_ref, other_ref, cos_ref, sin_ref, *refs):
    blocks, theirs = refs[:n], refs[n : n + n // 2 + 1]
    w_ref, small_ref, gain_ref, normed_ref, inv_ref, q_ref, k_ref, v_ref, lse_ref, att_ref, window, sems = refs[n + n // 2 + 1 :]
    first_x = place_ref[2] // 2 % 2 == 0
    ours_at = pl.ds(pl.multiple_of(jnp.where(first_x, 0, ALONE + SHARED), LANES), ALONE)
    theirs_at = pl.ds(pl.multiple_of(jnp.where(first_x, ALONE + SHARED, 0), LANES), ALONE)
    other_x = [theirs[0], theirs[n // 2]]
    for k in range(1, n // 2):
        other_x += [theirs[k].at[pl.ds(0, rows)], theirs[k].at[pl.ds(rows, rows)]]
    copies = []
    for k in range(n):
        source = blocks[k].at[pl.ds(rows, SMALL_ROWS)]
        copies.append(pltpu.make_async_copy(source, small_ref.at[k], sems.at[k]))
    for k in range(n):
        at = pl.ds(pl.multiple_of(owner_ref[k] * rows, rows), rows)
        block = blocks[k].at[pl.ds(0, rows)]
        for source, target in (
            (block.at[:, pl.ds(0, ALONE)], w_ref.at[at, ours_at]),
            (block.at[:, pl.ds(ALONE, SHARED)], w_ref.at[at, pl.ds(ALONE, SHARED)]),
            (other_x[k], w_ref.at[at, theirs_at]),
        ):
            copies.append(pltpu.make_async_copy(source, target, sems.at[len(copies)]))
    for copy in copies:
        copy.start()
    packets = (own_ref, other_ref)
    scaled = []
    for g, packet in enumerate(packets):
        values = packet[:HALO].astype(f32)
        inv = inverse_rms(values)
        inv_ref[g * TOK_DEV : (g + 1) * TOK_DEV] = inv[:TOK_DEV]
        scaled.append(values * inv)
    for k in range(n):
        copies[k].wait()
    for k in range(n):
        put_lanes(gain_ref, small_ref[k, :1, :LANES].astype(f32), owner_ref[k], rows)
    gain = gain_ref[...]
    for g in range(2):
        base = 2 * TOK_DEV * g
        normed = (scaled[g] * gain).astype(bf16)
        window[base : base + HALF] = jnp.zeros((HALF, D), bf16)
        window[base + HALF : base + TOK_DEV] = normed[TOK_DEV:]
        window[base + TOK_DEV : base + 2 * TOK_DEV] = normed[:TOK_DEV]
        normed_ref[g * TOK_DEV : (g + 1) * TOK_DEV] = normed[:TOK_DEV]
    for copy in copies[n:]:
        copy.wait()
    q_both = dot(normed_ref[...], w_ref[:, :QC])
    kv_both = dot(window[...], w_ref[:, QC:])
    cos, sin = cos_ref[...], sin_ref[...]
    lane = lane_index((TOK_DEV, LANES))
    for g in range(2):
        tok = slice(g * TOK_DEV, (g + 1) * TOK_DEV)
        win = slice(2 * g * TOK_DEV, 2 * (g + 1) * TOK_DEV)
        q_lin, kv_lin = q_both[tok], kv_both[win]
        allowed = allowed_pairs(place_ref[0], packets[g])
        v_ref[win] = kv_lin[:, KC:].astype(bf16)
        lse = jnp.zeros((TOK_DEV, LANES), f32)
        for pair in range(KC // LANES):
            cols = slice(pair * LANES, (pair + 1) * LANES)
            keys = rotate(kv_lin[:, cols], cos, sin)
            k_ref[win, cols] = keys.astype(bf16)
            key_sides = apart(keys)
            value_sides = apart(kv_lin[:, KC + pair * LANES : KC + (pair + 1) * LANES])
            for one in range(2):
                head = 2 * pair + one
                q_cols = slice(head * LANES, (head + 1) * LANES)
                queries = rotate(q_lin[:, q_cols], cos[TOK_DEV:], sin[TOK_DEV:]).astype(bf16)
                q_ref[tok, q_cols] = queries
                out = 0.0
                for side in range(2):
                    scores = dot_t(queries, key_sides[one][side]) * SCORE_SCALE
                    scores = jnp.where(allowed, scores, NEG_LARGE)
                    highest = jnp.max(scores, -1, keepdims=True)
                    raised = jnp.exp(scores - highest)
                    log_total = highest + jnp.log(jnp.sum(raised, -1, keepdims=True))
                    lse = jnp.where(lane == 2 * head + side, log_total, lse)
                    probs = jnp.exp(scores - log_total).astype(bf16)
                    out = out + dot(probs, value_sides[one][side])
                att_ref[tok, q_cols] = out.astype(bf16)
        lse_ref[tok] = lse


def both_halves(place_ref, mine, got):
    first_core = place_ref[1] == 0
    mine, got = mine.astype(f32), got.astype(f32)
    return jnp.concatenate([jnp.where(first_core, mine, got), jnp.where(first_core, got, mine)], 1)


def output_kernel(n, rows, place_ref, owner_ref, att_ref, got_ref, *refs):
    blocks, (w_ref, both_ref, own_ref, send_ref, sems) = refs[:n], refs[n:]
    copies = fetch(n, rows, owner_ref, ((blocks, w_ref),), sems)
    own, other = slice(0, TOK_DEV), slice(TOK_DEV, 2 * TOK_DEV)
    both_ref[own] = both_halves(place_ref, att_ref[own], got_ref[other]).astype(bf16)
    both_ref[other] = both_halves(place_ref, att_ref[other], got_ref[own]).astype(bf16)
    for copy in copies:
        copy.wait()
    proj = dot(both_ref[...], w_ref[...])
    own_ref[...] = proj[own]
    send_ref[...] = proj[other]


def hidden_kernel(n, rows, experts, place_ref, owner_ref, own_ref, got_ref, tok_ref, small_ref, gain_ref, router_ref, chosen_ref, hidden_ref, inv_ref, ffn_ref, router):
    for k in range(n):
        tiles = [small_ref[k, :, i * LANES : (i + 1) * LANES].astype(f32) for i in range(1 + 2 * experts // SMALL_ROWS)]
        put_lanes(gain_ref, tiles[0][1:2], owner_ref[k], rows)
        put_lanes(router, jnp.concatenate(tiles[1 : 1 + experts // SMALL_ROWS], 0), owner_ref[k], rows)
        chosen = jnp.concatenate(tiles[1 + experts // SMALL_ROWS :], 0)
        chosen = jnp.concatenate([chosen, jnp.zeros((LANES - experts, LANES), f32)], 0).T
        chosen_ref[k * TOK_DEV : (k + 1) * TOK_DEV] = chosen[:, :experts]
    router_ref[...] = router[...].astype(bf16)
    hidden = tok_ref[...].astype(f32) + RESIDUAL_SCALE * both_halves(place_ref, own_ref[...], got_ref[...])
    hidden_ref[...] = hidden
    inv = inverse_rms(hidden)
    inv_ref[...] = inv
    ffn_ref[...] = (hidden * inv * gain_ref[...]).astype(bf16)


def block_lanes(ref, row, owner, rows):
    start = owner * rows
    piece = ref[row : row + 1, pl.ds(pl.multiple_of(start // LANES * LANES, LANES), LANES)]
    if rows < LANES:
        piece = pltpu.roll(piece, (LANES - start % LANES) % LANES, 1)
    return piece


def hidden_grad_kernel(experts, back0_ref, back1_ref, back2_ref, gates_ref, ffn_ref, hidden_ref, inv_ref, gain_ref, router_ref, up_ref, branch_ref, small_ref):
    back = back0_ref[...].astype(f32) + back1_ref[...].astype(f32) + back2_ref[...].astype(f32)
    gate_grad = back[:, D : D + experts] + back[:, D + experts : D + 2 * experts]
    gates = gates_ref[...]
    logit_grad = (gates * (gate_grad - jnp.sum(gates * gate_grad, -1, keepdims=True))).astype(bf16)
    hidden, inv, gain = hidden_ref[...], inv_ref[...], gain_ref[...]
    grad = back[:, :D] + dot(logit_grad, router_ref[...])
    scaled = grad * gain
    through = inv * scaled - hidden * (inv * inv * inv) * jnp.mean(scaled * hidden, -1, keepdims=True)
    hidden_grad = up_ref[...].astype(f32) + through
    branch_ref[...] = (RESIDUAL_SCALE * hidden_grad).astype(bf16)
    small_ref[:experts] = t_dot(logit_grad, ffn_ref[...])
    small_ref[experts : experts + 1] = jnp.sum(grad * hidden * inv, 0, keepdims=True)


def output_grad_kernel(place_ref, own_ref, got_ref, w_ref, keep_ref, send_ref, cols_ref):
    half = D // 2
    first_core = place_ref[1] == 0
    both = jnp.concatenate([own_ref[...], got_ref[...]], 0).astype(f32)
    cols = jnp.where(first_core, both[:, :half], both[:, half:]).astype(bf16)
    cols_ref[...] = cols
    grad = dot_t(cols, w_ref[...])
    keep_ref[...] = jnp.where(first_core, grad[:, :QC], grad[:, QC:])
    send_ref[...] = jnp.where(first_core, grad[:, QC:], grad[:, :QC]).astype(bf16)


def output_weight_grad_kernel(n, rows, small_count, owner_ref, both_ref, cols_ref, small_ref, *refs):
    blocks, grads = refs[:n], refs[n]
    grads[...] = t_dot(both_ref[...], cols_ref[...])
    packed = grads.shape[1] // LANES
    for k in range(n):
        at = pl.ds(pl.multiple_of(owner_ref[k] * rows, rows), rows)
        blocks[k][:rows] = grads[at, :].astype(bf16)
        blocks[k][rows:] = jnp.zeros((blocks[k].shape[0] - rows, grads.shape[1]), bf16)
        for i in range(small_count):
            piece = block_lanes(small_ref, i, owner_ref[k], rows)
            lane = i % packed * LANES
            blocks[k][rows + i // packed : rows + i // packed + 1, lane : lane + LANES] = piece.astype(bf16)


def attention_grad_kernel(place_ref, own_ref, other_ref, q_ref, k_ref, v_ref, lse_ref, att_ref, ag_ref, ag_got_ref, cos_ref, sin_ref, q_pre_ref, kv_own_ref, kv_before_ref):
    cos, sin = cos_ref[...], sin_ref[...]
    low = lane_index((TOK_DEV, LANES)) < HEAD_DIM
    for g, packet_ref in enumerate((own_ref, other_ref)):
        tok = slice(g * TOK_DEV, (g + 1) * TOK_DEV)
        there = slice((1 - g) * TOK_DEV, (2 - g) * TOK_DEV)
        win = slice(2 * g * TOK_DEV, 2 * (g + 1) * TOK_DEV)
        halo = slice(g * HALF, (g + 1) * HALF)
        allowed = allowed_pairs(place_ref[0], packet_ref)
        for pair in range(KC // LANES):
            cols = slice(pair * LANES, (pair + 1) * LANES)
            key_sides, value_sides = apart(k_ref[win, cols]), apart(v_ref[win, cols])
            key_grad = jnp.zeros((2 * TOK_DEV, LANES), f32)
            value_grad = jnp.zeros((2 * TOK_DEV, LANES), f32)
            for one in range(2):
                head = 2 * pair + one
                q_cols = slice(head * LANES, (head + 1) * LANES)
                queries = q_ref[tok, q_cols]
                grads = (ag_ref[tok, q_cols] + ag_got_ref[there, q_cols].astype(f32)).astype(bf16)
                query_sides, grad_sides = apart(queries), apart(grads)
                product = grads.astype(f32) * att_ref[tok, q_cols].astype(f32)
                query_grad = jnp.zeros((TOK_DEV, LANES), f32)
                for side in range(2):
                    k_side, v_side = key_sides[one][side], value_sides[one][side]
                    log_total = lse_ref[tok, 2 * head + side : 2 * head + side + 1]
                    delta = jnp.sum(jnp.where(low == (side == 0), product, 0.0), -1, keepdims=True)
                    scores = dot_t(queries, k_side) * SCORE_SCALE
                    probs = jnp.where(allowed, jnp.exp(scores - log_total), 0.0)
                    prob_grad = dot_t(grads, v_side)
                    score_grad = (probs * (prob_grad - delta) * SCORE_SCALE).astype(bf16)
                    query_grad = query_grad + dot(score_grad, k_side)
                    key_grad = key_grad + t_dot(score_grad, query_sides[side][one])
                    value_grad = value_grad + t_dot(probs.astype(bf16), grad_sides[side][one])
                q_pre_ref[tok, q_cols] = rotate_back(query_grad, cos[TOK_DEV:], sin[TOK_DEV:]).astype(bf16)
            v_cols = slice(KC + pair * LANES, KC + (pair + 1) * LANES)
            key_grad = rotate_back(key_grad, cos, sin)
            kv_own_ref[tok, cols] = key_grad[TOK_DEV:]
            kv_own_ref[tok, v_cols] = value_grad[TOK_DEV:]
            kv_before_ref[halo, cols] = key_grad[HALF:TOK_DEV].astype(bf16)
            kv_before_ref[halo, v_cols] = value_grad[HALF:TOK_DEV].astype(bf16)


def projection_grad_kernel(n, rows, owner_ref, q_pre_ref, kv_own_ref, later_ref, normed_ref, w_ref, own_ref, other_ref, inv_ref, *refs):
    blocks, (aig_own_ref, aig_send_ref, grads, gain_grad) = refs[:n], refs[n:]
    kv, later = kv_own_ref[...], later_ref[...].astype(f32)
    parts = []
    for g in range(2):
        at = g * TOK_DEV
        parts += [kv[at : at + HALF], kv[at + HALF : at + TOK_DEV] + later[g * HALF : (g + 1) * HALF]]
    pre = jnp.concatenate([q_pre_ref[...], jnp.concatenate(parts, 0).astype(bf16)], 1)
    grads[...] = t_dot(normed_ref[...], pre)
    aig = dot_t(pre, w_ref[...])
    values = jnp.concatenate([own_ref[:TOK_DEV], other_ref[:TOK_DEV]], 0).astype(f32)
    gain_grad[...] = jnp.sum(aig * values * inv_ref[...], 0, keepdims=True)
    for k in range(n):
        at = pl.ds(pl.multiple_of(owner_ref[k] * rows, rows), rows)
        blocks[k][:rows] = grads[at, :].astype(bf16)
        blocks[k][rows:] = jnp.zeros((blocks[k].shape[0] - rows, D), bf16)
        blocks[k][rows : rows + 1, :LANES] = block_lanes(gain_grad, 0, owner_ref[k], rows).astype(bf16)
    aig_own_ref[...] = aig[:TOK_DEV]
    aig_send_ref[...] = aig[TOK_DEV:]


def input_grad_kernel(aig_ref, got_ref, own_ref, inv_ref, gain_ref, up_ref, out_ref):
    grad = aig_ref[...] + got_ref[...]
    values, inv = own_ref[:TOK_DEV].astype(f32), inv_ref[:TOK_DEV]
    scaled = grad * gain_ref[...]
    through = inv * scaled - values * (inv * inv * inv) * jnp.mean(scaled * values, -1, keepdims=True)
    out_ref[...] = (up_ref[...].astype(f32) + through).astype(bf16)


def assemble_kernel(experts, place_ref, in_own, in_got, out_own, out_got, wq_ref, wk_ref, wv_ref, wo_ref, gain_1_ref, gain_2_ref, router_ref):
    rows = wq_ref.shape[0]
    half = D // 2
    for core, first, second, low, high in ((0, in_own, in_got, out_own, out_got), (1, in_got, in_own, out_got, out_own)):

        @pl.when(place_ref[1] == core)
        def _(sides=((first, low), (second, high))):
            for c, (into, out) in enumerate(sides):
                wq_ref[:, c * QC : (c + 1) * QC] = into[:rows, :QC]
                wk_ref[:, c * KC : (c + 1) * KC] = into[:rows, QC : QC + KC]
                wv_ref[:, c * KC : (c + 1) * KC] = into[:rows, QC + KC :]
                wo_ref[:, c * half : (c + 1) * half] = out[:rows]

    gain_1_ref[...] = in_own[rows : rows + 1, :rows] + in_got[rows : rows + 1, :rows]
    small = out_own[rows:] + out_got[rows:]
    packed = half // LANES
    for i in range(experts + 1):
        piece = small[i // packed : i // packed + 1, i % packed * LANES : i % packed * LANES + rows]
        if i < experts:
            router_ref[i : i + 1] = piece
        else:
            gain_2_ref[...] = piece


def expert_kernel(size, count, experts, shard_ref, *refs):
    x_refs, up_refs = refs[:count], refs[count : 2 * count]
    chosen_ref, router_ref, wg_ref, wu_ref, wd_ref = refs[2 * count : 2 * count + 5]
    refs = refs[-(2 * count + 6 + 3) :]
    back_refs, mix_refs = refs[:count], refs[count : 2 * count]
    gates_ref, all_x, all_act, all_row, all_gate, all_up = refs[2 * count : 2 * count + 6]
    back_acc, mix_acc, cols_acc = refs[-3:]
    e = pl.program_id(0)
    rows = size * count
    x = jnp.concatenate([ref[...] for ref in x_refs], 0)
    grad = RESIDUAL_SCALE * jnp.concatenate([ref[...] for ref in up_refs], 0).astype(f32)

    @pl.when(e == 0)
    def _():
        chosen = chosen_ref[...] > 0
        logits = jnp.where(chosen, dot_t(x, router_ref[...]), NEG_LARGE)
        raised = jnp.where(chosen, jnp.exp(logits - jnp.max(logits, -1, keepdims=True)), 0.0)
        gates_ref[...] = raised / jnp.sum(raised, -1, keepdims=True)
        all_x[...] = x

    here = lax.broadcasted_iota(jnp.int32, (rows, experts), 1) == shard_ref[0] * EXP_DEV + e
    gate = jnp.sum(jnp.where(here, gates_ref[...], 0.0), -1, keepdims=True)
    gate_pre = dot(x, wg_ref[0])
    up_pre = dot(x, wu_ref[0])
    gate_sig = 1.0 / (1.0 + jnp.exp(-gate_pre))
    silu = gate_pre * gate_sig
    activated = (silu * up_pre).astype(bf16)
    all_act[0] = activated
    expert_out = dot(activated, wd_ref[0]).astype(bf16).astype(f32)
    mix = gate * expert_out
    cols = jnp.where(here, jnp.sum(grad * expert_out, -1, keepdims=True), 0.0)
    row_grad = (gate * grad).astype(bf16)
    all_row[0] = row_grad
    unit = dot_t(row_grad, wd_ref[0])
    gate_grad = (unit * up_pre * gate_sig * (1.0 + gate_pre * (1.0 - gate_sig))).astype(bf16)
    up_grad = (unit * silu).astype(bf16)
    all_gate[0] = gate_grad
    all_up[0] = up_grad
    back = dot_t(gate_grad, wg_ref[0]) + dot_t(up_grad, wu_ref[0])

    @pl.when(e == 0)
    def _():
        back_acc[...] = back
        mix_acc[...] = mix
        cols_acc[...] = cols

    @pl.when(e == EXP_DEV - 1)
    def _():
        whole_back = (back_acc[...] + back).astype(bf16)
        whole_mix = (mix_acc[...] + mix).astype(bf16)
        whole_cols = cols_acc[...] + cols
        high = whole_cols.astype(bf16)
        low = (whole_cols - high.astype(f32)).astype(bf16)
        for k in range(count):
            part = slice(k * size, (k + 1) * size)
            back_refs[k][:, :D] = whole_back[part]
            back_refs[k][:, D:] = jnp.zeros((size, LANES), bf16)
            back_refs[k][:, D : D + experts] = high[part]
            back_refs[k][:, D + experts : D + 2 * experts] = low[part]
            mix_refs[k][...] = whole_mix[part]


def expert_weight_kernel(replicas, place_ref, x_ref, act_ref, row_ref, gate_ref, up_ref, keep_ref, send_ref, wide, tall):
    x = x_ref[...]
    for kind, grads in enumerate((gate_ref, up_ref)):
        tall[...] = t_dot(x, grads[0])
        own = tall.shape[0] // replicas
        for j in range(replicas // 2):
            for target, core in ((keep_ref, place_ref[1]), (send_ref, 1 - place_ref[1])):
                at = pl.ds(pl.multiple_of((2 * j + core) * own, own), own)
                target[kind, j] = tall[at, :].astype(bf16)
    wide[...] = t_dot(act_ref[0], row_ref[0])
    own = wide.shape[0] // replicas
    half = wide.shape[1] // 2
    for j in range(replicas // 2):
        for target, core in ((keep_ref, place_ref[1]), (send_ref, 1 - place_ref[1])):
            at = pl.ds(pl.multiple_of((2 * j + core) * own, own), own)
            target[2, j, :own] = wide[at, :half].astype(bf16)
            target[2, j, own:] = wide[at, half:].astype(bf16)


def expert_weight_grads(replicas, place, held, e):
    group_in, act, row, gate, up = held
    ff = act.shape[2]
    own = D // replicas
    shape = (3, replicas // 2, own, ff)

    def one(width):
        return pl.BlockSpec((1, group_in.shape[0], width), lambda i: (e, 0, 0))

    return pl.pallas_call(
        functools.partial(expert_weight_kernel, replicas),
        grid=(1,),
        in_specs=[
            pl.BlockSpec(memory_space=pltpu.SMEM),
            pl.BlockSpec(group_in.shape, lambda i: (0, 0)),
            one(ff),
            one(D),
            one(ff),
            one(ff),
        ],
        out_specs=[pl.BlockSpec(shape, lambda i: (0, 0, 0, 0))] * 2,
        out_shape=[jax.ShapeDtypeStruct(shape, bf16)] * 2,
        scratch_shapes=[pltpu.VMEM((ff, D), f32), pltpu.VMEM((D, ff), f32)],
        compiler_params=pltpu.CompilerParams(vmem_limit_bytes=32 * 2**20),
        cost_estimate=pl.CostEstimate(flops=2**32, bytes_accessed=2**23, transcendentals=0),
    )(place, group_in, act, row, gate, up)


def expert_sum_kernel(*refs):
    keeps, gots, (gate_ref, up_ref, down_ref) = refs[:EXP_DEV], refs[EXP_DEV : 2 * EXP_DEV], refs[2 * EXP_DEV :]
    own = down_ref.shape[1]
    for e in range(EXP_DEV):
        total = [keeps[e][kind].astype(f32) + gots[e][kind].astype(f32) for kind in range(3)]
        gate_ref[e] = total[0]
        up_ref[e] = total[1]
        down_ref[e, :, : total[2].shape[1]] = total[2][:own]
        down_ref[e, :, total[2].shape[1] :] = total[2][own:]


def replica_split_kernel(place_ref, keep_ref, got_ref, stay_ref, send_ref):
    here = place_ref[2] // 2 % 2
    for kind in range(3):
        for j in range(stay_ref.shape[1]):
            for target, at in ((stay_ref, 2 * j + here), (send_ref, 2 * j + 1 - here)):
                target[kind, j] = (keep_ref[kind, at].astype(f32) + got_ref[kind, at].astype(f32)).astype(bf16)


def run_experts(block, count, total, shard, x, up, chosen, router, w_gate, w_up, w_down, held):
    rows = TOK_DEV * count
    experts = chosen.shape[1]
    ff = w_gate.shape[2]
    at = block // count

    def whole(shape):
        return pl.BlockSpec(shape, lambda e: (0,) * len(shape))

    def one(shape):
        return pl.BlockSpec((1,) + shape, lambda e: (e,) + (0,) * len(shape))

    def filled(width):
        return pl.BlockSpec((1, rows, width), lambda e: (e, at, 0))

    every = TOK_DEV * total
    out_shape = (
        [jax.ShapeDtypeStruct((TOK_DEV, D + LANES), bf16)] * count
        + [jax.ShapeDtypeStruct((TOK_DEV, D), bf16)] * count
        + [jax.ShapeDtypeStruct((rows, experts), f32)]
    )
    held_shape = [
        jax.ShapeDtypeStruct((every, D), bf16),
        jax.ShapeDtypeStruct((EXP_DEV, every, ff), bf16),
        jax.ShapeDtypeStruct((EXP_DEV, every, D), bf16),
        jax.ShapeDtypeStruct((EXP_DEV, every, ff), bf16),
        jax.ShapeDtypeStruct((EXP_DEV, every, ff), bf16),
    ]
    out_specs = (
        [whole((TOK_DEV, D + LANES))] * count
        + [whole((TOK_DEV, D))] * count
        + [whole((rows, experts))]
        + [pl.BlockSpec((rows, D), lambda e: (at, 0))]
        + [filled(ff), filled(D), filled(ff), filled(ff)]
    )
    in_specs = [
        pl.BlockSpec(memory_space=pltpu.SMEM),
        *[whole((TOK_DEV, D))] * (2 * count),
        pl.BlockSpec((rows, experts), lambda e: (at, 0)),
        whole(router.shape),
        one(w_gate.shape[1:]),
        one(w_up.shape[1:]),
        one(w_down.shape[1:]),
    ]
    args = [shard, *x, *up, chosen, router, w_gate, w_up, w_down]
    aliases = {}
    if held is not None:
        aliases = {len(args) + k: len(out_shape) + k for k in range(len(held))}
        in_specs = in_specs + [pl.BlockSpec(memory_space=pl.ANY)] * len(held)
        args = args + list(held)
    flops = 12 * rows * D * ff * EXP_DEV
    outs = pl.pallas_call(
        functools.partial(expert_kernel, TOK_DEV, count, experts),
        grid=(EXP_DEV,),
        in_specs=in_specs,
        out_specs=out_specs,
        out_shape=out_shape + held_shape,
        scratch_shapes=[
            pltpu.VMEM((rows, D), f32),
            pltpu.VMEM((rows, D), f32),
            pltpu.VMEM((rows, experts), f32),
        ],
        input_output_aliases=aliases,
        compiler_params=pltpu.CompilerParams(vmem_limit_bytes=24 * 2**20),
        cost_estimate=pl.CostEstimate(
            flops=flops, bytes_accessed=6 * D * ff * EXP_DEV + 16 * rows * D, transcendentals=rows * ff * EXP_DEV
        ),
    )(*args)
    return outs[:count], outs[count : 2 * count], outs[2 * count], outs[2 * count + 1 :]


def per_device(
    tokens,
    segment_ids,
    expert_ids,
    attn_gain,
    w_query,
    w_key,
    w_value,
    w_output,
    ffn_gain,
    w_router,
    w_gate,
    w_up,
    w_down,
    out_grad,
):
    shard = lax.axis_index("shard")
    core = lax.axis_index("rep") % 2
    ring = Ring()
    n = ring.n
    experts = EXP_DEV * n
    rows = w_query.shape[0]
    half_width = D // 2

    replicas = lax.axis_size("rep")
    place = jnp.stack([shard, core, lax.axis_index("rep")]).astype(jnp.int32)
    owners = ring.row
    cos, sin = rotary_tables()
    shift_up = [(i, i + 1) for i in range(n - 1)]
    shift_down = [(i + 1, i) for i in range(n - 1)]

    in_own, in_theirs, out_own = call(
        split_kernel,
        [vmem((rows + SMALL_ROWS, WIDE), bf16), vmem((rows, ALONE), bf16), vmem((rows, half_width), bf16)],
        [place],
        [attn_gain[None], ffn_gain[None], w_router.T, expert_ids[0].T, w_query, w_key, w_value, w_output],
        limit=60,
    )
    in_ring, theirs = Gather(ring, in_own), [in_theirs]

    def cross_in():
        if len(theirs) > 2:
            in_ring.got, theirs[-2] = together(in_ring.got, theirs[-2])
        theirs.append(swap(jnp.concatenate([in_ring.got[o][:rows, :ALONE] for o in in_ring.new], axis=0), 2))

    in_ring.step()
    cross_in()
    seg_row = jnp.pad(segment_ids.astype(bf16), ((0, SEG_ROWS - 1), (0, D - TOK_DEV)))
    before = jnp.concatenate([tokens[0, HALF:], seg_row], axis=0)
    before = lax.ppermute(after(before, in_ring.got[-1]), "shard", shift_up)
    packet = jnp.concatenate([tokens[0], before, seg_row], axis=0)
    in_ring.step()
    cross_in()
    packet_other = swap(after(packet, in_ring.got[-2]), 1)
    while in_ring.left > 1:
        in_ring.step()
        cross_in()
    out_ring = Gather(ring, after(out_own, in_ring.got[-in_ring.done[-1]]), flip=True)
    in_ring.step()
    cross_in()
    out_ring.hop(1)
    out_ring.got, up_own = after((out_ring.got, out_grad[0]), *in_ring.blocks())
    up = Gather(ring, up_own, flip=True)
    out_ring.step()
    up.step()
    in_w, small, first_gain, normed, inv_first, queries, keys, values, log_total, att = call(
        functools.partial(attention_kernel, n, rows),
        [
            vmem((D, D), bf16),
            vmem((n, SMALL_ROWS, WIDE), bf16),
            vmem((1, D), f32),
            vmem((2 * TOK_DEV, D), bf16),
            vmem((2 * TOK_DEV, 1), f32),
            vmem((2 * TOK_DEV, QC), bf16),
            vmem((4 * TOK_DEV, KC), bf16),
            vmem((4 * TOK_DEV, KC), bf16),
            vmem((2 * TOK_DEV, LANES), f32),
            vmem((2 * TOK_DEV, QC), bf16),
        ],
        [place, owners],
        [packet, packet_other, cos, sin],
        [pltpu.VMEM((4 * TOK_DEV, D), bf16), pltpu.SemaphoreType.DMA((4 * n,))],
        flops=2**32,
        anywhere=[*in_ring.blocks(), *theirs],
    )
    out_ring.got, up.got, att = together(out_ring.got, up.got, att)
    att_got = swap(att, 1)
    while out_ring.left:
        out_ring.step()
    out_blocks, att_got, up.got = together(out_ring.blocks(), att_got, up.got)
    if up.left > 1:
        up.step()
    out_w, attended, proj, proj_send = call(
        functools.partial(output_kernel, n, rows),
        [
            vmem((QW, half_width), bf16),
            vmem((2 * TOK_DEV, QW), bf16),
            vmem((TOK_DEV, half_width), f32),
            vmem((TOK_DEV, half_width), f32),
        ],
        [place, owners],
        [att, att_got],
        [pltpu.SemaphoreType.DMA((n,))],
        flops=2**30,
        anywhere=out_blocks,
    )
    second_gain, router, group_chosen, hidden, inv_second, ffn_inputs = call(
        functools.partial(hidden_kernel, n, rows, experts),
        [
            vmem((1, D), f32),
            vmem((experts, D), bf16),
            vmem((n * TOK_DEV, experts), f32),
            vmem((TOK_DEV, D), f32),
            vmem((TOK_DEV, 1), f32),
            vmem((TOK_DEV, D), bf16),
        ],
        [place, owners],
        [proj, swap(proj_send, 1), tokens[0], small],
        [pltpu.VMEM((experts, D), f32)],
        flops=2**28,
    )


    group = Gather(ring, ffn_inputs)
    while group.left:
        group.step()
        if up.left:
            up.step()
    held = None
    back_parts = [None] * n
    own_gates = None
    mix_parts = [None] * n
    runs = [(0, 1)] + [(k, 2) for k in range(2, n, 2)] + [(1, 1)]
    for block, count in runs:
        part = slice(block, block + count)
        backs, mixes, gates, held = run_experts(
            block,
            count,
            n,
            place[:1],
            [group.got[o] for o in ring.offsets[part]],
            up.blocks()[part],
            group_chosen,
            router,
            w_gate,
            w_up,
            w_down,
            held,
        )
        back_parts[part] = backs
        mix_parts[part] = mixes
        own_gates = gates if block == 0 else own_gates

    back, mix = Scatter(ring, back_parts), Scatter(ring, mix_parts, flip=True)
    stays, crossing, made = [], [], []
    while back.left:
        if back.left == 1:
            back.got = after(back.got, made)
            mix.sums = after(mix.sums, back.got)
            mix.hop(1)
        back.step()
        if len(stays) < EXP_DEV:
            held = after(held, back.got)
            keep, send = expert_weight_grads(replicas, place, held, len(stays))
            made.append(send)
            stay, send = call(
                replica_split_kernel,
                [vmem((3, replicas // 4, *keep.shape[2:]), bf16)] * 2,
                [place],
                [keep, swap(send, 1)],
            )
            stays.append(stay)
            crossing.append(send)
    own_gates, crossing[0] = together(own_gates, crossing[0])
    crossing[0] = swap(crossing[0], 2)

    branch, out_small = call(
        functools.partial(hidden_grad_kernel, experts),
        [vmem((TOK_DEV, D), bf16), vmem((experts + 1, D), f32)],
        [],
        [
            *back.terms(),
            own_gates,
            ffn_inputs,
            hidden,
            inv_second,
            second_gain,
            router,
            out_grad[0],
        ],
        flops=2**28,
    )
    ag_keep, ag_send, branch_cols = call(
        output_grad_kernel,
        [
            vmem((2 * TOK_DEV, QC), f32),
            vmem((2 * TOK_DEV, QC), bf16),
            vmem((2 * TOK_DEV, half_width), bf16),
        ],
        [place],
        [branch, swap(branch, 1), out_w],
        flops=2**29,
    )
    mix.got, mix.sums = after((mix.got, mix.sums), *back.terms())
    mix.step()
    ag_got = swap(ag_send, 1)
    extra = -(-(experts + 1) // (8 * (half_width // LANES))) * 8
    out_blocks = call(
        functools.partial(output_weight_grad_kernel, n, rows, experts + 1),
        [vmem((rows + extra, half_width), bf16)] * n,
        [owners],
        [attended, branch_cols, out_small],
        [pltpu.VMEM((QW, half_width), f32)],
        flops=2**29,
    )
    ag_got, out_blocks = together(ag_got, out_blocks)
    q_pre, kv_own, kv_before = call(
        attention_grad_kernel,
        [
            vmem((2 * TOK_DEV, QC), bf16),
            vmem((2 * TOK_DEV, 2 * KC), f32),
            vmem((TOK_DEV, 2 * KC), bf16),
        ],
        [place],
        [packet, packet_other, queries, keys, values, log_total, att, ag_keep, ag_got, cos, sin],
        flops=2**32,
    )
    later = lax.ppermute(kv_before, "shard", shift_down)
    mix.got = after(mix.got, kv_before)
    if mix.left > 1:
        mix.step()
    later, out_blocks = together(later, out_blocks)
    out = Scatter(ring, out_blocks, flip=True)
    out.step()
    *in_blocks, aig_own, aig_send = call(
        functools.partial(projection_grad_kernel, n, rows),
        [vmem((rows + 8, D), bf16)] * n + [vmem((TOK_DEV, D), f32)] * 2,
        [owners],
        [q_pre, kv_own, later, normed, in_w, packet, packet_other, inv_first],
        [pltpu.VMEM((D, D), f32), pltpu.VMEM((1, D), f32)],
        flops=2**32,
    )
    in_blocks, crossing[0], mix.got = together(in_blocks, crossing[0], mix.got)
    crossing[1] = swap(after(crossing[1], crossing[0]), 2)

    def owned(sums):
        own, ahead, behind = sums.terms()
        return rep_sum(own.astype(f32) + ahead.astype(f32) + behind.astype(f32))

    into = Scatter(ring, in_blocks)
    into.step()
    out.step()
    into.got, out.got = together(into.got, out.got)
    into.step()
    out.step()
    into.got, out.got, crossing[1] = together(into.got, out.got, crossing[1])
    into.step()
    while out.left:
        out.step()
    aig_got = swap(aig_send, 1)
    into.got, out.got, aig_got = together(into.got, out.got, aig_got)
    input_grad = call(
        input_grad_kernel,
        [vmem((TOK_DEV, D), bf16)],
        [],
        [aig_own, aig_got, packet, inv_first, first_gain, out_grad[0]],
    )[0]
    out_sum = owned(out)
    mix.got = after(mix.got, into.got)
    if mix.left:
        mix.hop(1)
    while into.left:
        into.step()
    into.got, out_sum, mix.got = together(into.got, out_sum, mix.got)
    out_got = swap(out_sum, 1)
    left = replicas // 4
    for bit in list(bits())[2:]:
        left //= 2
        here = (lax.axis_index("rep") // bit) % 2
        for e in range(EXP_DEV):
            total = (stays[e].astype(f32) + crossing[e].astype(f32)).astype(bf16)
            pairs = total.reshape(3, left, 2, *total.shape[2:])
            stays[e] = lax.dynamic_index_in_dim(pairs, here, 2, False)
            crossing[e] = swap(lax.dynamic_index_in_dim(pairs, 1 - here, 2, False), bit)
    ff, own_rows = w_gate.shape[2], D // replicas
    gate_sum, up_sum, down_sum = call(
        expert_sum_kernel,
        [
            vmem((EXP_DEV, own_rows, ff), f32),
            vmem((EXP_DEV, own_rows, ff), f32),
            vmem((EXP_DEV, ff // replicas, D), f32),
        ],
        [],
        [part[:, 0] for part in stays + crossing],
    )
    mix.got = after(mix.got, into.got)
    while mix.left:
        mix.step()

    in_sum = owned(into)
    in_sum, mix.got = together(in_sum, mix.got)
    moe_sum = sum(term.astype(f32) for term in mix.terms())
    in_got = swap(in_sum, 1)
    g_query, g_key, g_value, g_output, gain_1, gain_2, g_router = call(
        functools.partial(assemble_kernel, experts),
        [
            vmem((rows, QW), f32),
            vmem((rows, KW), f32),
            vmem((rows, KW), f32),
            vmem((rows, D), f32),
            vmem((1, rows), f32),
            vmem((1, rows), f32),
            vmem((experts, rows), f32),
        ],
        [place],
        [in_sum, in_got, out_sum, out_got],
    )
    mixed = (hidden + RESIDUAL_SCALE * moe_sum).astype(bf16)
    return (
        mixed[None],
        input_grad[None],
        gain_1[0],
        g_query,
        g_key,
        g_value,
        g_output,
        gain_2[0],
        g_router.T,
        gate_sum,
        up_sum,
        down_sum,
    )


def solution(mesh):
    return jax.shard_map(
        per_device,
        mesh=mesh,
        in_specs=(
            P("rep", "shard", None),
            P("rep", "shard"),
            P("rep", "shard", None),
            P("shard"),
            P("shard", None),
            P("shard", None),
            P("shard", None),
            P("shard", None),
            P("shard"),
            P("shard", None),
            P("shard", None, None),
            P("shard", None, None),
            P("shard", None, None),
            P("rep", "shard", None),
        ),
        out_specs=(
            P("rep", "shard", None),
            P("rep", "shard", None),
            P("shard"),
            P("shard", None),
            P("shard", None),
            P("shard", None),
            P("shard", None),
            P("shard"),
            P("shard", None),
            P("shard", "rep", None),
            P("shard", "rep", None),
            P("shard", "rep", None),
        ),
        check_vma=False,
    )
```
